32 devices in a mesh: item: 4 (over y, x), frame: 8 (over z, core).
Axes of the slice: x: 2, y: 2, z: 4, core: 2. Of those that a mesh axis runs over, the one named last changes fastest.
Arguments:
- tokens: bfloat16 [4, 16, 448, 1152], P('item', 'frame'), may hold values from -6 to 6
- cotangent: bfloat16 [4, 16, 448, 1152], P('item', 'frame'), may hold values from -6 to 6
- patch_counts: int32 [12], replicated, may hold values from 64 to 256, as said below
- assignment: int32 [12], replicated, may hold values from 0 to 3, as said below
- timesteps: int32 [12], replicated, may hold values from 0 to 999
- class_ids: int32 [12], replicated, may hold values from 0 to 100
- w_qkv: bfloat16 [1152, 3456], P('frame'), may hold values from -0.1875 to 0.1875
- w_out: bfloat16 [1152, 1152], P('frame'), may hold values from -0.75 to 0.75
- w_fc1: bfloat16 [1152, 4608], P('frame'), may hold values from -0.1875 to 0.1875
- b_fc1: bfloat16 [4608], P('frame'), may hold values from -3 to 3
- w_fc2: bfloat16 [4608, 1152], P('frame'), may hold values from -0.09375 to 0.09375
- w_ada: bfloat16 [1152, 6912], P(None, 'frame'), may hold values from -0.1875 to 0.1875
- b_ada: bfloat16 [6912], P('frame'), may hold values from -3 to 3
- class_table: float32 [101, 1152], replicated, may hold values from -6 to 6
Outputs:
- block_out: bfloat16 [4, 16, 448, 1152], P('item', 'frame')
- grad_tokens: bfloat16 [4, 16, 448, 1152], P('item', 'frame')
- grad_w_qkv: float32 [1152, 3456], P('frame')
- grad_w_out: float32 [1152, 1152], P('frame')
- grad_w_fc1: float32 [1152, 4608], P('frame')
- grad_b_fc1: float32 [4608], P('frame')
- grad_w_fc2: float32 [4608, 1152], P('frame')
- grad_w_ada: float32 [1152, 6912], P(None, 'frame')
- grad_b_ada: float32 [6912], P('frame')
- grad_class_table: float32 [101, 1152], replicated
The draws below stay inside these ranges and needn't reach their ends.
Inputs may be any that keep to these rules, and one draw needn't show every extreme that they name: `patch_counts`: each clip holds 256 or 64 patches a frame. The clips of one group hold at most 448 patches a frame together, at most one of them with 256, and some group holds exactly 448. `assignment`: every group holds one to four clips.
All inputs are finite; a program needn't handle non-finite values.
Results may differ from the reference program's by a relative error of at most 0.02.
Values may be sent and summed in bfloat16 or wider, within the bound.
No kernel may reach another device: no remote copies, remote signals or barrier semaphores. Data moves between devices by JAX's collectives and lax.ppermute only.
A program may use at most 256 MiB of HBM per device.

```python
import math
import jax
import jax.numpy as jnp
from jax import lax

D = 1152
HEADS = 16
FF = 4608
CLASSES = 101
PATCH_HI = 256
PATCH_LO = 64
CAP = 448
FRAMES = 16
TIMESTEPS = 1000
GROUPS = 4
ITEMS = 12


def group_layout(key):
    slots = 4 * GROUPS
    key_full, key_order, key_high = jax.random.split(key, 3)
    full_group = jax.random.randint(key_full, (), 0, GROUPS)
    order = jax.random.permutation(key_order, slots).astype(jnp.int32)
    slot_ids = jnp.arange(slots, dtype=jnp.int32)
    first_slot = slot_ids % 4 == 0
    score = jnp.where(first_slot, order - slots, order)
    score = jnp.where(slot_ids // 4 == full_group, slot_ids % 4 - 3 * slots, score)
    chosen = jnp.sort(jnp.argsort(score)[:ITEMS])
    high = (jax.random.randint(key_high, (slots,), 0, 4) < 3) | (slot_ids // 4 == full_group)
    counts = jnp.where(first_slot[chosen] & high[chosen], PATCH_HI, PATCH_LO).astype(jnp.int32)
    return (counts, (chosen // 4).astype(jnp.int32))


def draw_patch_counts(key, part):
    counts, _ = group_layout(key)
    return counts


def draw_assignment(key, part):
    _, owners = group_layout(key)
    return owners


def with_ends(drawn, stream_key, low, high):
    shape = drawn.shape
    index_at = [jax.random.randint(jax.random.fold_in(stream_key, axis), (), 0, shape[axis]) for axis in range(len(shape))]
    drawn = drawn.at[tuple(index_at)].set(low)
    longest = shape.index(max(shape))
    index_at[longest] = (index_at[longest] + 1) % shape[longest]
    return drawn.at[tuple(index_at)].set(high)


def level_of(own_key, dims, cuts, least, top_value):
    gain = 1.0
    for axis_at, blocks in cuts:
        draws = jax.random.uniform(jax.random.fold_in(jax.random.fold_in(own_key, 6), axis_at), (blocks,), jnp.float32, least / len(cuts), top_value / len(cuts))
        gain = gain * jnp.repeat(jnp.exp(draws), dims[axis_at] // blocks).reshape((-1,) + (1,) * (len(dims) - 1 - axis_at))
    return gain


def scatter_about(rng, extent, width, reach, pieces=(), held_as=jnp.bfloat16):
    values = jax.random.normal(rng, extent, jnp.float32) * width
    if len(pieces) > 0:
        values = level_of(rng, extent, pieces, -0.22, 0.18) * values
    return jnp.clip(values, min=-reach, max=reach).astype(held_as)


def setup_inputs(seed: int = 0) -> dict:
    seeds = jax.random.split(jax.random.key(seed), 15)
    return {
        "tokens": scatter_about(seeds[0], (GROUPS, FRAMES, CAP, D), 1.0, 6.0, ((0, 4), (1, 8))),
        "cotangent": scatter_about(seeds[1], (GROUPS, FRAMES, CAP, D), 1.0, 6.0, ((0, 4), (1, 8))),
        "patch_counts": draw_patch_counts(jax.random.fold_in(seeds[14], 71), 0),
        "assignment": draw_assignment(jax.random.fold_in(seeds[14], 71), 0),
        "timesteps": with_ends(jax.random.randint(seeds[4], (ITEMS,), 0, TIMESTEPS), jax.random.fold_in(seeds[4], 1), 0, TIMESTEPS - 1).astype(jnp.int32),
        "class_ids": with_ends(jax.random.randint(seeds[5], (ITEMS,), 0, CLASSES), jax.random.fold_in(seeds[5], 1), 0, CLASSES - 1).astype(jnp.int32),
        "w_qkv": scatter_about(seeds[6], (D, 3 * D), D ** -0.5, 0.1875, ((0, 8),)),
        "w_out": scatter_about(seeds[7], (D, D), (D // 16) ** -0.5, 0.75, ((0, 8),)),
        "w_fc1": scatter_about(seeds[8], (D, FF), D ** -0.5, 0.1875, ((0, 8),)),
        "b_fc1": scatter_about(seeds[9], (FF,), 0.5, 3.0, ((0, 8),)),
        "w_fc2": scatter_about(seeds[10], (FF, D), FF ** -0.5, 0.09375, ((0, 8),)),
        "w_ada": scatter_about(seeds[11], (D, 6 * D), D ** -0.5, 0.1875, ((1, 8),)),
        "b_ada": scatter_about(seeds[12], (6 * D,), 0.5, 3.0, ((0, 8),)),
        "class_table": scatter_about(seeds[13], (CLASSES, D), 1.0, 6.0, (), jnp.float32),
    }


@jax.custom_vjp
def low(v):
    return lax.optimization_barrier(v.astype(jnp.bfloat16)).astype(jnp.float32)

@jax.custom_vjp
def low_back(v):
    return v

def low_keep(v):
    return (low(v), None)

def low_pass(kept, grad):
    return (grad,)

def back_keep(v):
    return (v, None)

def back_low(kept, grad):
    return (low(grad),)
low.defvjp(low_keep, low_pass)
low_back.defvjp(back_keep, back_low)
HIGHEST = lax.Precision.HIGHEST

def layer_norm(values):
    center = values - lax.optimization_barrier(jnp.mean(values, axis=-1, keepdims=True))
    return center * lax.rsqrt(lax.optimization_barrier(jnp.mean(center * center, axis=-1, keepdims=True)) + 1e-06)

def time_features(timesteps):
    half_width = D // 2
    frequency = jnp.exp(-math.log(10000.0) * jnp.arange(half_width, dtype=jnp.float32) / half_width)
    angles = timesteps.astype(jnp.float32)[:, None] * frequency[None, :]
    return jnp.concatenate([jnp.cos(angles), jnp.sin(angles)], axis=1)

def row_items(patch_counts, assignment, group_idx, total):
    numbers = jnp.arange(patch_counts.shape[0], dtype=jnp.int32)
    same_group = assignment[None, :] == assignment[:, None]
    earlier = numbers[None, :] < numbers[:, None]
    offsets = lax.optimization_barrier(jnp.sum(jnp.where(same_group & earlier, patch_counts[None, :], 0), axis=1))
    row_ids = jnp.arange(total, dtype=jnp.int32)[:, None]
    inside = (assignment[None, :] == group_idx) & (row_ids >= offsets[None, :]) & (row_ids < offsets[None, :] + patch_counts[None, :])
    return inside.astype(jnp.float32)

def block_rows(inputs, row_mod, valid_rows, w_qkv, w_out, w_fc1, b_fc1, w_fc2):
    frames, row_count, model_width = inputs.shape
    head_dim = model_width // HEADS
    attn_scale = 1.0 / math.sqrt(head_dim)
    shift_attn, scale_attn, gate_attn, shift_mlp, scale_mlp, gate_mlp = jnp.split(row_mod, 6, axis=1)
    first_in = low(layer_norm(inputs) * (1.0 + scale_attn) + shift_attn)
    projected = low(low_back(jnp.einsum('fpd,de->fpe', first_in, w_qkv, precision=HIGHEST)))
    queries = projected[..., :model_width].reshape(frames, row_count, HEADS, head_dim)
    key_rows = projected[..., model_width:2 * model_width].reshape(frames, row_count, HEADS, head_dim)
    value_rows = projected[..., 2 * model_width:].reshape(frames, row_count, HEADS, head_dim)
    scores = low_back(jnp.einsum('iphd,jphd->phij', queries, key_rows, precision=HIGHEST) * attn_scale)
    attn_prob = jax.nn.softmax(scores, axis=-1)
    mixed_heads = jnp.einsum('phij,jphd->iphd', low(attn_prob), value_rows, precision=HIGHEST)
    mixed_heads = low(low_back(mixed_heads)).reshape(frames, row_count, model_width)
    attn_out = low_back(jnp.einsum('fpd,de->fpe', mixed_heads, w_out, precision=HIGHEST))
    middle = inputs + gate_attn * attn_out
    second_in = low(layer_norm(middle) * (1.0 + scale_mlp) + shift_mlp)
    pre_act = low_back(jnp.einsum('fpd,de->fpe', second_in, w_fc1, precision=HIGHEST) + b_fc1)
    post_act = low(jax.nn.gelu(pre_act, approximate=True))
    mlp_out = low_back(jnp.einsum('fpe,ed->fpd', post_act, w_fc2, precision=HIGHEST))
    return valid_rows[None, :, None] * (middle + gate_mlp * mlp_out)

def reference(tokens, cotangent, patch_counts, assignment, timesteps, class_ids, w_qkv, w_out, w_fc1, b_fc1, w_fc2, w_ada, b_ada, class_table):
    group_ids = jnp.arange(GROUPS, dtype=jnp.int32)
    layouts = lax.map(lambda group_idx: row_items(patch_counts, assignment, group_idx, CAP), group_ids)
    features = time_features(timesteps)
    floats = [array.astype(jnp.float32) for array in (tokens, w_qkv, w_out, w_fc1, b_fc1, w_fc2, w_ada, b_ada, class_table)]

    def forward(inputs, w_qkv, w_out, w_fc1, b_fc1, w_fc2, w_ada, b_ada, table_rows):
        condition = features + table_rows[class_ids]
        modulation = low(jnp.dot(jax.nn.silu(condition), w_ada, precision=HIGHEST) + b_ada)

        def one_group(carried, pair_in):
            group_in, layout = pair_in
            row_mod = jnp.dot(layout, modulation, precision=HIGHEST)
            valid_rows = lax.optimization_barrier(jnp.sum(layout, axis=1))
            return (carried, block_rows(group_in, row_mod, valid_rows, w_qkv, w_out, w_fc1, b_fc1, w_fc2))
        _, result = lax.scan(jax.checkpoint(one_group), jnp.zeros((), jnp.float32), (inputs, layouts))
        return result
    result, pullback = jax.vjp(forward, *floats)
    gradients = pullback(cotangent.astype(jnp.float32))
    return (result.astype(jnp.bfloat16), gradients[0].astype(jnp.bfloat16), gradients[1], gradients[2], gradients[3], gradients[4], gradients[5], gradients[6], gradients[7], gradients[8])
```

```python
import math

import jax
import jax.numpy as jnp
from jax import lax
from jax.experimental import pallas as pl
from jax.experimental.pallas import tpu as pltpu
from jax.sharding import PartitionSpec as P

D = 1152
HEADS = 16
CLASSES = 101


HIGHEST = lax.Precision.HIGHEST
ROW_DIMS = (((0,), (0,)), ((), ()))
COL_DIMS = (((1,), (1,)), ((), ()))


def layer_norm(values):
    center = values - jnp.mean(values, axis=-1, keepdims=True)
    return center * lax.rsqrt(jnp.mean(center * center, axis=-1, keepdims=True) + 1e-06)


def time_features(timesteps):
    half_width = D // 2
    frequency = jnp.exp(-math.log(10000.0) * jnp.arange(half_width, dtype=jnp.float32) / half_width)
    angles = timesteps.astype(jnp.float32)[:, None] * frequency[None, :]
    return jnp.concatenate([jnp.cos(angles), jnp.sin(angles)], axis=1)


def row_items(patch_counts, assignment, group_idx, total):
    numbers = jnp.arange(patch_counts.shape[0], dtype=jnp.int32)
    same_group = assignment[None, :] == assignment[:, None]
    earlier = numbers[None, :] < numbers[:, None]
    offsets = jnp.sum(jnp.where(same_group & earlier, patch_counts[None, :], 0), axis=1)
    row_ids = jnp.arange(total, dtype=jnp.int32)[:, None]
    inside = (
        (assignment[None, :] == group_idx)
        & (row_ids >= offsets[None, :])
        & (row_ids < offsets[None, :] + patch_counts[None, :])
    )
    return inside.astype(jnp.float32)


def gelu_tanh(pre_vals):
    return jax.nn.gelu(pre_vals, approximate=True)

LANES = 128


def head_windows(heads, head_dim):
    windows = []
    for head in range(heads):
        low, high = head * head_dim, (head + 1) * head_dim
        windows.append((low // LANES * LANES, -(-high // LANES) * LANES, low, high))
    return windows


def lane_mask(window):
    start, end, low, high = window
    lanes = start + lax.broadcasted_iota(jnp.int32, (1, end - start), 1)
    return ((lanes >= low) & (lanes < high)).astype(jnp.float32).astype(jnp.bfloat16)


def add_window(totals, window, value):
    start, end, _, _ = window
    for lane in range(start, end, LANES):
        piece = value[:, lane - start : lane - start + LANES]
        totals[lane] = piece if lane not in totals else totals[lane] + piece


def joined(totals):
    return jnp.concatenate([totals[lane] for lane in sorted(totals)], axis=1)


def same_position(rows, frames):
    left = lax.broadcasted_iota(jnp.int32, (rows, rows), 0) // frames
    right = lax.broadcasted_iota(jnp.int32, (rows, rows), 1) // frames
    return left == right


def head_probs(queries, keys, inside, scale):
    scores = lax.dot_general(queries, keys, COL_DIMS, preferred_element_type=jnp.float32) * scale
    scores = jnp.where(inside, scores, -1e30)
    weights = jnp.exp(scores - jnp.max(scores, axis=1, keepdims=True))
    return weights / jnp.sum(weights, axis=1, keepdims=True)


def attend_kernel(frames, scale, proj_ref, mixed_ref):
    rows, width = mixed_ref.shape
    inside = same_position(rows, frames)
    totals = {}
    for window in head_windows(HEADS, width // HEADS):
        cols = slice(window[0], window[1])
        mask = lane_mask(window)
        prob = head_probs(proj_ref[0, :, cols] * mask, proj_ref[1, :, cols], inside, scale)
        add_window(
            totals,
            window,
            jnp.dot(
                prob.astype(jnp.bfloat16),
                proj_ref[2, :, cols] * mask,
                preferred_element_type=jnp.float32,
            ),
        )
    mixed_ref[...] = joined(totals).astype(jnp.bfloat16)


def attend_back_kernel(frames, scale, proj_ref, grad_ref, out_ref):
    rows, width = grad_ref.shape
    inside = same_position(rows, frames)
    to_query, to_key, to_value = {}, {}, {}
    for window in head_windows(HEADS, width // HEADS):
        cols = slice(window[0], window[1])
        mask = lane_mask(window)
        queries = proj_ref[0, :, cols] * mask
        keys = proj_ref[1, :, cols]
        grads = grad_ref[:, cols] * mask
        prob = head_probs(queries, keys, inside, scale)
        grad_prob = lax.dot_general(
            grads, proj_ref[2, :, cols], COL_DIMS, preferred_element_type=jnp.float32
        )
        weighted = prob * grad_prob
        grad_scores = weighted - prob * jnp.sum(weighted, axis=1, keepdims=True)
        grad_scores = grad_scores.astype(jnp.bfloat16)
        add_window(
            to_value,
            window,
            lax.dot_general(
                prob.astype(jnp.bfloat16), grads, ROW_DIMS, preferred_element_type=jnp.float32
            ),
        )
        add_window(
            to_query,
            window,
            jnp.dot(grad_scores, keys * mask, preferred_element_type=jnp.float32),
        )
        add_window(
            to_key,
            window,
            lax.dot_general(grad_scores, queries, ROW_DIMS, preferred_element_type=jnp.float32),
        )
    out_ref[0] = (joined(to_query) * scale).astype(jnp.bfloat16)
    out_ref[1] = (joined(to_key) * scale).astype(jnp.bfloat16)
    out_ref[2] = joined(to_value).astype(jnp.bfloat16)


def tile_rows(positions, frames):
    for count in (8, 4, 2):
        if positions % count == 0:
            return count * frames
    return frames


def attend(projected, positions, frames, scale):
    _, rows, width = projected.shape
    tile = tile_rows(positions, frames)
    return pl.pallas_call(
        lambda *refs: attend_kernel(frames, scale, *refs),
        out_shape=jax.ShapeDtypeStruct((rows, width), jnp.bfloat16),
        grid=(rows // tile,),
        in_specs=[pl.BlockSpec((3, tile, width), lambda step: (0, step, 0))],
        out_specs=pl.BlockSpec((tile, width), lambda step: (step, 0)),
        cost_estimate=pl.CostEstimate(
            flops=22 * 10**9, bytes_accessed=8 * rows * width, transcendentals=0
        ),
        compiler_params=pltpu.CompilerParams(vmem_limit_bytes=40 << 20),
        name="attend",
    )(projected)


def attend_back(projected, grad_mixed, positions, frames, scale):
    _, rows, width = projected.shape
    tile = tile_rows(positions, frames)
    return pl.pallas_call(
        lambda *refs: attend_back_kernel(frames, scale, *refs),
        out_shape=jax.ShapeDtypeStruct((3, rows, width), jnp.bfloat16),
        grid=(rows // tile,),
        in_specs=[
            pl.BlockSpec((3, tile, width), lambda step: (0, step, 0)),
            pl.BlockSpec((tile, width), lambda step: (step, 0)),
        ],
        out_specs=pl.BlockSpec((3, tile, width), lambda step: (0, step, 0)),
        cost_estimate=pl.CostEstimate(
            flops=46 * 10**9, bytes_accessed=14 * rows * width, transcendentals=0
        ),
        compiler_params=pltpu.CompilerParams(vmem_limit_bytes=40 << 20),
        name="attend_back",
    )(projected, grad_mixed)


VMEM_LIMIT = 52 << 20
BF16, F32 = jnp.bfloat16, jnp.float32


def row_tile(rows):
    for tile in (224, 128, 112, 64, 32, 16):
        if rows % tile == 0:
            return tile
    return rows


def dot(left, right, dims=(((1,), (0,)), ((), ()))):
    return lax.dot_general(left, right, dims, preferred_element_type=F32)


def call(kernel, name, grid, ins, outs, scratch=(), flops=0, vmem=VMEM_LIMIT):
    moved = sum(array.size * array.dtype.itemsize for array, _ in ins)
    moved += sum(math.prod(shape) * jnp.dtype(dtype).itemsize for shape, dtype, _ in outs)
    return pl.pallas_call(
        kernel,
        out_shape=[jax.ShapeDtypeStruct(shape, dtype) for shape, dtype, _ in outs],
        grid=grid,
        in_specs=[spec for _, spec in ins],
        out_specs=[spec for _, _, spec in outs],
        scratch_shapes=list(scratch),
        cost_estimate=pl.CostEstimate(flops=flops, bytes_accessed=moved, transcendentals=0),
        compiler_params=pltpu.CompilerParams(vmem_limit_bytes=vmem),
        name=name,
    )(*[array for array, _ in ins])


HBM = pl.BlockSpec(memory_space=pl.ANY)
SCALARS = pl.BlockSpec(memory_space=pltpu.SMEM)


def whole(array):
    return pl.BlockSpec(array.shape, lambda step: (0,) * array.ndim)


def tiled(tile, width):
    return pl.BlockSpec((tile, width), lambda step: (step, 0))


class Pieces:
    def __init__(self, arrays, places, shape, slot_first):
        self.arrays, self.places, self.shape, self.slot_first = arrays, places, shape, slot_first

    def start(self, where_ref, refs, full, sems):
        for ref, place in zip(refs, self.places):
            slot, first, count = place(where_ref[0], where_ref[1])
            span = pl.ds(first, count)
            target = full.at[slot, span] if self.slot_first else full.at[span, slot]
            pltpu.make_async_copy(ref, target, sems.at[slot]).start()

    def wait(self, slot, full, sems):
        part = full.at[slot] if self.slot_first else full.at[:, slot]
        pltpu.make_async_copy(part, part, sems.at[slot]).wait()

    def scratch(self):
        return [pltpu.VMEM(self.shape, BF16), pltpu.SemaphoreType.DMA((5,))]


def norm_parts(values):
    center = values - jnp.mean(values, axis=1, keepdims=True)
    inverse = lax.rsqrt(jnp.mean(center * center, axis=1, keepdims=True) + 1e-06)
    return center * inverse, inverse


def norm_back(normed, inverse, grad):
    mean_grad = jnp.mean(grad, axis=1, keepdims=True)
    mean_both = jnp.mean(grad * normed, axis=1, keepdims=True)
    return (grad - mean_grad - normed * mean_both) * inverse


def row_order(rows, first, count, inner, outer):
    at = first + lax.broadcasted_iota(jnp.int32, (count, rows), 0)
    source = lax.broadcasted_iota(jnp.int32, (count, rows), 1)
    return (source == (at % outer) * inner + at // outer).astype(F32).astype(BF16)


def clip_sums(hot, values):
    high = values.astype(BF16)
    low = (values - high.astype(F32)).astype(BF16)
    return dot(hot, high, ROW_DIMS) + dot(hot, low, ROW_DIMS)


def add_into(ref, index, value):
    @pl.when(pl.program_id(0) == 0)
    def _():
        ref[index] = jnp.zeros_like(ref[index])

    ref[index] += value


def qkv_call(where, arrived, hot, mod, pieces, positions, frames):
    rows, width = arrived.shape
    tile = row_tile(rows)
    steps = rows // tile
    count = len(pieces.arrays)

    def kernel(where_ref, x_ref, hot_ref, mod_ref, *rest):
        piece_refs, rest = rest[:count], rest[count:]
        x_out, first_out, proj_out, full_out, full, sems = rest
        step = pl.program_id(0)

        @pl.when(step == 0)
        def _():
            pieces.start(where_ref, piece_refs, full, sems)

        order = row_order(rows, step * tile, tile, positions, frames)
        inputs = dot(order, x_ref[...])
        x_out[...] = inputs.astype(BF16)
        normed, _ = norm_parts(inputs)
        shift = dot(hot_ref[...], mod_ref[:, :width])
        scale = dot(hot_ref[...], mod_ref[:, width : 2 * width])
        first = (normed * (1.0 + scale) + shift).astype(BF16)
        first_out[...] = first
        back = pltpu.make_async_copy(full, full_out, sems.at[4])

        @pl.when(step == 0)
        def _():
            for slot in range(4):
                pieces.wait(slot, full, sems)
            back.start()

        for slot in range(3):
            proj_out[slot] = dot(first, full[slot]).astype(BF16)

        @pl.when(step == steps - 1)
        def _():
            back.wait()

    return call(
        kernel,
        "project",
        (steps,),
        [
            (where, SCALARS),
            (arrived, whole(arrived)),
            (hot, tiled(tile, hot.shape[1])),
            (mod, whole(mod)),
            *[(array, HBM) for array in pieces.arrays],
        ],
        [
            ((rows, width), BF16, tiled(tile, width)),
            ((rows, width), BF16, tiled(tile, width)),
            ((3, rows, width), BF16, pl.BlockSpec((3, tile, width), lambda step: (0, step, 0))),
            (pieces.shape, BF16, HBM),
        ],
        pieces.scratch(),
        flops=20 * 10**9,
    )


def out_call(mixed, x_rows, hot, mod, full_attn):
    rows, width = mixed.shape
    tile = row_tile(rows)

    def kernel(mixed_ref, x_ref, hot_ref, mod_ref, w_ref, attn_out, middle_out, second_out):
        attn = dot(mixed_ref[...], w_ref[0])
        hot = hot_ref[...]
        middle = x_ref[...].astype(F32) + dot(hot, mod_ref[:, 2 * width : 3 * width]) * attn
        normed, _ = norm_parts(middle)
        shift = dot(hot, mod_ref[:, 3 * width : 4 * width])
        scale = dot(hot, mod_ref[:, 4 * width : 5 * width])
        attn_out[...] = attn.astype(BF16)
        middle_out[...] = middle
        second_out[...] = (normed * (1.0 + scale) + shift).astype(BF16)

    return call(
        kernel,
        "attn_out",
        (rows // tile,),
        [
            (mixed, tiled(tile, width)),
            (x_rows, tiled(tile, width)),
            (hot, tiled(tile, hot.shape[1])),
            (mod, whole(mod)),
            (full_attn, pl.BlockSpec((1, width, width), lambda step: (3, 0, 0))),
        ],
        [
            ((rows, width), BF16, tiled(tile, width)),
            ((rows, width), F32, tiled(tile, width)),
            ((rows, width), BF16, tiled(tile, width)),
        ],
        flops=9 * 10**9,
    )


GELU_A = math.sqrt(2.0 / math.pi)
GELU_B = GELU_A * 0.044715


def fc1_call(where, second_in, bias, pieces):
    rows, width = second_in.shape
    tile = row_tile(rows)
    steps = rows // tile
    count = len(pieces.arrays)
    part = pieces.shape[2]

    def kernel(where_ref, x_ref, bias_ref, *rest):
        piece_refs, rest = rest[:count], rest[count:]
        post_out, slope_out, full_out, full, sems = rest
        step = pl.program_id(0)
        back = pltpu.make_async_copy(full, full_out, sems.at[4])

        @pl.when(step == 0)
        def _():
            pieces.start(where_ref, piece_refs, full, sems)
            for slot in range(4):
                pieces.wait(slot, full, sems)
            back.start()

        for slot in range(4):
            cols = slice(slot * part, (slot + 1) * part)
            pre = dot(x_ref[...], full[slot]) + bias_ref[:, cols].astype(F32)
            square = pre * pre
            curve = jnp.tanh(pre * (GELU_A + GELU_B * square))
            half = 0.5 + 0.5 * curve
            post_out[:, cols] = (pre * half).astype(BF16)
            rise = (0.5 * pre) * (1.0 - curve * curve)
            slope_out[:, cols] = (half + rise * (GELU_A + 3.0 * GELU_B * square)).astype(BF16)

        @pl.when(step == steps - 1)
        def _():
            back.wait()

    return call(
        kernel,
        "fc1",
        (steps,),
        [
            (where, SCALARS),
            (second_in, tiled(tile, width)),
            (bias, whole(bias)),
            *[(array, HBM) for array in pieces.arrays],
        ],
        [
            ((rows, 4 * part), BF16, tiled(tile, 4 * part)),
            ((rows, 4 * part), BF16, tiled(tile, 4 * part)),
            (pieces.shape, BF16, HBM),
        ],
        pieces.scratch(),
        flops=25 * 10**9,
    )


def cot_call(arrived, hot, mod, positions, frames):
    rows, width = arrived.shape
    tile = row_tile(rows)

    def kernel(cot_ref, hot_ref, mod_ref, rows_out, mlp_out):
        order = row_order(rows, pl.program_id(0) * tile, tile, positions, frames)
        hot = hot_ref[...]
        valid = jnp.sum(hot.astype(F32), axis=1, keepdims=True)
        grad = dot(order, cot_ref[...]) * valid
        rows_out[...] = grad.astype(BF16)
        mlp_out[...] = (grad * dot(hot, mod_ref[:, 5 * width :])).astype(BF16)

    return call(
        kernel,
        "cotangent",
        (rows // tile,),
        [
            (arrived, whole(arrived)),
            (hot, tiled(tile, hot.shape[1])),
            (mod, whole(mod)),
        ],
        [
            ((rows, width), BF16, tiled(tile, width)),
            ((rows, width), BF16, tiled(tile, width)),
        ],
        flops=6 * 10**9,
    )


def fc2_call(where, post_act, slope, grad_mlp, grad_rows, middle, hot, mod, pieces, positions, frames):
    rows, hidden = post_act.shape
    width = grad_mlp.shape[1]
    tile = row_tile(rows)
    steps = rows // tile
    count = len(pieces.arrays)
    clips = hot.shape[1]
    turns = pieces.shape[0] // 4
    part = hidden // 4

    def kernel(where_ref, post_ref, slope_ref, gmlp_ref, grows_ref, mid_ref, hot_ref, mod_ref, *rest):
        piece_refs, rest = rest[:count], rest[count:]
        block_out, pre_out, bias_out, gate_out, full, sems, held = rest
        step = pl.program_id(0)

        @pl.when(step == 0)
        def _():
            pieces.start(where_ref, piece_refs, full, sems)
            for slot in range(4):
                pieces.wait(slot, full, sems)

        total = None
        for at in range(4):
            cols = slice(at * part, (at + 1) * part)
            weight = full[at * turns : (at + 1) * turns].reshape(part, width)
            term = dot(post_ref[:, cols], weight)
            total = term if total is None else total + term
            grad_pre = (dot(gmlp_ref[...], weight, COL_DIMS) * slope_ref[:, cols].astype(F32)).astype(BF16)
            pre_out[:, cols] = grad_pre
            add_into(
                bias_out,
                (slice(None), cols),
                jnp.sum(grad_pre.astype(F32), axis=0, keepdims=True),
            )
        hot = hot_ref[...]
        valid = jnp.sum(hot.astype(F32), axis=1, keepdims=True)
        gate = dot(hot, mod_ref[:, 5 * width :])
        result = valid * (mid_ref[...] + gate * total)
        held[pl.ds(pl.multiple_of(step * tile, 16), tile), :] = result.astype(BF16)
        add_into(gate_out, slice(None), clip_sums(hot, grows_ref[...].astype(F32) * total))

        @pl.when(step == steps - 1)
        def _():
            for at in range(steps):
                order = row_order(rows, at * tile, tile, frames, positions)
                block_out[at * tile : (at + 1) * tile, :] = dot(order, held[...]).astype(BF16)

    return call(
        kernel,
        "fc2",
        (steps,),
        [
            (where, SCALARS),
            (post_act, tiled(tile, hidden)),
            (slope, tiled(tile, hidden)),
            (grad_mlp, tiled(tile, width)),
            (grad_rows, tiled(tile, width)),
            (middle, tiled(tile, width)),
            (hot, tiled(tile, clips)),
            (mod, whole(mod)),
            *[(array, HBM) for array in pieces.arrays],
        ],
        [
            ((rows, width), BF16, pl.BlockSpec((rows, width), lambda step: (0, 0))),
            ((rows, hidden), BF16, tiled(tile, hidden)),
            ((1, hidden), F32, pl.BlockSpec((1, hidden), lambda step: (0, 0))),
            ((clips, width), F32, pl.BlockSpec((clips, width), lambda step: (0, 0))),
        ],
        [*pieces.scratch(), pltpu.VMEM((rows, width), BF16)],
        flops=44 * 10**9,
    )


def fc1_back_call(grad_pre, full_fc1, middle, attn_out, grad_rows, hot, mod, full_attn):
    rows, hidden = grad_pre.shape
    width = middle.shape[1]
    tile = row_tile(rows)
    clips = hot.shape[1]
    part = hidden // 4

    def kernel(pre_ref, w_ref, mid_ref, attn_ref, grows_ref, hot_ref, mod_ref, wo_ref, *outs):
        gmid_out, gattn_out, gmix_out, sums_out = outs
        grad = None
        for at in range(4):
            term = dot(pre_ref[:, at * part : (at + 1) * part], w_ref[at], COL_DIMS)
            grad = term if grad is None else grad + term
        hot = hot_ref[...]
        scale = dot(hot, mod_ref[:, 4 * width : 5 * width])
        gate = dot(hot, mod_ref[:, 2 * width : 3 * width])
        normed, inverse = norm_parts(mid_ref[...])
        grad_middle = grows_ref[...].astype(F32) + norm_back(normed, inverse, grad * (1.0 + scale))
        gmid_out[...] = grad_middle
        grad_attn = (grad_middle * gate).astype(BF16)
        gattn_out[...] = grad_attn
        gmix_out[...] = dot(grad_attn, wo_ref[0], COL_DIMS).astype(BF16)
        add_into(sums_out, 0, clip_sums(hot, grad_middle * attn_ref[...].astype(F32)))
        add_into(sums_out, 1, clip_sums(hot, grad))
        add_into(sums_out, 2, clip_sums(hot, grad * normed))

    return call(
        kernel,
        "fc1_back",
        (rows // tile,),
        [
            (grad_pre, tiled(tile, hidden)),
            (full_fc1, whole(full_fc1)),
            (middle, tiled(tile, width)),
            (attn_out, tiled(tile, width)),
            (grad_rows, tiled(tile, width)),
            (hot, tiled(tile, clips)),
            (mod, whole(mod)),
            (full_attn, pl.BlockSpec((1, width, width), lambda step: (3, 0, 0))),
        ],
        [
            ((rows, width), F32, tiled(tile, width)),
            ((rows, width), BF16, tiled(tile, width)),
            ((rows, width), BF16, tiled(tile, width)),
            ((3, clips, width), F32, pl.BlockSpec((3, clips, width), lambda step: (0, 0, 0))),
        ],
        flops=32 * 10**9,
    )


def qkv_back_call(grad_proj, full_attn, x_rows, grad_middle, hot, mod, positions, frames):
    _, rows, width = grad_proj.shape
    tile = row_tile(rows)
    steps = rows // tile
    clips = hot.shape[1]

    def kernel(proj_ref, w_ref, x_ref, gmid_ref, hot_ref, mod_ref, tok_out, sums_out, held):
        step = pl.program_id(0)
        grad = None
        for at in range(3):
            term = dot(proj_ref[at], w_ref[at], COL_DIMS)
            grad = term if grad is None else grad + term
        hot = hot_ref[...]
        scale = dot(hot, mod_ref[:, width : 2 * width])
        normed, inverse = norm_parts(x_ref[...].astype(F32))
        result = gmid_ref[...] + norm_back(normed, inverse, grad * (1.0 + scale))
        held[pl.ds(pl.multiple_of(step * tile, 16), tile), :] = result.astype(BF16)
        add_into(sums_out, 0, clip_sums(hot, grad))
        add_into(sums_out, 1, clip_sums(hot, grad * normed))

        @pl.when(step == steps - 1)
        def _():
            for at in range(steps):
                order = row_order(rows, at * tile, tile, frames, positions)
                tok_out[at * tile : (at + 1) * tile, :] = dot(order, held[...]).astype(BF16)

    return call(
        kernel,
        "project_back",
        (steps,),
        [
            (grad_proj, pl.BlockSpec((3, tile, width), lambda step: (0, step, 0))),
            (full_attn, pl.BlockSpec((3, width, width), lambda step: (0, 0, 0))),
            (x_rows, tiled(tile, width)),
            (grad_middle, tiled(tile, width)),
            (hot, tiled(tile, clips)),
            (mod, whole(mod)),
        ],
        [
            ((rows, width), BF16, pl.BlockSpec((rows, width), lambda step: (0, 0))),
            ((2, clips, width), F32, pl.BlockSpec((2, clips, width), lambda step: (0, 0, 0))),
        ],
        [pltpu.VMEM((rows, width), BF16)],
        flops=23 * 10**9,
    )


def split_store(product, where_ref, keep_out, give_out, rows, slot_first):
    units = product.shape[0] // rows
    for core in range(2):

        @pl.when(where_ref[1] == core)
        def _():
            for unit in range(units):
                piece = product[unit * rows : (unit + 1) * rows]
                side = unit % 2 if slot_first else unit // 4
                out = keep_out if side == core else give_out
                if slot_first:
                    out[0, unit // 2] = piece
                else:
                    out[unit % 4, 0] = piece


def terms_out(chips, rows, width, slot_first):
    if slot_first:
        spec = pl.BlockSpec((1, chips, rows, width), lambda step: (step, 0, 0, 0))
    else:
        spec = pl.BlockSpec((4, 1, rows, width), lambda step: (0, step, 0, 0))
    return [((4, chips, rows, width), BF16, spec)] * 2


def fc2_terms(where, post_act, grad_mlp, chips):
    count, hidden = post_act.shape
    width = grad_mlp.shape[1]
    block, rows = hidden // chips, hidden // chips // 8

    def kernel(where_ref, left_ref, right_ref, keep_out, give_out):
        product = dot(left_ref[...], right_ref[...], ROW_DIMS).astype(BF16)
        split_store(product, where_ref, keep_out, give_out, rows, False)

    return call(
        kernel,
        "fc2_terms",
        (chips,),
        [
            (where, SCALARS),
            (post_act, pl.BlockSpec((count, block), lambda step: (0, step))),
            (grad_mlp, whole(grad_mlp)),
        ],
        terms_out(chips, rows, width, False),
        flops=18 * 10**9,
    )


def fc1_terms(where, second_in, grad_pre, chips):
    count, hidden = grad_pre.shape
    width = second_in.shape[1]
    rows, part = width // chips // 2, hidden // 4

    def kernel(where_ref, left_ref, right_ref, keep_out, give_out):
        product = dot(left_ref[...], right_ref[...], ROW_DIMS).astype(BF16)
        split_store(product, where_ref, keep_out, give_out, rows, True)

    return call(
        kernel,
        "fc1_terms",
        (4,),
        [
            (where, SCALARS),
            (second_in, whole(second_in)),
            (grad_pre, pl.BlockSpec((count, part), lambda step: (0, step))),
        ],
        terms_out(chips, rows, part, True),
        flops=18 * 10**9,
    )


def attn_terms(where, first_in, grad_proj, mixed, grad_attn, chips):
    count, width = first_in.shape
    rows = width // chips // 2

    def kernel(where_ref, first_ref, proj_ref, mixed_ref, attn_ref, keep_out, give_out):
        step = pl.program_id(0)

        @pl.when(step < 3)
        def _():
            product = dot(first_ref[...], proj_ref[0], ROW_DIMS).astype(BF16)
            split_store(product, where_ref, keep_out, give_out, rows, True)

        @pl.when(step == 3)
        def _():
            product = dot(mixed_ref[...], attn_ref[...], ROW_DIMS).astype(BF16)
            split_store(product, where_ref, keep_out, give_out, rows, True)

    return call(
        kernel,
        "attn_terms",
        (4,),
        [
            (where, SCALARS),
            (first_in, whole(first_in)),
            (
                grad_proj,
                pl.BlockSpec((1, count, width), lambda step: (jnp.minimum(step, 2), 0, 0)),
            ),
            (mixed, whole(mixed)),
            (grad_attn, whole(grad_attn)),
        ],
        terms_out(chips, rows, width, True),
        flops=19 * 10**9,
    )


X_SWAP = [(0, 1), (1, 0), (2, 3), (3, 2)]
Y_SWAP = [(0, 2), (2, 0), (1, 3), (3, 1)]


def swap_x(value):
    return lax.ppermute(value, "item", X_SWAP)


def swap_y(value):
    return lax.ppermute(value, "item", Y_SWAP)


def swap_core(value):
    count = lax.axis_size("frame")
    return lax.ppermute(value, "frame", [(at, at ^ 1) for at in range(count)])


def is_square():
    return lax.axis_size("item") == 4 and lax.axis_size("frame") % 2 == 0


def after(value, *others):
    return lax.optimization_barrier((value, *others))[0]


def after2(values, *others):
    return lax.optimization_barrier((*values, *others))[: len(values)]


def pick(stack, index):
    return lax.dynamic_index_in_dim(stack, index, 0, keepdims=False)


def by_column_quarter(stack):
    return jnp.concatenate([stack[part] for part in range(4)], axis=1)


def gather_frame(parts):
    if not is_square():
        return lax.all_gather(parts, "frame", axis=1)
    return lax.all_gather(pick(parts, lax.axis_index("item")), "frame", axis=0)


class Spread:
    def __init__(self, gathered, slot_first):
        self.gathered, self.slot_first = gathered, slot_first
        self.square = is_square()

    def near(self, *wait_for):
        if not self.square:
            return ()
        self.gathered = after(self.gathered, *wait_for)
        half = self.gathered.shape[0] // 2
        core = lax.axis_index("frame") % 2
        own = lax.dynamic_slice_in_dim(self.gathered, core * half, half, 0)
        self.cut = half // 2
        self.from_x, self.from_y = swap_x(own), swap_y(own)
        return self.from_x, self.from_y

    def far(self, *wait_for):
        if not self.square:
            return ()
        from_x, from_y = after2((self.from_x, self.from_y), *wait_for)
        self.far_low, self.far_high = swap_y(from_x[: self.cut]), swap_x(from_y[self.cut :])
        self.core_x, self.core_y = swap_core(from_x), swap_core(from_y)
        return self.far_low, self.far_high

    def pieces(self):
        gathered, slot_first = self.gathered, self.slot_first
        if not self.square:
            _, count, rows, width = gathered.shape
            if slot_first:
                return Pieces(
                    [gathered[part].reshape(count * rows, width) for part in range(4)],
                    [lambda item, core, part=part: (part, 0, count * rows) for part in range(4)],
                    (4, count * rows, width),
                    True,
                )
            return Pieces(
                [gathered[part] for part in range(4)],
                [lambda item, core, part=part: (part, 0, count) for part in range(4)],
                (count, 4, rows, width),
                False,
            )
        count, rows, width = gathered.shape
        half, cut = count // 2, self.cut
        far = [self.far_low, self.far_high]
        arrays = [gathered, self.from_x, self.from_y, *far, self.core_x, self.core_y]
        arrays += [swap_core(value) for value in far]
        unit = rows if slot_first else 1
        if slot_first:
            arrays = [array.reshape(-1, width) for array in arrays]
            shape = (4, count * rows, width)
        else:
            shape = (count, 4, rows, width)
        places = [lambda item, core: (item, 0, count * unit)]
        for flip in (0, 1):
            for slot, start, length in ((1, 0, half), (2, 0, half), (3, 0, cut), (3, cut, half - cut)):
                places.append(
                    lambda item, core, flip=flip, slot=slot, start=start, length=length: (
                        item ^ slot,
                        ((core ^ flip) * half + start) * unit,
                        length * unit,
                    )
                )
        return Pieces(arrays, places, shape, slot_first)


class Collect:
    def __init__(self, keep, give):
        self.keep, self.give = keep, give
        self.item = lax.axis_index("item")

    def pair(self):
        self.got = swap_core(self.give)

    def near(self, *wait_for):
        got = after(self.got, *wait_for)
        cut = self.keep.shape[1] // 2
        item = self.item

        def low(slot):
            return pick(self.keep[:, :cut], slot) + pick(got[:, :cut], slot)

        def high(slot):
            return pick(self.keep[:, cut:], slot) + pick(got[:, cut:], slot)

        x_out = jnp.stack([low(item ^ 1), low(item ^ 3)])
        y_out = jnp.stack([high(item ^ 2), high(item ^ 3)])
        self.low, self.low_on = low(item), low(item ^ 2)
        self.high, self.high_on = high(item), high(item ^ 1)
        self.x_in, self.y_in = swap_x(x_out), swap_y(y_out)
        return self.low, self.low_on, self.high, self.high_on, x_out, y_out

    def far(self, *wait_for):
        x_in, y_in = after2((self.x_in, self.y_in), *wait_for)
        low_on, high_on = self.low_on + x_in[1], self.high_on + y_in[1]
        self.low, self.high = self.low + x_in[0], self.high + y_in[0]
        self.y_far, self.x_far = swap_y(low_on), swap_x(high_on)
        return low_on, high_on

    def line(self, *wait_for):
        y_far, x_far = after2((self.y_far, self.x_far), *wait_for)
        plane = jnp.concatenate([self.low + y_far, self.high + x_far], axis=0)
        count = lax.axis_size("frame")
        groups = [list(range(side, count, 2)) for side in range(2)]
        self.own = lax.psum_scatter(
            plane, "frame", scatter_dimension=0, tiled=False, axis_index_groups=groups
        )
        return (plane,)

    def finish(self):
        own, item = self.own, self.item
        far = lax.ppermute(own, "item", [(at, at ^ 3) for at in range(4)])
        stack = jnp.stack([own, swap_x(own), swap_y(own), far])
        return jnp.stack([pick(stack, item ^ part) for part in range(4)])


def sum_plain(partial):
    share = lax.psum_scatter(partial.astype(BF16), "frame", scatter_dimension=1, tiled=False)
    return lax.psum(share, "item")


def share_small(value):
    count = lax.axis_size("frame")
    return lax.all_to_all(
        jnp.broadcast_to(value[None], (count, *value.shape)), "frame", 0, 0, tiled=False
    )


def sum_items(value):
    if not is_square():
        return lax.psum(value.astype(BF16), "item").astype(F32)
    value = value + swap_x(value.astype(BF16)).astype(F32)
    return value + swap_y(value.astype(BF16)).astype(F32)


def round_up(number, unit):
    return -(-number // unit) * unit


def body(
    tokens,
    cotangent,
    patch_counts,
    assignment,
    timesteps,
    class_ids,
    w_qkv,
    w_out,
    w_fc1,
    b_fc1,
    w_fc2,
    w_ada,
    b_ada,
    class_table,
):
    frame_count = lax.axis_size("frame")
    group_idx = lax.axis_index("item")
    frame_pos = lax.axis_index("frame")
    _, own_frames, capacity, width = tokens.shape
    frames = own_frames * frame_count
    positions = capacity // frame_count
    rows = frames * positions
    clips = patch_counts.shape[0]
    attn_scale = 1.0 / math.sqrt(width // HEADS)
    where = jnp.stack([group_idx, frame_pos % 2, frame_pos]).astype(jnp.int32)

    def to_positions(value):
        chunks = value[0].reshape(own_frames, frame_count, positions, width).transpose(1, 0, 2, 3)
        return lax.all_to_all(chunks, "frame", 0, 0, tiled=True).reshape(rows, width)

    def to_frames(value, *wait_for):
        chunks = value.reshape(frame_count, own_frames, positions, width)
        moved = after(lax.all_to_all(chunks, "frame", 0, 0, tiled=True), *wait_for)
        return moved.transpose(1, 0, 2, 3).reshape(1, own_frames, capacity, width)

    layout = row_items(patch_counts, assignment, group_idx, capacity)
    my_rows = lax.dynamic_slice_in_dim(layout, frame_pos * positions, positions, 0)
    class_hot = (class_ids[:, None] == jnp.arange(CLASSES, dtype=jnp.int32)[None, :]).astype(F32)
    condition = time_features(timesteps) + jnp.dot(class_hot, class_table, precision=HIGHEST)
    activated = jax.nn.silu(condition)
    ada_part = jnp.dot(activated, w_ada.astype(F32), precision=HIGHEST) + b_ada.astype(F32)

    ada_cols, bias_cols = b_ada.shape[0], b_fc1.shape[0]
    small_rows, small_cols = round_up(clips + 1, 16), round_up(max(ada_cols, bias_cols), LANES)
    small = jnp.concatenate(
        [
            jnp.pad(ada_part.astype(BF16), ((0, 0), (0, small_cols - ada_cols))),
            jnp.pad(b_fc1[None], ((0, small_rows - clips - 1), (0, small_cols - bias_cols))),
        ],
        axis=0,
    )
    x_arrived = to_positions(tokens)
    small_all = share_small(after(small, x_arrived))
    clip_slots = round_up(clips, 16)
    mod = small_all[:, :clips, :ada_cols].transpose(1, 0, 2).reshape(clips, -1)
    mod = jnp.pad(mod, ((0, clip_slots - clips), (0, 0)))
    bias = small_all[:, clips, :bias_cols].reshape(1, -1)
    hot = jnp.pad(my_rows.astype(BF16), ((0, 0), (0, clip_slots - clips)))
    hot = jnp.repeat(hot, frames, axis=0)

    shard_rows = w_out.shape[0]
    got_attn = gather_frame(jnp.stack([*jnp.split(w_qkv, 3, axis=1), w_out]))
    spread_attn = Spread(got_attn, True)
    near_attn = spread_attn.near()
    got_fc1 = gather_frame(
        after(jnp.stack(jnp.split(w_fc1, 4, axis=1)), x_arrived, *near_attn)
    )
    far_attn = spread_attn.far()
    fc2_rows = w_fc2.shape[0] // 4
    got_fc2 = gather_frame(after(w_fc2.reshape(4, fc2_rows, width), *far_attn))

    square = is_square()
    chips = frame_count // 2
    spread_fc1 = Spread(got_fc1, True)
    spread_fc2 = Spread(got_fc2, False)
    cot_arrived = to_positions(after(cotangent, x_arrived))
    near_fc1 = spread_fc1.near(*far_attn)
    x_rows, first_in, projected, full_attn = qkv_call(
        where, x_arrived, hot, mod, spread_attn.pieces(), positions, frames
    )
    mixed = attend(after(projected, *near_fc1), positions, frames, attn_scale)
    far_fc1 = spread_fc1.far()
    near_fc2 = spread_fc2.near(*far_fc1)
    attn_out, middle, second_in = out_call(
        after(mixed, *far_fc1), x_rows, hot, mod, full_attn
    )
    far_fc2 = spread_fc2.far()
    grad_rows, grad_mlp = cot_call(after(cot_arrived, second_in), hot, mod, positions, frames)
    post_act, slope, full_fc1 = fc1_call(
        where, after(second_in, grad_mlp), bias, spread_fc1.pieces()
    )

    if square:
        sum_fc2 = Collect(*fc2_terms(where, post_act, after(grad_mlp, *near_fc2), chips))
        sum_fc2.pair()
        seen = (sum_fc2.give,)
    else:
        part_fc2 = lax.dot_general(post_act, grad_mlp, ROW_DIMS, preferred_element_type=F32)
        part_fc2 = part_fc2.reshape(frame_count, 4, fc2_rows, width).transpose(1, 0, 2, 3)
        seen = ()
    block_rows, grad_pre, part_bias, sum_gate_mlp = fc2_call(
        where,
        post_act,
        slope,
        after(grad_mlp, *seen),
        grad_rows,
        middle,
        hot,
        mod,
        spread_fc2.pieces(),
        positions,
        frames,
    )
    if square:
        seen = sum_fc2.near(grad_pre)
        sum_fc1 = Collect(*fc1_terms(where, second_in, after(grad_pre, *seen), chips))
        sum_fc1.pair()
        seen = (sum_fc1.give,)
    else:
        part_fc1 = [dot(second_in, part, ROW_DIMS) for part in jnp.split(grad_pre, 4, axis=1)]
        part_fc1 = jnp.stack(part_fc1).reshape(4, frame_count, shard_rows, -1)
    grad_middle, grad_attn, grad_mixed, sums_mlp = fc1_back_call(
        after(grad_pre, *seen), full_fc1, middle, attn_out, grad_rows, hot, mod, full_attn
    )
    block_out = to_frames(block_rows, grad_mixed)
    seen = ()
    if square:
        seen = (*sum_fc2.far(grad_mixed), *sum_fc1.near(grad_mixed), block_out)
    grad_proj = attend_back(
        projected, after(grad_mixed, *seen), positions, frames, attn_scale
    )
    if square:
        seen = (*sum_fc2.line(grad_proj), *sum_fc1.far(grad_proj))
        sum_attn = Collect(
            *attn_terms(where, first_in, after(grad_proj, *seen), mixed, grad_attn, chips)
        )
        sum_attn.pair()
        seen = (*sum_fc1.line(sum_attn.give), *sum_attn.near())
    else:
        part_attn = [dot(first_in, grad_proj[part], ROW_DIMS) for part in range(3)]
        part_attn = jnp.stack([*part_attn, dot(mixed, grad_attn, ROW_DIMS)])
        part_attn = part_attn.reshape(4, frame_count, shard_rows, width)
    token_rows, sums_attn = qkv_back_call(
        after(grad_proj, *seen), full_attn, x_rows, grad_middle, hot, mod, positions, frames
    )
    if square:
        sum_attn.far(token_rows)
        sum_attn.line()
        sum_fc2, sum_fc1, sum_attn = sum_fc2.finish(), sum_fc1.finish(), sum_attn.finish()
    else:
        sum_fc2, sum_fc1, sum_attn = sum_plain(part_fc2), sum_plain(part_fc1), sum_plain(part_attn)
    part_mod = jnp.concatenate([sums_attn, sums_mlp, sum_gate_mlp[None]], axis=0)[:, :clips]
    part_mod = part_mod.transpose(1, 0, 2).reshape(clips, frame_count, ada_cols)
    part_small = jnp.concatenate(
        [
            jnp.pad(part_mod, ((0, 0), (0, 0), (0, small_cols - ada_cols))),
            jnp.pad(
                part_bias.reshape(1, frame_count, bias_cols),
                ((0, small_rows - clips - 1), (0, 0), (0, small_cols - bias_cols)),
            ),
        ],
        axis=0,
    ).astype(BF16)
    small_terms = lax.all_to_all(part_small.transpose(1, 0, 2), "frame", 0, 0, tiled=False)
    grad_tokens = to_frames(after(token_rows, small_terms))
    small_sum = sum_items(jnp.sum(small_terms.astype(F32), axis=0))
    grad_modulation = small_sum[:clips, :ada_cols]
    sum_bias = small_sum[clips, :bias_cols]
    grad_w_ada = lax.dot_general(activated, grad_modulation, ROW_DIMS, precision=HIGHEST)
    grad_b_ada = jnp.sum(grad_modulation, axis=0)
    act_part = lax.dot_general(grad_modulation, w_ada.astype(F32), COL_DIMS, precision=HIGHEST)
    grad_activated = jnp.sum(share_small(act_part.astype(BF16)).astype(F32), axis=0)
    _, silu_back = jax.vjp(jax.nn.silu, condition)
    grad_condition = silu_back(grad_activated)[0]
    grad_table = lax.dot_general(class_hot, grad_condition, ROW_DIMS, precision=HIGHEST)
    return (
        block_out,
        grad_tokens,
        by_column_quarter(sum_attn)[:, : 3 * width].astype(F32),
        sum_attn[3].astype(F32),
        by_column_quarter(sum_fc1).astype(F32),
        sum_bias,
        sum_fc2.reshape(-1, width).astype(F32),
        grad_w_ada,
        grad_b_ada,
        grad_table,
    )


def solution(mesh):
    return jax.shard_map(
        body,
        mesh=mesh,
        in_specs=(
            P("item", "frame", None, None),
            P("item", "frame", None, None),
            P(),
            P(),
            P(),
            P(),
            P("frame", None),
            P("frame", None),
            P("frame", None),
            P("frame"),
            P("frame", None),
            P(None, "frame"),
            P("frame"),
            P(),
        ),
        out_specs=(
            P("item", "frame", None, None),
            P("item", "frame", None, None),
            P("frame", None),
            P("frame", None),
            P("frame", None),
            P("frame"),
            P("frame", None),
            P(None, "frame"),
            P("frame"),
            P(),
        ),
        check_vma=False,
    )
```

```python
import math

import jax
import jax.numpy as jnp
from jax import lax
from jax.experimental import pallas as pl
from jax.experimental.pallas import tpu as pltpu
from jax.sharding import PartitionSpec as P

D = 1152
HEADS = 16
CLASSES = 101


HIGHEST = lax.Precision.HIGHEST
ROW_DIMS = (((0,), (0,)), ((), ()))
COL_DIMS = (((1,), (1,)), ((), ()))


def layer_norm(values):
    center = values - jnp.mean(values, axis=-1, keepdims=True)
    return center * lax.rsqrt(jnp.mean(center * center, axis=-1, keepdims=True) + 1e-06)


def time_features(timesteps):
    half_width = D // 2
    frequency = jnp.exp(-math.log(10000.0) * jnp.arange(half_width, dtype=jnp.float32) / half_width)
    angles = timesteps.astype(jnp.float32)[:, None] * frequency[None, :]
    return jnp.concatenate([jnp.cos(angles), jnp.sin(angles)], axis=1)


def row_items(patch_counts, assignment, group_idx, total):
    numbers = jnp.arange(patch_counts.shape[0], dtype=jnp.int32)
    same_group = assignment[None, :] == assignment[:, None]
    earlier = numbers[None, :] < numbers[:, None]
    offsets = jnp.sum(jnp.where(same_group & earlier, patch_counts[None, :], 0), axis=1)
    row_ids = jnp.arange(total, dtype=jnp.int32)[:, None]
    inside = (
        (assignment[None, :] == group_idx)
        & (row_ids >= offsets[None, :])
        & (row_ids < offsets[None, :] + patch_counts[None, :])
    )
    return inside.astype(jnp.float32)


def gelu_tanh(pre_vals):
    return jax.nn.gelu(pre_vals, approximate=True)

LANES = 128


def head_windows(heads, head_dim):
    windows = []
    for head in range(heads):
        low, high = head * head_dim, (head + 1) * head_dim
        windows.append((low // LANES * LANES, -(-high // LANES) * LANES, low, high))
    return windows


def lane_mask(window):
    start, end, low, high = window
    lanes = start + lax.broadcasted_iota(jnp.int32, (1, end - start), 1)
    return ((lanes >= low) & (lanes < high)).astype(jnp.float32).astype(jnp.bfloat16)


def add_window(totals, window, value):
    start, end, _, _ = window
    for lane in range(start, end, LANES):
        piece = value[:, lane - start : lane - start + LANES]
        totals[lane] = piece if lane not in totals else totals[lane] + piece


def joined(totals):
    return jnp.concatenate([totals[lane] for lane in sorted(totals)], axis=1)


class Spots:
    def __init__(self, rows, frames):
        self.frames = frames
        spot = lax.broadcasted_iota(jnp.int32, (frames, rows), 1) // frames
        self.own = [spot == at for at in range(rows // frames)]
        self.masks = [own.astype(jnp.float32).astype(jnp.bfloat16) for own in self.own]

    def compact(self, full):
        found = full[: self.frames]
        for at, own in enumerate(self.own[1:], 1):
            found = jnp.where(own, full[at * self.frames : (at + 1) * self.frames], found)
        return found

    def expand(self, compact):
        return jnp.concatenate([compact * mask for mask in self.masks], axis=0)

    def probs(self, queries, keys, scale):
        scores = lax.dot_general(keys, queries, COL_DIMS, preferred_element_type=jnp.float32)
        scores = self.compact(scores) * scale
        weights = jnp.exp(scores - jnp.max(scores, axis=0, keepdims=True))
        return weights / jnp.sum(weights, axis=0, keepdims=True)


def attend_kernel(frames, scale, proj_ref, mixed_ref):
    rows, width = mixed_ref.shape
    spots = Spots(rows, frames)
    totals = {}
    for window in head_windows(HEADS, width // HEADS):
        query, key, value = [
            slice(part * width + window[0], part * width + window[1]) for part in range(3)
        ]
        mask = lane_mask(window)
        prob = spots.probs(proj_ref[:, query] * mask, proj_ref[:, key], scale)
        add_window(
            totals,
            window,
            lax.dot_general(
                spots.expand(prob.astype(jnp.bfloat16)),
                proj_ref[:, value] * mask,
                ROW_DIMS,
                preferred_element_type=jnp.float32,
            ),
        )
    mixed_ref[...] = joined(totals).astype(jnp.bfloat16)


def attend_back_kernel(frames, scale, proj_ref, grad_ref, out_ref):
    rows, width = grad_ref.shape
    spots = Spots(rows, frames)
    to_query, to_key, to_value = {}, {}, {}
    for window in head_windows(HEADS, width // HEADS):
        query, key, value = [
            slice(part * width + window[0], part * width + window[1]) for part in range(3)
        ]
        mask = lane_mask(window)
        queries = proj_ref[:, query] * mask
        keys = proj_ref[:, key]
        grads = grad_ref[:, window[0] : window[1]] * mask
        prob = spots.probs(queries, keys, scale)
        grad_prob = spots.compact(
            lax.dot_general(
                proj_ref[:, value], grads, COL_DIMS, preferred_element_type=jnp.float32
            )
        )
        weighted = prob * grad_prob
        grad_scores = weighted - prob * jnp.sum(weighted, axis=0, keepdims=True)
        grad_scores = spots.expand(grad_scores.astype(jnp.bfloat16))
        prob_low = spots.expand(prob.astype(jnp.bfloat16))
        add_window(
            to_value, window, jnp.dot(prob_low, grads, preferred_element_type=jnp.float32)
        )
        add_window(
            to_key, window, jnp.dot(grad_scores, queries, preferred_element_type=jnp.float32)
        )
        add_window(
            to_query,
            window,
            lax.dot_general(
                grad_scores, keys * mask, ROW_DIMS, preferred_element_type=jnp.float32
            ),
        )
    out_ref[:, :width] = (joined(to_query) * scale).astype(jnp.bfloat16)
    out_ref[:, width : 2 * width] = (joined(to_key) * scale).astype(jnp.bfloat16)
    out_ref[:, 2 * width :] = joined(to_value).astype(jnp.bfloat16)


def tile_rows(positions, frames):
    for count in (8, 4, 2):
        if positions % count == 0:
            return count * frames
    return frames


def attend(projected, positions, frames, scale):
    rows, width = projected.shape[0], projected.shape[1] // 3
    tile = tile_rows(positions, frames)
    return pl.pallas_call(
        lambda *refs: attend_kernel(frames, scale, *refs),
        out_shape=jax.ShapeDtypeStruct((rows, width), jnp.bfloat16),
        grid=(rows // tile,),
        in_specs=[pl.BlockSpec((tile, 3 * width), lambda step: (step, 0))],
        out_specs=pl.BlockSpec((tile, width), lambda step: (step, 0)),
        cost_estimate=pl.CostEstimate(
            flops=13 * 10**9, bytes_accessed=8 * rows * width, transcendentals=0
        ),
        compiler_params=pltpu.CompilerParams(vmem_limit_bytes=VMEM_LIMIT),
        name="attend",
    )(projected)


def attend_back(projected, grad_mixed, positions, frames, scale):
    rows, width = projected.shape[0], projected.shape[1] // 3
    tile = tile_rows(positions, frames)
    return pl.pallas_call(
        lambda *refs: attend_back_kernel(frames, scale, *refs),
        out_shape=jax.ShapeDtypeStruct((rows, 3 * width), jnp.bfloat16),
        grid=(rows // tile,),
        in_specs=[
            pl.BlockSpec((tile, 3 * width), lambda step: (step, 0)),
            pl.BlockSpec((tile, width), lambda step: (step, 0)),
        ],
        out_specs=pl.BlockSpec((tile, 3 * width), lambda step: (step, 0)),
        cost_estimate=pl.CostEstimate(
            flops=27 * 10**9, bytes_accessed=14 * rows * width, transcendentals=0
        ),
        compiler_params=pltpu.CompilerParams(vmem_limit_bytes=VMEM_LIMIT),
        name="attend_back",
    )(projected, grad_mixed)


VMEM_LIMIT = 58 << 20
BF16, F32 = jnp.bfloat16, jnp.float32


def row_tile(rows):
    for tile in (224, 128, 112, 64, 32, 16):
        if rows % tile == 0:
            return tile
    return rows


def dot(left, right, dims=(((1,), (0,)), ((), ()))):
    return lax.dot_general(left, right, dims, preferred_element_type=F32)


def call(kernel, name, grid, ins, outs, scratch=(), flops=0, vmem=VMEM_LIMIT):
    moved = sum(array.size * array.dtype.itemsize for array, _ in ins)
    moved += sum(math.prod(shape) * jnp.dtype(dtype).itemsize for shape, dtype, _ in outs)
    return pl.pallas_call(
        kernel,
        out_shape=[jax.ShapeDtypeStruct(shape, dtype) for shape, dtype, _ in outs],
        grid=grid,
        in_specs=[spec for _, spec in ins],
        out_specs=[spec for _, _, spec in outs],
        scratch_shapes=list(scratch),
        cost_estimate=pl.CostEstimate(flops=flops, bytes_accessed=moved, transcendentals=0),
        compiler_params=pltpu.CompilerParams(vmem_limit_bytes=vmem),
        name=name,
    )(*[array for array, _ in ins])


HBM = pl.BlockSpec(memory_space=pl.ANY)
SCALARS = pl.BlockSpec(memory_space=pltpu.SMEM)


def whole(array):
    return pl.BlockSpec(array.shape, lambda step: (0,) * array.ndim)


def tiled(tile, width):
    return pl.BlockSpec((tile, width), lambda step: (step, 0))


class Pieces:
    def __init__(self, arrays, places, shape, by_columns):
        self.arrays, self.places, self.shape, self.by_columns = arrays, places, shape, by_columns

    def start(self, where_ref, refs, full, sems):
        for ref, place in zip(refs, self.places):
            slot, first, count = place(where_ref[0], where_ref[1])
            if self.by_columns:
                width = self.shape[2] // 2
                column = pl.multiple_of(slot % 2 * width, width)
                target = full.at[slot // 2, pl.ds(first, count), pl.ds(column, width)]
                pltpu.make_async_copy(ref, target, sems.at[slot // 2]).start()
                continue
            half = self.shape[0] // 2
            for turn in range(count):
                target = full.at[first + turn, slot]
                pltpu.make_async_copy(ref.at[turn], target, sems.at[(first + turn) // half]).start()

    def part(self, full, half):
        if self.by_columns:
            return full.at[half]
        turns = self.shape[0] // 2
        return full.at[half * turns : (half + 1) * turns]

    def wait(self, half, full, sems):
        part = self.part(full, half)
        pltpu.make_async_copy(part, part, sems.at[half]).wait()

    def scratch(self):
        return [pltpu.VMEM(self.shape, BF16), pltpu.SemaphoreType.DMA((3,))]


def norm_parts(values):
    center = values - jnp.mean(values, axis=1, keepdims=True)
    inverse = lax.rsqrt(jnp.mean(center * center, axis=1, keepdims=True) + 1e-06)
    return center * inverse, inverse


def norm_back(normed, inverse, grad):
    mean_grad = jnp.mean(grad, axis=1, keepdims=True)
    mean_both = jnp.mean(grad * normed, axis=1, keepdims=True)
    return (grad - mean_grad - normed * mean_both) * inverse


def gather_order(first, count, frames, positions, own_frames, chunk):
    at = first + lax.broadcasted_iota(jnp.int32, (count, frames // own_frames * chunk), 0)
    source = lax.broadcasted_iota(jnp.int32, (count, frames // own_frames * chunk), 1)
    frame, position = at % frames, at // frames
    wanted = frame // own_frames * chunk + frame % own_frames * positions + position
    return (source == wanted).astype(F32).astype(BF16)


def row_order(rows, first, count, inner, outer):
    at = first + lax.broadcasted_iota(jnp.int32, (count, rows), 0)
    source = lax.broadcasted_iota(jnp.int32, (count, rows), 1)
    return (source == (at % outer) * inner + at // outer).astype(F32).astype(BF16)


def clip_sums(hot, values):
    high = values.astype(BF16)
    low = (values - high.astype(F32)).astype(BF16)
    return dot(hot, high, ROW_DIMS) + dot(hot, low, ROW_DIMS)


def first_step(step, action):
    @pl.when(step == 0)
    def _():
        action()


def add_into(ref, index, value):
    @pl.when(pl.program_id(0) == 0)
    def _():
        ref[index] = jnp.zeros_like(ref[index])

    ref[index] += value


def qkv_call(where, arrived, hot, mod, pieces, positions, frames, own_frames):
    rows, width = positions * frames, arrived.shape[1]
    chunk = arrived.shape[0] * own_frames // frames
    tile = row_tile(rows)
    steps = rows // tile
    count = len(pieces.arrays)

    def kernel(where_ref, x_ref, hot_ref, mod_ref, *rest):
        piece_refs, rest = rest[:count], rest[count:]
        x_out, first_out, proj_out, full_out, full, sems = rest
        step = pl.program_id(0)

        @pl.when(step == 0)
        def _():
            pieces.start(where_ref, piece_refs, full, sems)

        order = gather_order(step * tile, tile, frames, positions, own_frames, chunk)
        inputs = dot(order, x_ref[...])
        x_out[...] = inputs.astype(BF16)
        normed, _ = norm_parts(inputs)
        shift = dot(hot_ref[...], mod_ref[:, :width])
        scale = dot(hot_ref[...], mod_ref[:, width : 2 * width])
        first = (normed * (1.0 + scale) + shift).astype(BF16)
        first_out[...] = first
        back = pltpu.make_async_copy(full, full_out, sems.at[2])
        first_step(step, lambda: pieces.wait(0, full, sems))
        proj_out[:, : 2 * width] = dot(first, full[0]).astype(BF16)
        first_step(step, lambda: pieces.wait(1, full, sems))
        first_step(step, back.start)
        proj_out[:, 2 * width :] = dot(first, full[1, :, :width]).astype(BF16)

        @pl.when(step == steps - 1)
        def _():
            back.wait()

    return call(
        kernel,
        "project",
        (steps,),
        [
            (where, SCALARS),
            (arrived, whole(arrived)),
            (hot, tiled(tile, hot.shape[1])),
            (mod, whole(mod)),
            *[(array, HBM) for array in pieces.arrays],
        ],
        [
            ((rows, width), BF16, tiled(tile, width)),
            ((rows, width), BF16, tiled(tile, width)),
            ((rows, 3 * width), BF16, tiled(tile, 3 * width)),
            (pieces.shape, BF16, HBM),
        ],
        pieces.scratch(),
        flops=20 * 10**9,
    )


def out_call(mixed, x_rows, hot, mod, full_attn):
    rows, width = mixed.shape
    tile = row_tile(rows)

    def kernel(mixed_ref, x_ref, hot_ref, mod_ref, w_ref, attn_out, middle_out, second_out):
        attn = dot(mixed_ref[...], w_ref[0])
        hot = hot_ref[...]
        middle = x_ref[...].astype(F32) + dot(hot, mod_ref[:, 2 * width : 3 * width]) * attn
        normed, _ = norm_parts(middle)
        shift = dot(hot, mod_ref[:, 3 * width : 4 * width])
        scale = dot(hot, mod_ref[:, 4 * width : 5 * width])
        attn_out[...] = attn.astype(BF16)
        middle_out[...] = middle
        second_out[...] = (normed * (1.0 + scale) + shift).astype(BF16)

    return call(
        kernel,
        "attn_out",
        (rows // tile,),
        [
            (mixed, tiled(tile, width)),
            (x_rows, tiled(tile, width)),
            (hot, tiled(tile, hot.shape[1])),
            (mod, whole(mod)),
            (full_attn, pl.BlockSpec((1, width, width), lambda step: (1, 0, 1))),
        ],
        [
            ((rows, width), BF16, tiled(tile, width)),
            ((rows, width), F32, tiled(tile, width)),
            ((rows, width), BF16, tiled(tile, width)),
        ],
        flops=9 * 10**9,
    )


GELU_A = math.sqrt(2.0 / math.pi)
GELU_B = GELU_A * 0.044715


def fc1_call(where, second_in, bias, pieces):
    rows, width = second_in.shape
    tile = row_tile(rows)
    steps = rows // tile
    count = len(pieces.arrays)
    part = pieces.shape[2]

    def kernel(where_ref, x_ref, bias_ref, *rest):
        piece_refs, rest = rest[:count], rest[count:]
        post_out, slope_out, full_out, full, sems = rest
        step = pl.program_id(0)
        back = pltpu.make_async_copy(full, full_out, sems.at[2])
        first_step(step, lambda: pieces.start(where_ref, piece_refs, full, sems))
        for half in range(2):
            first_step(step, lambda half=half: pieces.wait(half, full, sems))
            if half:
                first_step(step, back.start)
            cols = slice(half * part, (half + 1) * part)
            pre = dot(x_ref[...], full[half]) + bias_ref[:, cols].astype(F32)
            square = pre * pre
            curve = jnp.tanh(pre * (GELU_A + GELU_B * square))
            half = 0.5 + 0.5 * curve
            post_out[:, cols] = (pre * half).astype(BF16)
            rise = (0.5 * pre) * (1.0 - curve * curve)
            slope_out[:, cols] = (half + rise * (GELU_A + 3.0 * GELU_B * square)).astype(BF16)

        @pl.when(step == steps - 1)
        def _():
            back.wait()

    return call(
        kernel,
        "fc1",
        (steps,),
        [
            (where, SCALARS),
            (second_in, tiled(tile, width)),
            (bias, whole(bias)),
            *[(array, HBM) for array in pieces.arrays],
        ],
        [
            ((rows, 2 * part), BF16, tiled(tile, 2 * part)),
            ((rows, 2 * part), BF16, tiled(tile, 2 * part)),
            (pieces.shape, BF16, HBM),
        ],
        pieces.scratch(),
        flops=25 * 10**9,
    )


def cot_call(arrived, hot, mod, positions, frames, own_frames):
    rows, width = arrived.shape
    tile = row_tile(rows)

    def kernel(cot_ref, hot_ref, mod_ref, rows_out, mlp_out):
        first = pl.program_id(0) * tile
        order = gather_order(first, tile, frames, positions, own_frames, own_frames * positions)
        hot = hot_ref[...]
        valid = jnp.sum(hot.astype(F32), axis=1, keepdims=True)
        grad = dot(order, cot_ref[...]) * valid
        rows_out[...] = grad.astype(BF16)
        mlp_out[...] = (grad * dot(hot, mod_ref[:, 5 * width :])).astype(BF16)

    return call(
        kernel,
        "cotangent",
        (rows // tile,),
        [
            (arrived, whole(arrived)),
            (hot, tiled(tile, hot.shape[1])),
            (mod, whole(mod)),
        ],
        [
            ((rows, width), BF16, tiled(tile, width)),
            ((rows, width), BF16, tiled(tile, width)),
        ],
        flops=6 * 10**9,
    )


def fc2_call(where, post_act, slope, grad_mlp, grad_rows, middle, hot, mod, pieces, positions, frames):
    rows, hidden = post_act.shape
    width = grad_mlp.shape[1]
    tile = row_tile(rows)
    steps = rows // tile
    count = len(pieces.arrays)
    clips = hot.shape[1]
    part = hidden // 2

    def kernel(where_ref, post_ref, slope_ref, gmlp_ref, grows_ref, mid_ref, hot_ref, mod_ref, *rest):
        piece_refs, rest = rest[:count], rest[count:]
        block_out, pre_out, bias_out, gate_out, full, sems, held = rest
        step = pl.program_id(0)

        first_step(step, lambda: pieces.start(where_ref, piece_refs, full, sems))
        total = None
        for half in range(2):
            first_step(step, lambda half=half: pieces.wait(half, full, sems))
            cols = slice(half * part, (half + 1) * part)
            weight = pieces.part(full, half)[...].reshape(part, width)
            term = dot(post_ref[:, cols], weight)
            total = term if total is None else total + term
            grad_pre = (dot(gmlp_ref[...], weight, COL_DIMS) * slope_ref[:, cols].astype(F32)).astype(BF16)
            pre_out[:, cols] = grad_pre
            add_into(
                bias_out,
                (slice(None), cols),
                jnp.sum(grad_pre.astype(F32), axis=0, keepdims=True),
            )
        hot = hot_ref[...]
        valid = jnp.sum(hot.astype(F32), axis=1, keepdims=True)
        gate = dot(hot, mod_ref[:, 5 * width :])
        result = valid * (mid_ref[...] + gate * total)
        held[pl.ds(pl.multiple_of(step * tile, 16), tile), :] = result.astype(BF16)
        add_into(gate_out, slice(None), clip_sums(hot, grows_ref[...].astype(F32) * total))

        @pl.when(step == steps - 1)
        def _():
            for at in range(steps):
                order = row_order(rows, at * tile, tile, frames, positions)
                block_out[at * tile : (at + 1) * tile, :] = dot(order, held[...]).astype(BF16)

    return call(
        kernel,
        "fc2",
        (steps,),
        [
            (where, SCALARS),
            (post_act, tiled(tile, hidden)),
            (slope, tiled(tile, hidden)),
            (grad_mlp, tiled(tile, width)),
            (grad_rows, tiled(tile, width)),
            (middle, tiled(tile, width)),
            (hot, tiled(tile, clips)),
            (mod, whole(mod)),
            *[(array, HBM) for array in pieces.arrays],
        ],
        [
            ((rows, width), BF16, pl.BlockSpec((rows, width), lambda step: (0, 0))),
            ((rows, hidden), BF16, tiled(tile, hidden)),
            ((1, hidden), F32, pl.BlockSpec((1, hidden), lambda step: (0, 0))),
            ((clips, width), F32, pl.BlockSpec((clips, width), lambda step: (0, 0))),
        ],
        [*pieces.scratch(), pltpu.VMEM((rows, width), BF16)],
        flops=44 * 10**9,
    )


def fc1_back_call(grad_pre, full_fc1, middle, attn_out, grad_rows, hot, mod, full_attn):
    rows, hidden = grad_pre.shape
    width = middle.shape[1]
    tile = row_tile(rows)
    clips = hot.shape[1]
    part = hidden // 2

    def kernel(pre_ref, w_ref, mid_ref, attn_ref, grows_ref, hot_ref, mod_ref, wo_ref, *outs):
        gmid_out, gattn_out, gmix_out, sums_out, held, sems = outs
        step = pl.program_id(0)
        loads = [pltpu.make_async_copy(w_ref.at[at], held.at[at], sems.at[at]) for at in range(2)]
        grad = None
        for at in range(2):
            if not at:
                first_step(step, loads[0].start)
                first_step(step, loads[1].start)
            first_step(step, loads[at].wait)
            term = dot(pre_ref[:, at * part : (at + 1) * part], held[at], COL_DIMS)
            grad = term if grad is None else grad + term
        hot = hot_ref[...]
        scale = dot(hot, mod_ref[:, 4 * width : 5 * width])
        gate = dot(hot, mod_ref[:, 2 * width : 3 * width])
        normed, inverse = norm_parts(mid_ref[...])
        grad_middle = grows_ref[...].astype(F32) + norm_back(normed, inverse, grad * (1.0 + scale))
        gmid_out[...] = grad_middle
        grad_attn = (grad_middle * gate).astype(BF16)
        gattn_out[...] = grad_attn
        gmix_out[...] = dot(grad_attn, wo_ref[0], COL_DIMS).astype(BF16)
        add_into(sums_out, 0, clip_sums(hot, grad_middle * attn_ref[...].astype(F32)))
        add_into(sums_out, 1, clip_sums(hot, grad))
        add_into(sums_out, 2, clip_sums(hot, grad * normed))

    return call(
        kernel,
        "fc1_back",
        (rows // tile,),
        [
            (grad_pre, tiled(tile, hidden)),
            (full_fc1, HBM),
            (middle, tiled(tile, width)),
            (attn_out, tiled(tile, width)),
            (grad_rows, tiled(tile, width)),
            (hot, tiled(tile, clips)),
            (mod, whole(mod)),
            (full_attn, pl.BlockSpec((1, width, width), lambda step: (1, 0, 1))),
        ],
        [
            ((rows, width), F32, tiled(tile, width)),
            ((rows, width), BF16, tiled(tile, width)),
            ((rows, width), BF16, tiled(tile, width)),
            ((3, clips, width), F32, pl.BlockSpec((3, clips, width), lambda step: (0, 0, 0))),
        ],
        [pltpu.VMEM(full_fc1.shape, BF16), pltpu.SemaphoreType.DMA((2,))],
        flops=32 * 10**9,
    )


def qkv_back_call(grad_proj, full_attn, x_rows, grad_middle, hot, mod, positions, frames):
    rows, width = x_rows.shape
    tile = row_tile(rows)
    steps = rows // tile
    clips = hot.shape[1]

    def kernel(proj_ref, w_ref, x_ref, gmid_ref, hot_ref, mod_ref, tok_out, sums_out, held, w_held, sems):
        step = pl.program_id(0)
        loads = [
            pltpu.make_async_copy(w_ref.at[0], w_held.at[0], sems.at[0]),
            pltpu.make_async_copy(
                w_ref.at[1, :, :width], w_held.at[1, :, :width], sems.at[1]
            ),
        ]
        first_step(step, loads[0].start)
        first_step(step, loads[1].start)
        first_step(step, loads[0].wait)
        grad = dot(proj_ref[:, : 2 * width], w_held[0], COL_DIMS)
        first_step(step, loads[1].wait)
        grad += dot(proj_ref[:, 2 * width :], w_held[1, :, :width], COL_DIMS)
        hot = hot_ref[...]
        scale = dot(hot, mod_ref[:, width : 2 * width])
        normed, inverse = norm_parts(x_ref[...].astype(F32))
        result = gmid_ref[...] + norm_back(normed, inverse, grad * (1.0 + scale))
        held[pl.ds(pl.multiple_of(step * tile, 16), tile), :] = result.astype(BF16)
        add_into(sums_out, 0, clip_sums(hot, grad))
        add_into(sums_out, 1, clip_sums(hot, grad * normed))

        @pl.when(step == steps - 1)
        def _():
            for at in range(steps):
                order = row_order(rows, at * tile, tile, frames, positions)
                tok_out[at * tile : (at + 1) * tile, :] = dot(order, held[...]).astype(BF16)

    return call(
        kernel,
        "project_back",
        (steps,),
        [
            (grad_proj, tiled(tile, 3 * width)),
            (full_attn, HBM),
            (x_rows, tiled(tile, width)),
            (grad_middle, tiled(tile, width)),
            (hot, tiled(tile, clips)),
            (mod, whole(mod)),
        ],
        [
            ((rows, width), BF16, pl.BlockSpec((rows, width), lambda step: (0, 0))),
            ((2, clips, width), F32, pl.BlockSpec((2, clips, width), lambda step: (0, 0, 0))),
        ],
        [
            pltpu.VMEM((rows, width), BF16),
            pltpu.VMEM(full_attn.shape, BF16),
            pltpu.SemaphoreType.DMA((2,)),
        ],
        flops=23 * 10**9,
    )


def split_store(product, where_ref, keep_out, give_out, rows, slot_first, slot=0):
    units = product.shape[0] // rows
    for core in range(2):

        @pl.when(where_ref[1] == core)
        def _():
            for unit in range(units):
                piece = product[unit * rows : (unit + 1) * rows]
                side = unit % 2 if slot_first else unit // 4
                out = keep_out if side == core else give_out
                if slot_first:
                    out[slot, unit // 2] = piece
                else:
                    out[unit % 4, 0] = piece


def terms_out(chips, rows, width, slot_first, slots=1):
    if slot_first:
        spec = pl.BlockSpec((slots, chips, rows, width), lambda step: (step, 0, 0, 0))
    else:
        spec = pl.BlockSpec((4, 1, rows, width), lambda step: (0, step, 0, 0))
    return [((4, chips, rows, width), BF16, spec)] * 2


def fc2_terms(where, post_act, grad_mlp, chips):
    count, hidden = post_act.shape
    width = grad_mlp.shape[1]
    block, rows = hidden // chips, hidden // chips // 8

    def kernel(where_ref, left_ref, right_ref, keep_out, give_out):
        product = dot(left_ref[...], right_ref[...], ROW_DIMS).astype(BF16)
        split_store(product, where_ref, keep_out, give_out, rows, False)

    return call(
        kernel,
        "fc2_terms",
        (chips,),
        [
            (where, SCALARS),
            (post_act, pl.BlockSpec((count, block), lambda step: (0, step))),
            (grad_mlp, whole(grad_mlp)),
        ],
        terms_out(chips, rows, width, False),
        flops=18 * 10**9,
    )


def fc1_terms(where, second_in, grad_pre, chips):
    count, hidden = grad_pre.shape
    width = second_in.shape[1]
    rows, part = width // chips // 2, hidden // 4

    def kernel(where_ref, left_ref, right_ref, keep_out, give_out):
        product = dot(left_ref[...], right_ref[...], ROW_DIMS).astype(BF16)
        for slot in range(2):
            piece = product[:, slot * part : (slot + 1) * part]
            split_store(piece, where_ref, keep_out, give_out, rows, True, slot)

    return call(
        kernel,
        "fc1_terms",
        (2,),
        [
            (where, SCALARS),
            (second_in, whole(second_in)),
            (grad_pre, pl.BlockSpec((count, 2 * part), lambda step: (0, step))),
        ],
        terms_out(chips, rows, part, True, 2),
        flops=18 * 10**9,
    )


def attn_terms(where, first_in, grad_proj, mixed, grad_attn, chips):
    count, width = first_in.shape
    rows = width // chips // 2

    def kernel(where_ref, first_ref, proj_ref, mixed_ref, attn_ref, keep_out, give_out):
        step = pl.program_id(0)

        @pl.when(step < 3)
        def _():
            product = dot(first_ref[...], proj_ref[...], ROW_DIMS).astype(BF16)
            split_store(product, where_ref, keep_out, give_out, rows, True)

        @pl.when(step == 3)
        def _():
            product = dot(mixed_ref[...], attn_ref[...], ROW_DIMS).astype(BF16)
            split_store(product, where_ref, keep_out, give_out, rows, True)

    return call(
        kernel,
        "attn_terms",
        (4,),
        [
            (where, SCALARS),
            (first_in, whole(first_in)),
            (
                grad_proj,
                pl.BlockSpec((count, width), lambda step: (0, jnp.minimum(step, 2))),
            ),
            (mixed, whole(mixed)),
            (grad_attn, whole(grad_attn)),
        ],
        terms_out(chips, rows, width, True),
        flops=19 * 10**9,
    )


def plane_terms(where, keep, got):
    _, chips, rows, width = keep.shape
    cut = chips // 2
    flips = (1, 3, 2, 0)

    def place(step, where_ref):
        flip = 0
        for at in range(4):
            flip = jnp.where(step == at, flips[at], flip)
        return where_ref[0] ^ flip, 0, 0, 0

    def kernel(where_ref, keep_ref, got_ref, x_out, y_out, stay_out):
        targets = {
            1: ((x_out, 0), (stay_out, 3)),
            3: ((x_out, 1), (y_out, 1)),
            2: ((stay_out, 1), (y_out, 0)),
            0: ((stay_out, 0), (stay_out, 2)),
        }
        for at, flip in enumerate(flips):

            @pl.when(pl.program_id(0) == at)
            def _(flip=flip):
                for half, (out, slot) in enumerate(targets[flip]):
                    span = slice(half * cut, half * cut + cut)
                    out[slot] = keep_ref[0, span] + got_ref[0, span]

    block = (1, chips, rows, width)
    shapes = [(2, cut, rows, width), (2, cut, rows, width), (4, cut, rows, width)]
    return pl.pallas_call(
        kernel,
        out_shape=[jax.ShapeDtypeStruct(shape, BF16) for shape in shapes],
        grid_spec=pltpu.PrefetchScalarGridSpec(
            num_scalar_prefetch=1,
            grid=(4,),
            in_specs=[pl.BlockSpec(block, place), pl.BlockSpec(block, place)],
            out_specs=[
                pl.BlockSpec(shape, lambda step, where_ref: (0, 0, 0, 0)) for shape in shapes
            ],
        ),
        cost_estimate=pl.CostEstimate(
            flops=7 * 10**9, bytes_accessed=6 * keep.size, transcendentals=0
        ),
        compiler_params=pltpu.CompilerParams(vmem_limit_bytes=VMEM_LIMIT),
        name="plane_terms",
    )(where, keep, got)


X_SWAP = [(0, 1), (1, 0), (2, 3), (3, 2)]
Y_SWAP = [(0, 2), (2, 0), (1, 3), (3, 1)]


def swap_x(value):
    return lax.ppermute(value, "item", X_SWAP)


def swap_y(value):
    return lax.ppermute(value, "item", Y_SWAP)


def swap_core(value):
    count = lax.axis_size("frame")
    return lax.ppermute(value, "frame", [(at, at ^ 1) for at in range(count)])


def is_square():
    return lax.axis_size("item") == 4 and lax.axis_size("frame") % 2 == 0


def after(value, *others):
    return lax.optimization_barrier((value, *others))[0]


def after2(values, *others):
    return lax.optimization_barrier((*values, *others))[: len(values)]


def pick(stack, index):
    return lax.dynamic_index_in_dim(stack, index, 0, keepdims=False)


def by_column_quarter(stack):
    return jnp.concatenate([stack[part] for part in range(4)], axis=1)


def gather_frame(parts):
    if not is_square():
        return lax.all_gather(parts, "frame", axis=1)
    return lax.all_gather(pick(parts, lax.axis_index("item")), "frame", axis=0)


class Spread:
    def __init__(self, gathered, slot_first):
        self.gathered, self.slot_first = gathered, slot_first
        self.square = is_square()

    def near(self, *wait_for):
        if not self.square:
            return ()
        self.gathered = after(self.gathered, *wait_for)
        half = self.gathered.shape[0] // 2
        core = lax.axis_index("frame") % 2
        own = lax.dynamic_slice_in_dim(self.gathered, core * half, half, 0)
        self.cut = half // 2
        self.from_x, self.from_y = swap_x(own), swap_y(own)
        return self.from_x, self.from_y

    def far(self, *wait_for):
        if not self.square:
            return ()
        from_x, from_y = after2((self.from_x, self.from_y), *wait_for)
        self.far_low, self.far_high = swap_y(from_x[: self.cut]), swap_x(from_y[self.cut :])
        self.core_x, self.core_y = swap_core(from_x), swap_core(from_y)
        return self.far_low, self.far_high

    def pieces(self):
        gathered, slot_first = self.gathered, self.slot_first
        if not self.square:
            _, count, rows, width = gathered.shape
            if slot_first:
                return Pieces(
                    [gathered[part].reshape(count * rows, width) for part in range(4)],
                    [lambda item, core, part=part: (part, 0, count * rows) for part in range(4)],
                    (2, count * rows, 2 * width),
                    True,
                )
            return Pieces(
                [gathered[part] for part in range(4)],
                [lambda item, core, part=part: (part, 0, count) for part in range(4)],
                (count, 4, rows, width),
                False,
            )
        count, rows, width = gathered.shape
        half, cut = count // 2, self.cut
        far = [self.far_low, self.far_high]
        arrays = [gathered, self.from_x, self.from_y, *far, self.core_x, self.core_y]
        arrays += [swap_core(value) for value in far]
        unit = rows if slot_first else 1
        if slot_first:
            arrays = [array.reshape(-1, width) for array in arrays]
            shape = (2, count * rows, 2 * width)
        else:
            shape = (count, 4, rows, width)
        places = [lambda item, core: (item, 0, count * unit)]
        for flip in (0, 1):
            for slot, start, length in ((1, 0, half), (2, 0, half), (3, 0, cut), (3, cut, half - cut)):
                places.append(
                    lambda item, core, flip=flip, slot=slot, start=start, length=length: (
                        item ^ slot,
                        ((core ^ flip) * half + start) * unit,
                        length * unit,
                    )
                )
        return Pieces(arrays, places, shape, slot_first)


class Collect:
    def __init__(self, where, keep, give):
        self.where, self.keep, self.give = where, keep, give
        self.item = lax.axis_index("item")

    def pair(self, *wait_for):
        self.give = after(self.give, *wait_for)
        self.got = swap_core(self.give)

    def near(self, *wait_for):
        got = after(self.got, *wait_for)
        x_out, y_out, self.stay = plane_terms(self.where, self.keep, got)
        self.x_in, self.y_in = swap_x(x_out), swap_y(y_out)
        return (self.stay,)

    def far(self, *wait_for):
        x_in, y_in = after2((self.x_in, self.y_in), *wait_for)
        low_on, high_on = self.stay[1] + x_in[1], self.stay[3] + y_in[1]
        self.low, self.high = self.stay[0] + x_in[0], self.stay[2] + y_in[0]
        self.y_far, self.x_far = swap_y(low_on), swap_x(high_on)
        return low_on, high_on

    def line(self, *wait_for):
        y_far, x_far = after2((self.y_far, self.x_far), *wait_for)
        plane = jnp.concatenate([self.low + y_far, self.high + x_far], axis=0)
        count = lax.axis_size("frame")
        groups = [list(range(side, count, 2)) for side in range(2)]
        self.own = lax.psum_scatter(
            plane, "frame", scatter_dimension=0, tiled=False, axis_index_groups=groups
        )
        return (plane,)

    def finish(self, *wait_for):
        own, item = after(self.own, *wait_for), self.item
        far = lax.ppermute(own, "item", [(at, at ^ 3) for at in range(4)])
        stack = jnp.stack([own, swap_x(own), swap_y(own), far])
        return jnp.stack([pick(stack, item ^ part) for part in range(4)])


def sum_plain(partial):
    share = lax.psum_scatter(partial.astype(BF16), "frame", scatter_dimension=1, tiled=False)
    return lax.psum(share, "item")


def share_small(value):
    count = lax.axis_size("frame")
    return lax.all_to_all(
        jnp.broadcast_to(value[None], (count, *value.shape)), "frame", 0, 0, tiled=False
    )


def sum_items(value):
    if not is_square():
        return lax.psum(value.astype(BF16), "item").astype(F32)
    value = value + swap_x(value.astype(BF16)).astype(F32)
    return value + swap_y(value.astype(BF16)).astype(F32)


def round_up(number, unit):
    return -(-number // unit) * unit


def body(
    tokens,
    cotangent,
    patch_counts,
    assignment,
    timesteps,
    class_ids,
    w_qkv,
    w_out,
    w_fc1,
    b_fc1,
    w_fc2,
    w_ada,
    b_ada,
    class_table,
):
    frame_count = lax.axis_size("frame")
    group_idx = lax.axis_index("item")
    frame_pos = lax.axis_index("frame")
    _, own_frames, capacity, width = tokens.shape
    frames = own_frames * frame_count
    positions = capacity // frame_count
    rows = frames * positions
    clips = patch_counts.shape[0]
    attn_scale = 1.0 / math.sqrt(width // HEADS)
    where = jnp.stack([group_idx, frame_pos % 2, frame_pos]).astype(jnp.int32)

    def to_positions(value, *extra):
        chunks = value[0].reshape(own_frames, frame_count, positions, width).transpose(1, 0, 2, 3)
        chunks = chunks.reshape(frame_count, own_frames * positions, width)
        for more in extra:
            more = jnp.broadcast_to(more[None], (frame_count, *more.shape))
            chunks = jnp.concatenate([chunks, more], axis=1)
        return lax.all_to_all(chunks, "frame", 0, 0, tiled=True)

    def to_frames(value, *wait_for):
        chunks = value.reshape(frame_count, own_frames, positions, width)
        moved = after(lax.all_to_all(chunks, "frame", 0, 0, tiled=True), *wait_for)
        return moved.transpose(1, 0, 2, 3).reshape(1, own_frames, capacity, width)

    layout = row_items(patch_counts, assignment, group_idx, capacity)
    my_rows = lax.dynamic_slice_in_dim(layout, frame_pos * positions, positions, 0)
    class_hot = (class_ids[:, None] == jnp.arange(CLASSES, dtype=jnp.int32)[None, :]).astype(F32)
    condition = time_features(timesteps) + jnp.dot(class_hot, class_table, precision=HIGHEST)
    activated = jax.nn.silu(condition)
    ada_part = jnp.dot(activated, w_ada.astype(F32), precision=HIGHEST) + b_ada.astype(F32)

    ada_cols, bias_cols = b_ada.shape[0], b_fc1.shape[0]
    small_rows, small_cols = round_up(clips + 1, 16), round_up(max(ada_cols, bias_cols), LANES)
    small = jnp.concatenate(
        [
            jnp.pad(ada_part.astype(BF16), ((0, 0), (0, width - ada_cols))),
            jnp.pad(b_fc1[None], ((0, small_rows - clips - 1), (0, width - bias_cols))),
        ],
        axis=0,
    )
    x_arrived = to_positions(tokens, small)
    small_all = x_arrived[:, own_frames * positions :]
    x_arrived = x_arrived.reshape(-1, width)
    clip_slots = round_up(clips, 16)
    mod = small_all[:, :clips, :ada_cols].transpose(1, 0, 2).reshape(clips, -1)
    mod = jnp.pad(mod, ((0, clip_slots - clips), (0, 0)))
    bias = small_all[:, clips, :bias_cols].reshape(1, -1)
    hot = jnp.pad(my_rows.astype(BF16), ((0, 0), (0, clip_slots - clips)))
    hot = jnp.repeat(hot, frames, axis=0)

    shard_rows = w_out.shape[0]
    got_attn = gather_frame(jnp.stack([*jnp.split(w_qkv, 3, axis=1), w_out]))
    spread_attn = Spread(got_attn, True)
    near_attn = spread_attn.near()
    got_fc1 = gather_frame(
        jnp.stack(jnp.split(w_fc1, 4, axis=1))
    )
    far_attn = spread_attn.far()
    fc2_rows = w_fc2.shape[0] // 4
    got_fc2 = gather_frame(after(w_fc2.reshape(4, fc2_rows, width), x_arrived, *far_attn))

    square = is_square()
    chips = frame_count // 2
    spread_fc1 = Spread(got_fc1, True)
    spread_fc2 = Spread(got_fc2, False)
    near_fc1 = spread_fc1.near(*far_attn)
    x_rows, first_in, projected, full_attn = qkv_call(
        where, x_arrived, hot, mod, spread_attn.pieces(), positions, frames, own_frames
    )
    cot_arrived = to_positions(after(cotangent, projected)).reshape(rows, width)
    mixed = attend(after(projected, *near_fc1), positions, frames, attn_scale)
    far_fc1 = spread_fc1.far()
    near_fc2 = spread_fc2.near(*far_fc1)
    attn_out, middle, second_in = out_call(
        after(mixed, *far_fc1), x_rows, hot, mod, full_attn
    )
    far_fc2 = spread_fc2.far()
    post_act, slope, full_fc1 = fc1_call(
        where, second_in, bias, spread_fc1.pieces()
    )
    grad_rows, grad_mlp = cot_call(after(cot_arrived, post_act), hot, mod, positions, frames, own_frames)

    if square:
        sum_fc2 = Collect(where, *fc2_terms(where, post_act, after(grad_mlp, *near_fc2), chips))
        sum_fc2.pair()
        seen = (sum_fc2.give,)
    else:
        part_fc2 = lax.dot_general(post_act, grad_mlp, ROW_DIMS, preferred_element_type=F32)
        part_fc2 = part_fc2.reshape(frame_count, 4, fc2_rows, width).transpose(1, 0, 2, 3)
        seen = ()
    block_rows, grad_pre, part_bias, sum_gate_mlp = fc2_call(
        where,
        post_act,
        slope,
        after(grad_mlp, *seen),
        grad_rows,
        middle,
        hot,
        mod,
        spread_fc2.pieces(),
        positions,
        frames,
    )
    if square:
        seen = sum_fc2.near(grad_pre)
        sum_fc1 = Collect(where, *fc1_terms(where, second_in, after(grad_pre, *seen), chips))
        sum_fc1.pair()
        seen = (sum_fc1.give,)
    else:
        part_fc1 = [dot(second_in, part, ROW_DIMS) for part in jnp.split(grad_pre, 4, axis=1)]
        part_fc1 = jnp.stack(part_fc1).reshape(4, frame_count, shard_rows, -1)
    grad_middle, grad_attn, grad_mixed, sums_mlp = fc1_back_call(
        after(grad_pre, *seen), full_fc1, middle, attn_out, grad_rows, hot, mod, full_attn
    )
    seen = ()
    if square:
        seen = (*sum_fc2.far(grad_mixed), *sum_fc1.near(grad_mixed))
    grad_proj = attend_back(
        projected, after(grad_mixed, *seen), positions, frames, attn_scale
    )
    block_out = to_frames(block_rows, grad_proj)
    if square:
        seen = (*sum_fc2.line(grad_proj), *sum_fc1.far(grad_proj), block_out)
        sum_attn = Collect(
            where, *attn_terms(where, first_in, after(grad_proj, *seen), mixed, grad_attn, chips)
        )
        seen = sum_fc1.line()
        sum_attn.pair(*seen)
        seen = (sum_attn.give, sum_fc2.own)
    else:
        part_attn = [dot(first_in, part, ROW_DIMS) for part in jnp.split(grad_proj, 3, axis=1)]
        part_attn = jnp.stack([*part_attn, dot(mixed, grad_attn, ROW_DIMS)])
        part_attn = part_attn.reshape(4, frame_count, shard_rows, width)
    token_rows, sums_attn = qkv_back_call(
        after(grad_proj, *seen), full_attn, x_rows, grad_middle, hot, mod, positions, frames
    )
    if square:
        sum_attn.near(token_rows, sum_fc1.own)
        sum_attn.far()
        seen = sum_attn.line()
        sum_fc2, sum_fc1, sum_attn = sum_fc2.finish(*seen), sum_fc1.finish(*seen), sum_attn.finish()
    else:
        seen = ()
        sum_fc2, sum_fc1, sum_attn = sum_plain(part_fc2), sum_plain(part_fc1), sum_plain(part_attn)
    grad_tokens = to_frames(token_rows, *seen)
    part_mod = jnp.concatenate([sums_attn, sums_mlp, sum_gate_mlp[None]], axis=0)[:, :clips]
    part_mod = part_mod.transpose(1, 0, 2).reshape(clips, frame_count, ada_cols)
    part_small = jnp.concatenate(
        [
            jnp.pad(part_mod, ((0, 0), (0, 0), (0, small_cols - ada_cols))),
            jnp.pad(
                part_bias.reshape(1, frame_count, bias_cols),
                ((0, small_rows - clips - 1), (0, 0), (0, small_cols - bias_cols)),
            ),
        ],
        axis=0,
    ).astype(BF16)
    small_terms = lax.all_to_all(after(part_small, *seen).transpose(1, 0, 2), "frame", 0, 0, tiled=False)
    small_sum = sum_items(jnp.sum(small_terms.astype(F32), axis=0))
    grad_modulation = small_sum[:clips, :ada_cols]
    sum_bias = small_sum[clips, :bias_cols]
    grad_w_ada = lax.dot_general(activated, grad_modulation, ROW_DIMS, precision=HIGHEST)
    grad_b_ada = jnp.sum(grad_modulation, axis=0)
    act_part = lax.dot_general(grad_modulation, w_ada.astype(F32), COL_DIMS, precision=HIGHEST)
    grad_activated = jnp.sum(share_small(act_part.astype(BF16)).astype(F32), axis=0)
    _, silu_back = jax.vjp(jax.nn.silu, condition)
    grad_condition = silu_back(grad_activated)[0]
    grad_table = lax.dot_general(class_hot, grad_condition, ROW_DIMS, precision=HIGHEST)
    return (
        block_out,
        grad_tokens,
        by_column_quarter(sum_attn)[:, : 3 * width].astype(F32),
        sum_attn[3].astype(F32),
        by_column_quarter(sum_fc1).astype(F32),
        sum_bias,
        sum_fc2.reshape(-1, width).astype(F32),
        grad_w_ada,
        grad_b_ada,
        grad_table,
    )


def solution(mesh):
    return jax.shard_map(
        body,
        mesh=mesh,
        in_specs=(
            P("item", "frame", None, None),
            P("item", "frame", None, None),
            P(),
            P(),
            P(),
            P(),
            P("frame", None),
            P("frame", None),
            P("frame", None),
            P("frame"),
            P("frame", None),
            P(None, "frame"),
            P("frame"),
            P(),
        ),
        out_specs=(
            P("item", "frame", None, None),
            P("item", "frame", None, None),
            P("frame", None),
            P("frame", None),
            P("frame", None),
            P("frame"),
            P("frame", None),
            P(None, "frame"),
            P("frame"),
            P(),
        ),
        check_vma=False,
    )
```

```python
import math

import jax
import jax.numpy as jnp
from jax import lax
from jax.experimental import pallas as pl
from jax.experimental.pallas import tpu as pltpu
from jax.sharding import PartitionSpec as P

D = 1152
HEADS = 16
CLASSES = 101


HIGHEST = lax.Precision.HIGHEST
ROW_DIMS = (((0,), (0,)), ((), ()))
COL_DIMS = (((1,), (1,)), ((), ()))


def layer_norm(values):
    center = values - jnp.mean(values, axis=-1, keepdims=True)
    return center * lax.rsqrt(jnp.mean(center * center, axis=-1, keepdims=True) + 1e-06)


def time_features(timesteps):
    half_width = D // 2
    frequency = jnp.exp(-math.log(10000.0) * jnp.arange(half_width, dtype=jnp.float32) / half_width)
    angles = timesteps.astype(jnp.float32)[:, None] * frequency[None, :]
    return jnp.concatenate([jnp.cos(angles), jnp.sin(angles)], axis=1)


def row_items(patch_counts, assignment, group_idx, total):
    numbers = jnp.arange(patch_counts.shape[0], dtype=jnp.int32)
    same_group = assignment[None, :] == assignment[:, None]
    earlier = numbers[None, :] < numbers[:, None]
    offsets = jnp.sum(jnp.where(same_group & earlier, patch_counts[None, :], 0), axis=1)
    row_ids = jnp.arange(total, dtype=jnp.int32)[:, None]
    inside = (
        (assignment[None, :] == group_idx)
        & (row_ids >= offsets[None, :])
        & (row_ids < offsets[None, :] + patch_counts[None, :])
    )
    return inside.astype(jnp.float32)


def gelu_tanh(pre_vals):
    return jax.nn.gelu(pre_vals, approximate=True)

LANES = 128


def head_windows(heads, head_dim):
    windows = []
    for head in range(heads):
        low, high = head * head_dim, (head + 1) * head_dim
        windows.append((low // LANES * LANES, -(-high // LANES) * LANES, low, high))
    return windows


def lane_mask(window):
    start, end, low, high = window
    lanes = start + lax.broadcasted_iota(jnp.int32, (1, end - start), 1)
    return ((lanes >= low) & (lanes < high)).astype(jnp.float32).astype(jnp.bfloat16)


def add_window(totals, window, value):
    start, end, _, _ = window
    for lane in range(start, end, LANES):
        piece = value[:, lane - start : lane - start + LANES]
        totals[lane] = piece if lane not in totals else totals[lane] + piece


def joined(totals):
    return jnp.concatenate([totals[lane] for lane in sorted(totals)], axis=1)


class Spots:
    def __init__(self, rows, frames):
        self.frames = frames
        spot = lax.broadcasted_iota(jnp.int32, (frames, rows), 1) // frames
        self.own = [spot == at for at in range(rows // frames)]
        self.masks = [own.astype(jnp.float32).astype(jnp.bfloat16) for own in self.own]

    def compact(self, full):
        found = full[: self.frames]
        for at, own in enumerate(self.own[1:], 1):
            found = jnp.where(own, full[at * self.frames : (at + 1) * self.frames], found)
        return found

    def expand(self, compact):
        return jnp.concatenate([compact * mask for mask in self.masks], axis=0)

    def probs(self, queries, keys, scale):
        scores = lax.dot_general(keys, queries, COL_DIMS, preferred_element_type=jnp.float32)
        scores = self.compact(scores) * scale
        weights = jnp.exp(scores - jnp.max(scores, axis=0, keepdims=True))
        return weights / jnp.sum(weights, axis=0, keepdims=True)


def attend_kernel(frames, scale, proj_ref, mixed_ref):
    rows, width = mixed_ref.shape
    spots = Spots(rows, frames)
    totals = {}
    for window in head_windows(HEADS, width // HEADS):
        query, key, value = [
            slice(part * width + window[0], part * width + window[1]) for part in range(3)
        ]
        mask = lane_mask(window)
        prob = spots.probs(proj_ref[:, query] * mask, proj_ref[:, key], scale)
        add_window(
            totals,
            window,
            lax.dot_general(
                spots.expand(prob.astype(jnp.bfloat16)),
                proj_ref[:, value] * mask,
                ROW_DIMS,
                preferred_element_type=jnp.float32,
            ),
        )
    mixed_ref[...] = joined(totals).astype(jnp.bfloat16)


def attend_back_kernel(frames, scale, proj_ref, grad_ref, out_ref):
    rows, width = grad_ref.shape
    spots = Spots(rows, frames)
    to_query, to_key, to_value = {}, {}, {}
    for window in head_windows(HEADS, width // HEADS):
        query, key, value = [
            slice(part * width + window[0], part * width + window[1]) for part in range(3)
        ]
        mask = lane_mask(window)
        queries = proj_ref[:, query] * mask
        keys = proj_ref[:, key]
        grads = grad_ref[:, window[0] : window[1]] * mask
        prob = spots.probs(queries, keys, scale)
        grad_prob = spots.compact(
            lax.dot_general(
                proj_ref[:, value], grads, COL_DIMS, preferred_element_type=jnp.float32
            )
        )
        weighted = prob * grad_prob
        grad_scores = weighted - prob * jnp.sum(weighted, axis=0, keepdims=True)
        grad_scores = spots.expand(grad_scores.astype(jnp.bfloat16))
        prob_low = spots.expand(prob.astype(jnp.bfloat16))
        add_window(
            to_value, window, jnp.dot(prob_low, grads, preferred_element_type=jnp.float32)
        )
        add_window(
            to_key, window, jnp.dot(grad_scores, queries, preferred_element_type=jnp.float32)
        )
        add_window(
            to_query,
            window,
            lax.dot_general(
                grad_scores, keys * mask, ROW_DIMS, preferred_element_type=jnp.float32
            ),
        )
    out_ref[:, :width] = (joined(to_query) * scale).astype(jnp.bfloat16)
    out_ref[:, width : 2 * width] = (joined(to_key) * scale).astype(jnp.bfloat16)
    out_ref[:, 2 * width :] = joined(to_value).astype(jnp.bfloat16)


def tile_rows(positions, frames):
    for count in (8, 4, 2):
        if positions % count == 0:
            return count * frames
    return frames


def attend(projected, positions, frames, scale):
    rows, width = projected.shape[0], projected.shape[1] // 3
    tile = tile_rows(positions, frames)
    return pl.pallas_call(
        lambda *refs: attend_kernel(frames, scale, *refs),
        out_shape=jax.ShapeDtypeStruct((rows, width), jnp.bfloat16),
        grid=(rows // tile,),
        in_specs=[pl.BlockSpec((tile, 3 * width), lambda step: (step, 0))],
        out_specs=pl.BlockSpec((tile, width), lambda step: (step, 0)),
        cost_estimate=pl.CostEstimate(
            flops=13 * 10**9, bytes_accessed=8 * rows * width, transcendentals=0
        ),
        compiler_params=pltpu.CompilerParams(vmem_limit_bytes=VMEM_LIMIT),
        name="attend",
    )(projected)


def attend_back(projected, grad_mixed, positions, frames, scale):
    rows, width = projected.shape[0], projected.shape[1] // 3
    tile = tile_rows(positions, frames)
    return pl.pallas_call(
        lambda *refs: attend_back_kernel(frames, scale, *refs),
        out_shape=jax.ShapeDtypeStruct((rows, 3 * width), jnp.bfloat16),
        grid=(rows // tile,),
        in_specs=[
            pl.BlockSpec((tile, 3 * width), lambda step: (step, 0)),
            pl.BlockSpec((tile, width), lambda step: (step, 0)),
        ],
        out_specs=pl.BlockSpec((tile, 3 * width), lambda step: (step, 0)),
        cost_estimate=pl.CostEstimate(
            flops=27 * 10**9, bytes_accessed=14 * rows * width, transcendentals=0
        ),
        compiler_params=pltpu.CompilerParams(vmem_limit_bytes=VMEM_LIMIT),
        name="attend_back",
    )(projected, grad_mixed)


VMEM_LIMIT = 58 << 20
BF16, F32 = jnp.bfloat16, jnp.float32


def row_tile(rows):
    for tile in (224, 128, 112, 64, 32, 16):
        if rows % tile == 0:
            return tile
    return rows


def dot(left, right, dims=(((1,), (0,)), ((), ()))):
    return lax.dot_general(left, right, dims, preferred_element_type=F32)


def call(kernel, name, grid, ins, outs, scratch=(), flops=0, vmem=VMEM_LIMIT):
    moved = sum(array.size * array.dtype.itemsize for array, _ in ins)
    moved += sum(math.prod(shape) * jnp.dtype(dtype).itemsize for shape, dtype, _ in outs)
    return pl.pallas_call(
        kernel,
        out_shape=[jax.ShapeDtypeStruct(shape, dtype) for shape, dtype, _ in outs],
        grid=grid,
        in_specs=[spec for _, spec in ins],
        out_specs=[spec for _, _, spec in outs],
        scratch_shapes=list(scratch),
        cost_estimate=pl.CostEstimate(flops=flops, bytes_accessed=moved, transcendentals=0),
        compiler_params=pltpu.CompilerParams(vmem_limit_bytes=vmem),
        name=name,
    )(*[array for array, _ in ins])


HBM = pl.BlockSpec(memory_space=pl.ANY)
SCALARS = pl.BlockSpec(memory_space=pltpu.SMEM)


def whole(array):
    return pl.BlockSpec(array.shape, lambda step: (0,) * array.ndim)


def tiled(tile, width):
    return pl.BlockSpec((tile, width), lambda step: (step, 0))


class Pieces:
    def __init__(self, arrays, places, shape, by_columns, flipped):
        self.arrays, self.places, self.shape = arrays, places, shape
        self.by_columns, self.flipped = by_columns, flipped

    def quarter(self, where_ref, turn):
        return where_ref[0] ^ turn if self.flipped else turn

    def columns(self, slot):
        width = self.shape[1] // 4
        return pl.ds(pl.multiple_of(slot * width, width), width)

    def start(self, where_ref, refs, full, sems):
        for ref, place in zip(refs, self.places):
            slot, first, count = place(where_ref[0], where_ref[1])
            if self.by_columns:
                target = full.at[pl.ds(first, count), self.columns(slot)]
                pltpu.make_async_copy(ref, target, sems.at[slot]).start()
                continue
            for turn in range(count):
                target = full.at[first + turn, slot]
                sem = sems.at[(first + turn) // (self.shape[0] // 4)]
                pltpu.make_async_copy(ref.at[turn], target, sem).start()

    def part(self, full, at):
        if self.by_columns:
            return full.at[:, self.columns(at)]
        turns = self.shape[0] // 4
        return full.at[at * turns : (at + 1) * turns]

    def wait(self, at, full, sems):
        part = self.part(full, at)
        pltpu.make_async_copy(part, part, sems.at[at]).wait()

    def scratch(self):
        return [pltpu.VMEM(self.shape, BF16), pltpu.SemaphoreType.DMA((5,))]


def norm_parts(values):
    center = values - jnp.mean(values, axis=1, keepdims=True)
    inverse = lax.rsqrt(jnp.mean(center * center, axis=1, keepdims=True) + 1e-06)
    return center * inverse, inverse


def norm_back(normed, inverse, grad):
    mean_grad = jnp.mean(grad, axis=1, keepdims=True)
    mean_both = jnp.mean(grad * normed, axis=1, keepdims=True)
    return (grad - mean_grad - normed * mean_both) * inverse


def gather_order(first, count, frames, positions, own_frames, chunk):
    at = first + lax.broadcasted_iota(jnp.int32, (count, 1), 0)
    source = lax.broadcasted_iota(jnp.int32, (1, frames // own_frames * chunk), 1)
    frame, position = at % frames, at // frames
    wanted = frame // own_frames * chunk + frame % own_frames * positions + position
    return (source == wanted).astype(F32).astype(BF16)


def row_order(rows, first, count, inner, outer):
    at = first + lax.broadcasted_iota(jnp.int32, (count, 1), 0)
    source = lax.broadcasted_iota(jnp.int32, (1, rows), 1)
    return (source == (at % outer) * inner + at // outer).astype(F32).astype(BF16)


def clip_sums(hot, values):
    high = values.astype(BF16)
    low = (values - high.astype(F32)).astype(BF16)
    return dot(hot, high, ROW_DIMS) + dot(hot, low, ROW_DIMS)


def by_tile(my_rows, mod, frames):
    count = row_tile(my_rows.shape[0] * frames) // frames
    tiles = my_rows.astype(BF16).reshape(-1, count, my_rows.shape[1])
    tiles = jnp.pad(tiles, ((0, 0), (0, -count % 8), (0, 0)))
    return lax.dot_general(tiles, mod, (((2,), (0,)), ((), ())), preferred_element_type=F32)


def tile_mod(mod):
    return pl.BlockSpec((1, *mod.shape[1:]), lambda step: (step, 0, 0))


def spread_rows(mod_ref, part, count, frames):
    width = mod_ref.shape[2] // 6
    cols = slice(part * width, (part + 1) * width)
    rows = [
        jnp.broadcast_to(mod_ref[0, at : at + 1, cols], (frames, width)) for at in range(count)
    ]
    return jnp.concatenate(rows, axis=0)


def first_step(step, action):
    @pl.when(step == 0)
    def _():
        action()


def add_into(ref, index, value):
    @pl.when(pl.program_id(0) == 0)
    def _():
        ref[index] = jnp.zeros_like(ref[index])

    ref[index] += value


def qkv_call(where, arrived, mod, pieces, positions, frames, own_frames):
    rows, width = positions * frames, arrived.shape[1]
    chunk = arrived.shape[0] * own_frames // frames
    tile = row_tile(rows)
    steps = rows // tile
    count = len(pieces.arrays)

    def kernel(where_ref, x_ref, mod_ref, *rest):
        piece_refs, rest = rest[:count], rest[count:]
        x_out, first_out, proj_out, full_out, full, sems = rest
        step = pl.program_id(0)

        @pl.when(step == 0)
        def _():
            pieces.start(where_ref, piece_refs, full, sems)

        order = gather_order(step * tile, tile, frames, positions, own_frames, chunk)
        inputs = dot(order, x_ref[...])
        x_out[...] = inputs.astype(BF16)
        normed, _ = norm_parts(inputs)
        shift = spread_rows(mod_ref, 0, tile // frames, frames)
        scale = spread_rows(mod_ref, 1, tile // frames, frames)
        first = (normed * (1.0 + scale) + shift).astype(BF16)
        first_out[...] = first
        back = pltpu.make_async_copy(full, full_out, sems.at[4])

        @pl.when(step == 0)
        def _():
            for turn in range(4):
                slot = pieces.quarter(where_ref, turn)
                pieces.wait(slot, full, sems)

                @pl.when(slot < 3)
                def _():
                    weight = pieces.part(full, slot)[...]
                    proj_out[:, pieces.columns(slot)] = dot(first, weight).astype(BF16)

            back.start()

        @pl.when(step > 0)
        def _():
            proj_out[...] = dot(first, full[:, : 3 * width]).astype(BF16)

        @pl.when(step == steps - 1)
        def _():
            back.wait()

    return call(
        kernel,
        "project",
        (steps,),
        [
            (where, SCALARS),
            (arrived, whole(arrived)),
            (mod, tile_mod(mod)),
            *[(array, HBM) for array in pieces.arrays],
        ],
        [
            ((rows, width), BF16, tiled(tile, width)),
            ((rows, width), BF16, tiled(tile, width)),
            ((rows, 3 * width), BF16, tiled(tile, 3 * width)),
            (pieces.shape, BF16, HBM),
        ],
        pieces.scratch(),
        flops=20 * 10**9,
    )


def out_call(mixed, x_rows, mod, full_attn, frames):
    rows, width = mixed.shape
    tile = row_tile(rows)

    def kernel(mixed_ref, x_ref, mod_ref, w_ref, attn_out, middle_out, second_out):
        attn = dot(mixed_ref[...], w_ref[...])
        shift, scale, gate = [
            spread_rows(mod_ref, part, tile // frames, frames)
            for part in (3, 4, 2)
        ]
        middle = x_ref[...].astype(F32) + gate * attn
        normed, _ = norm_parts(middle)
        attn_out[...] = attn.astype(BF16)
        middle_out[...] = middle
        second_out[...] = (normed * (1.0 + scale) + shift).astype(BF16)

    return call(
        kernel,
        "attn_out",
        (rows // tile,),
        [
            (mixed, tiled(tile, width)),
            (x_rows, tiled(tile, width)),
            (mod, tile_mod(mod)),
            (full_attn, pl.BlockSpec((width, width), lambda step: (0, 3))),
        ],
        [
            ((rows, width), BF16, tiled(tile, width)),
            ((rows, width), F32, tiled(tile, width)),
            ((rows, width), BF16, tiled(tile, width)),
        ],
        flops=9 * 10**9,
    )


GELU_A = math.sqrt(2.0 / math.pi)
GELU_B = GELU_A * 0.044715


def fc1_call(where, second_in, bias, pieces):
    rows, width = second_in.shape
    tile = row_tile(rows)
    steps = rows // tile
    count = len(pieces.arrays)
    part = pieces.shape[1] // 4

    def kernel(where_ref, x_ref, bias_ref, *rest):
        piece_refs, rest = rest[:count], rest[count:]
        post_out, slope_out, full_out, full, sems = rest
        step = pl.program_id(0)
        back = pltpu.make_async_copy(full, full_out, sems.at[4])

        def run(cols):
            pre = dot(x_ref[...], full[:, cols]) + bias_ref[:, cols].astype(F32)
            square = pre * pre
            curve = jnp.tanh(pre * (GELU_A + GELU_B * square))
            half = 0.5 + 0.5 * curve
            post_out[:, cols] = (pre * half).astype(BF16)
            rise = (0.5 * pre) * (1.0 - curve * curve)
            slope_out[:, cols] = (half + rise * (GELU_A + 3.0 * GELU_B * square)).astype(BF16)

        @pl.when(step == 0)
        def _():
            pieces.start(where_ref, piece_refs, full, sems)
            for turn in range(4):
                slot = pieces.quarter(where_ref, turn)
                pieces.wait(slot, full, sems)
                run(pieces.columns(slot))
            back.start()

        @pl.when(step > 0)
        def _():
            for half in range(2):
                run(slice(half * 2 * part, (half + 1) * 2 * part))

        @pl.when(step == steps - 1)
        def _():
            back.wait()

    return call(
        kernel,
        "fc1",
        (steps,),
        [
            (where, SCALARS),
            (second_in, tiled(tile, width)),
            (bias, whole(bias)),
            *[(array, HBM) for array in pieces.arrays],
        ],
        [
            ((rows, 4 * part), BF16, tiled(tile, 4 * part)),
            ((rows, 4 * part), BF16, tiled(tile, 4 * part)),
            (pieces.shape, BF16, HBM),
        ],
        pieces.scratch(),
        flops=25 * 10**9,
    )


def cot_call(arrived, hot, mod, positions, frames, own_frames):
    rows, width = arrived.shape
    tile = row_tile(rows)

    def kernel(cot_ref, hot_ref, mod_ref, rows_out, mlp_out):
        first = pl.program_id(0) * tile
        order = gather_order(first, tile, frames, positions, own_frames, own_frames * positions)
        hot = hot_ref[...]
        valid = jnp.sum(hot.astype(F32), axis=1, keepdims=True)
        grad = dot(order, cot_ref[...]) * valid
        rows_out[...] = grad.astype(BF16)
        mlp_out[...] = (grad * spread_rows(mod_ref, 5, tile // frames, frames)).astype(BF16)

    return call(
        kernel,
        "cotangent",
        (rows // tile,),
        [
            (arrived, whole(arrived)),
            (hot, tiled(tile, hot.shape[1])),
            (mod, tile_mod(mod)),
        ],
        [
            ((rows, width), BF16, tiled(tile, width)),
            ((rows, width), BF16, tiled(tile, width)),
        ],
        flops=6 * 10**9,
    )


def fc2_call(where, post_act, slope, grad_mlp, grad_rows, middle, hot, mod, pieces, positions, frames):
    rows, hidden = post_act.shape
    width = grad_mlp.shape[1]
    tile = row_tile(rows)
    steps = rows // tile
    count = len(pieces.arrays)
    clips = hot.shape[1]

    def kernel(where_ref, post_ref, slope_ref, gmlp_ref, grows_ref, mid_ref, hot_ref, mod_ref, *rest):
        piece_refs, rest = rest[:count], rest[count:]
        block_out, pre_out, bias_out, gate_out, full, sems, held, sums = rest
        step = pl.program_id(0)

        def run(first, last):
            part = hidden // 4
            cols = slice(first * part, last * part)
            turns = pieces.shape[0] // 4
            weight = full[first * turns : last * turns].reshape((last - first) * part, width)
            term = dot(post_ref[:, cols], weight)
            sums[...] = term if not first else sums[...] + term
            grad_pre = dot(gmlp_ref[...], weight, COL_DIMS) * slope_ref[:, cols].astype(F32)
            grad_pre = grad_pre.astype(BF16)
            pre_out[:, cols] = grad_pre
            total = jnp.sum(grad_pre.astype(F32), axis=0, keepdims=True)
            add_into(bias_out, (slice(None), cols), total)

        @pl.when(step == 0)
        def _():
            pieces.start(where_ref, piece_refs, full, sems)
            for at in range(4):
                pieces.wait(at, full, sems)
                run(at, at + 1)

        @pl.when(step > 0)
        def _():
            run(0, 2)
            run(2, 4)

        total = sums[...]
        hot = hot_ref[...]
        valid = jnp.sum(hot.astype(F32), axis=1, keepdims=True)
        gate = spread_rows(mod_ref, 5, tile // frames, frames)
        result = valid * (mid_ref[...] + gate * total)
        held[pl.ds(pl.multiple_of(step * tile, 16), tile), :] = result.astype(BF16)
        add_into(gate_out, slice(None), clip_sums(hot, grows_ref[...].astype(F32) * total))

        @pl.when(step == steps - 1)
        def _():
            for at in range(steps):
                order = row_order(rows, at * tile, tile, frames, positions)
                block_out[at * tile : (at + 1) * tile, :] = dot(order, held[...]).astype(BF16)

    return call(
        kernel,
        "fc2",
        (steps,),
        [
            (where, SCALARS),
            (post_act, tiled(tile, hidden)),
            (slope, tiled(tile, hidden)),
            (grad_mlp, tiled(tile, width)),
            (grad_rows, tiled(tile, width)),
            (middle, tiled(tile, width)),
            (hot, tiled(tile, clips)),
            (mod, tile_mod(mod)),
            *[(array, HBM) for array in pieces.arrays],
        ],
        [
            ((rows, width), BF16, pl.BlockSpec((rows, width), lambda step: (0, 0))),
            ((rows, hidden), BF16, tiled(tile, hidden)),
            ((1, hidden), F32, pl.BlockSpec((1, hidden), lambda step: (0, 0))),
            ((clips, width), F32, pl.BlockSpec((clips, width), lambda step: (0, 0))),
        ],
        [*pieces.scratch(), pltpu.VMEM((rows, width), BF16), pltpu.VMEM((tile, width), F32)],
        flops=44 * 10**9,
    )


def load_and_dot(step, left_ref, w_ref, held, sems, total, parts):
    width = left_ref.shape[1] // parts
    runs = [slice(at * width, (at + 1) * width) for at in range(parts)]
    loads = [
        pltpu.make_async_copy(w_ref.at[:, run], held.at[:, run], sems.at[at])
        for at, run in enumerate(runs)
    ]

    @pl.when(step == 0)
    def _():
        for load in loads:
            load.start()
        for at, load in enumerate(loads):
            load.wait()
            term = dot(left_ref[:, runs[at]], held[:, runs[at]], COL_DIMS)
            total[...] = term if not at else total[...] + term

    @pl.when(step > 0)
    def _():
        total[...] = dot(left_ref[...], held[...], COL_DIMS)

    return total[...]


def fc1_back_call(grad_pre, full_fc1, middle, attn_out, grad_rows, hot, mod, full_attn, frames):
    rows, hidden = grad_pre.shape
    width = middle.shape[1]
    tile = row_tile(rows)
    clips = hot.shape[1]

    def kernel(pre_ref, w_ref, mid_ref, attn_ref, grows_ref, hot_ref, mod_ref, wo_ref, *outs):
        gmid_out, gattn_out, gmix_out, sums_out, held, sems, total = outs
        step = pl.program_id(0)
        grad = load_and_dot(step, pre_ref, w_ref, held, sems, total, 4)
        hot = hot_ref[...]
        scale = spread_rows(mod_ref, 4, tile // frames, frames)
        gate = spread_rows(mod_ref, 2, tile // frames, frames)
        normed, inverse = norm_parts(mid_ref[...])
        grad_middle = grows_ref[...].astype(F32) + norm_back(normed, inverse, grad * (1.0 + scale))
        gmid_out[...] = grad_middle
        grad_attn = (grad_middle * gate).astype(BF16)
        gattn_out[...] = grad_attn
        gmix_out[...] = dot(grad_attn, wo_ref[...], COL_DIMS).astype(BF16)
        add_into(sums_out, 0, clip_sums(hot, grad_middle * attn_ref[...].astype(F32)))
        add_into(sums_out, 1, clip_sums(hot, grad))
        add_into(sums_out, 2, clip_sums(hot, grad * normed))

    return call(
        kernel,
        "fc1_back",
        (rows // tile,),
        [
            (grad_pre, tiled(tile, hidden)),
            (full_fc1, HBM),
            (middle, tiled(tile, width)),
            (attn_out, tiled(tile, width)),
            (grad_rows, tiled(tile, width)),
            (hot, tiled(tile, clips)),
            (mod, tile_mod(mod)),
            (full_attn, pl.BlockSpec((width, width), lambda step: (0, 3))),
        ],
        [
            ((rows, width), F32, tiled(tile, width)),
            ((rows, width), BF16, tiled(tile, width)),
            ((rows, width), BF16, tiled(tile, width)),
            ((3, clips, width), F32, pl.BlockSpec((3, clips, width), lambda step: (0, 0, 0))),
        ],
        [
            pltpu.VMEM(full_fc1.shape, BF16),
            pltpu.SemaphoreType.DMA((4,)),
            pltpu.VMEM((tile, width), F32),
        ],
        flops=32 * 10**9,
    )


def qkv_back_call(grad_proj, full_attn, x_rows, grad_middle, hot, mod, positions, frames):
    rows, width = x_rows.shape
    tile = row_tile(rows)
    steps = rows // tile
    clips = hot.shape[1]

    def kernel(proj_ref, w_ref, x_ref, gmid_ref, hot_ref, mod_ref, tok_out, sums_out, held, w_held, sems, total):
        step = pl.program_id(0)
        grad = load_and_dot(step, proj_ref, w_ref, w_held, sems, total, 3)
        hot = hot_ref[...]
        scale = spread_rows(mod_ref, 1, tile // frames, frames)
        normed, inverse = norm_parts(x_ref[...].astype(F32))
        result = gmid_ref[...] + norm_back(normed, inverse, grad * (1.0 + scale))
        held[pl.ds(pl.multiple_of(step * tile, 16), tile), :] = result.astype(BF16)
        add_into(sums_out, 0, clip_sums(hot, grad))
        add_into(sums_out, 1, clip_sums(hot, grad * normed))

        @pl.when(step == steps - 1)
        def _():
            for at in range(steps):
                order = row_order(rows, at * tile, tile, frames, positions)
                tok_out[at * tile : (at + 1) * tile, :] = dot(order, held[...]).astype(BF16)

    return call(
        kernel,
        "project_back",
        (steps,),
        [
            (grad_proj, tiled(tile, 3 * width)),
            (full_attn, HBM),
            (x_rows, tiled(tile, width)),
            (grad_middle, tiled(tile, width)),
            (hot, tiled(tile, clips)),
            (mod, tile_mod(mod)),
        ],
        [
            ((rows, width), BF16, pl.BlockSpec((rows, width), lambda step: (0, 0))),
            ((2, clips, width), F32, pl.BlockSpec((2, clips, width), lambda step: (0, 0, 0))),
        ],
        [
            pltpu.VMEM((rows, width), BF16),
            pltpu.VMEM((width, 3 * width), BF16),
            pltpu.SemaphoreType.DMA((3,)),
            pltpu.VMEM((tile, width), F32),
        ],
        flops=23 * 10**9,
    )


def split_store(product, where_ref, keep_out, give_out, rows, slot_first, slot=0):
    units = product.shape[0] // rows
    for core in range(2):

        @pl.when(where_ref[1] == core)
        def _():
            for unit in range(units):
                piece = product[unit * rows : (unit + 1) * rows]
                side = unit % 2 if slot_first else unit // 4
                out = keep_out if side == core else give_out
                if slot_first:
                    out[slot, unit // 2] = piece
                else:
                    out[unit % 4, 0] = piece


def terms_out(chips, rows, width, slot_first, slots=1):
    if slot_first:
        spec = pl.BlockSpec((slots, chips, rows, width), lambda step: (step, 0, 0, 0))
    else:
        spec = pl.BlockSpec((4, 1, rows, width), lambda step: (0, step, 0, 0))
    return [((4, chips, rows, width), BF16, spec)] * 2


def fc2_terms(where, post_act, grad_mlp, chips):
    count, hidden = post_act.shape
    width = grad_mlp.shape[1]
    block, rows = hidden // chips, hidden // chips // 8

    def kernel(where_ref, left_ref, right_ref, keep_out, give_out):
        product = dot(left_ref[...], right_ref[...], ROW_DIMS).astype(BF16)
        split_store(product, where_ref, keep_out, give_out, rows, False)

    return call(
        kernel,
        "fc2_terms",
        (chips,),
        [
            (where, SCALARS),
            (post_act, pl.BlockSpec((count, block), lambda step: (0, step))),
            (grad_mlp, whole(grad_mlp)),
        ],
        terms_out(chips, rows, width, False),
        flops=18 * 10**9,
    )


def fc1_terms(where, second_in, grad_pre, chips):
    count, hidden = grad_pre.shape
    width = second_in.shape[1]
    rows, part = width // chips // 2, hidden // 4

    def kernel(where_ref, left_ref, right_ref, keep_out, give_out):
        product = dot(left_ref[...], right_ref[...], ROW_DIMS).astype(BF16)
        for slot in range(2):
            piece = product[:, slot * part : (slot + 1) * part]
            split_store(piece, where_ref, keep_out, give_out, rows, True, slot)

    return call(
        kernel,
        "fc1_terms",
        (2,),
        [
            (where, SCALARS),
            (second_in, whole(second_in)),
            (grad_pre, pl.BlockSpec((count, 2 * part), lambda step: (0, step))),
        ],
        terms_out(chips, rows, part, True, 2),
        flops=18 * 10**9,
    )


def attn_terms(where, first_in, grad_proj, mixed, grad_attn, chips):
    count, width = first_in.shape
    rows = width // chips // 2

    def kernel(where_ref, first_ref, proj_ref, mixed_ref, attn_ref, keep_out, give_out):
        step = pl.program_id(0)

        @pl.when(step < 3)
        def _():
            product = dot(first_ref[...], proj_ref[...], ROW_DIMS).astype(BF16)
            split_store(product, where_ref, keep_out, give_out, rows, True)

        @pl.when(step == 3)
        def _():
            product = dot(mixed_ref[...], attn_ref[...], ROW_DIMS).astype(BF16)
            split_store(product, where_ref, keep_out, give_out, rows, True)

    return call(
        kernel,
        "attn_terms",
        (4,),
        [
            (where, SCALARS),
            (first_in, whole(first_in)),
            (
                grad_proj,
                pl.BlockSpec((count, width), lambda step: (0, jnp.minimum(step, 2))),
            ),
            (mixed, whole(mixed)),
            (grad_attn, whole(grad_attn)),
        ],
        terms_out(chips, rows, width, True),
        flops=19 * 10**9,
    )


def plane_terms(where, keep, got):
    _, chips, rows, width = keep.shape
    cut = chips // 2
    flips = (1, 3, 2, 0)

    def place(step, where_ref):
        flip = 0
        for at in range(4):
            flip = jnp.where(step == at, flips[at], flip)
        return where_ref[0] ^ flip, 0, 0, 0

    def kernel(where_ref, keep_ref, got_ref, x_out, y_out, stay_out):
        targets = {
            1: ((x_out, 0), (stay_out, 3)),
            3: ((x_out, 1), (y_out, 1)),
            2: ((stay_out, 1), (y_out, 0)),
            0: ((stay_out, 0), (stay_out, 2)),
        }
        for at, flip in enumerate(flips):

            @pl.when(pl.program_id(0) == at)
            def _(flip=flip):
                for half, (out, slot) in enumerate(targets[flip]):
                    span = slice(half * cut, half * cut + cut)
                    out[slot] = keep_ref[0, span] + got_ref[0, span]

    block = (1, chips, rows, width)
    shapes = [(2, cut, rows, width), (2, cut, rows, width), (4, cut, rows, width)]
    return pl.pallas_call(
        kernel,
        out_shape=[jax.ShapeDtypeStruct(shape, BF16) for shape in shapes],
        grid_spec=pltpu.PrefetchScalarGridSpec(
            num_scalar_prefetch=1,
            grid=(4,),
            in_specs=[pl.BlockSpec(block, place), pl.BlockSpec(block, place)],
            out_specs=[
                pl.BlockSpec(shape, lambda step, where_ref: (0, 0, 0, 0)) for shape in shapes
            ],
        ),
        cost_estimate=pl.CostEstimate(
            flops=7 * 10**9, bytes_accessed=6 * keep.size, transcendentals=0
        ),
        compiler_params=pltpu.CompilerParams(vmem_limit_bytes=VMEM_LIMIT),
        name="plane_terms",
    )(where, keep, got)


X_SWAP = [(0, 1), (1, 0), (2, 3), (3, 2)]
Y_SWAP = [(0, 2), (2, 0), (1, 3), (3, 1)]


def swap_x(value):
    return lax.ppermute(value, "item", X_SWAP)


def swap_y(value):
    return lax.ppermute(value, "item", Y_SWAP)


def swap_core(value):
    count = lax.axis_size("frame")
    return lax.ppermute(value, "frame", [(at, at ^ 1) for at in range(count)])


def is_square():
    return lax.axis_size("item") == 4 and lax.axis_size("frame") % 2 == 0


def after(value, *others):
    return lax.optimization_barrier((value, *others))[0]


def after2(values, *others):
    return lax.optimization_barrier((*values, *others))[: len(values)]


def pick(stack, index):
    return lax.dynamic_index_in_dim(stack, index, 0, keepdims=False)


def by_column_quarter(stack):
    return jnp.concatenate([stack[part] for part in range(4)], axis=1)


def gather_frame(parts):
    if not is_square():
        return lax.all_gather(parts, "frame", axis=1)
    return lax.all_gather(pick(parts, lax.axis_index("item")), "frame", axis=0)


class Spread:
    def __init__(self, gathered, slot_first):
        self.gathered, self.slot_first = gathered, slot_first
        self.square = is_square()

    def near(self, *wait_for):
        if not self.square:
            return ()
        self.gathered = after(self.gathered, *wait_for)
        half = self.gathered.shape[0] // 2
        core = lax.axis_index("frame") % 2
        own = lax.dynamic_slice_in_dim(self.gathered, core * half, half, 0)
        self.cut = half // 2
        self.from_x, self.from_y = swap_x(own), swap_y(own)
        return self.from_x, self.from_y

    def far(self, *wait_for):
        if not self.square:
            return ()
        from_x, from_y = after2((self.from_x, self.from_y), *wait_for)
        self.far_low, self.far_high = swap_y(from_x[: self.cut]), swap_x(from_y[self.cut :])
        self.core_x, self.core_y = swap_core(from_x), swap_core(from_y)
        return self.far_low, self.far_high

    def pieces(self):
        gathered, slot_first = self.gathered, self.slot_first
        if not self.square:
            _, count, rows, width = gathered.shape
            if slot_first:
                return Pieces(
                    [gathered[part].reshape(count * rows, width) for part in range(4)],
                    [lambda item, core, part=part: (part, 0, count * rows) for part in range(4)],
                    (count * rows, 4 * width),
                    True,
                    False,
                )
            return Pieces(
                [gathered[part] for part in range(4)],
                [lambda item, core, part=part: (part, 0, count) for part in range(4)],
                (count, 4, rows, width),
                False,
                False,
            )
        count, rows, width = gathered.shape
        half, cut = count // 2, self.cut
        far = [self.far_low, self.far_high]
        arrays = [gathered, self.from_x, self.from_y, *far, self.core_x, self.core_y]
        arrays += [swap_core(value) for value in far]
        unit = rows if slot_first else 1
        if slot_first:
            arrays = [array.reshape(-1, width) for array in arrays]
            shape = (count * rows, 4 * width)
        else:
            shape = (count, 4, rows, width)
        places = [lambda item, core: (item, 0, count * unit)]
        for flip in (0, 1):
            for slot, start, length in ((1, 0, half), (2, 0, half), (3, 0, cut), (3, cut, half - cut)):
                places.append(
                    lambda item, core, flip=flip, slot=slot, start=start, length=length: (
                        item ^ slot,
                        ((core ^ flip) * half + start) * unit,
                        length * unit,
                    )
                )
        order = (0, 1, 5, 2, 6, 3, 4, 7, 8)
        arrays, places = [arrays[at] for at in order], [places[at] for at in order]
        return Pieces(arrays, places, shape, slot_first, True)


class Collect:
    def __init__(self, where, keep, give):
        self.where, self.keep, self.give = where, keep, give
        self.item = lax.axis_index("item")

    def pair(self, *wait_for):
        self.give = after(self.give, *wait_for)
        self.got = swap_core(self.give)

    def near(self, *wait_for):
        got = after(self.got, *wait_for)
        x_out, y_out, self.stay = plane_terms(self.where, self.keep, got)
        self.x_in, self.y_in = swap_x(x_out), swap_y(y_out)
        return (self.stay,)

    def far(self, *wait_for):
        x_in, y_in = after2((self.x_in, self.y_in), *wait_for)
        low_on, high_on = self.stay[1] + x_in[1], self.stay[3] + y_in[1]
        self.low, self.high = self.stay[0] + x_in[0], self.stay[2] + y_in[0]
        self.y_far, self.x_far = swap_y(low_on), swap_x(high_on)
        return low_on, high_on

    def line(self, *wait_for):
        y_far, x_far = after2((self.y_far, self.x_far), *wait_for)
        plane = jnp.concatenate([self.low + y_far, self.high + x_far], axis=0)
        count = lax.axis_size("frame")
        groups = [list(range(side, count, 2)) for side in range(2)]
        self.own = lax.psum_scatter(
            plane, "frame", scatter_dimension=0, tiled=False, axis_index_groups=groups
        )
        return (plane,)

    def finish(self, *wait_for):
        own, item = after(self.own, *wait_for), self.item
        far = lax.ppermute(own, "item", [(at, at ^ 3) for at in range(4)])
        stack = jnp.stack([own, swap_x(own), swap_y(own), far])
        return jnp.stack([pick(stack, item ^ part) for part in range(4)])


def sum_plain(partial):
    share = lax.psum_scatter(partial.astype(BF16), "frame", scatter_dimension=1, tiled=False)
    return lax.psum(share, "item")


def share_small(value):
    count = lax.axis_size("frame")
    return lax.all_to_all(
        jnp.broadcast_to(value[None], (count, *value.shape)), "frame", 0, 0, tiled=False
    )


def sum_items(value):
    if not is_square():
        return lax.psum(value.astype(BF16), "item").astype(F32)
    low = value.astype(BF16)
    far = lax.ppermute(low, "item", [(at, at ^ 3) for at in range(4)])
    return value + swap_x(low).astype(F32) + swap_y(low).astype(F32) + far.astype(F32)


def round_up(number, unit):
    return -(-number // unit) * unit


def body(
    tokens,
    cotangent,
    patch_counts,
    assignment,
    timesteps,
    class_ids,
    w_qkv,
    w_out,
    w_fc1,
    b_fc1,
    w_fc2,
    w_ada,
    b_ada,
    class_table,
):
    frame_count = lax.axis_size("frame")
    group_idx = lax.axis_index("item")
    frame_pos = lax.axis_index("frame")
    _, own_frames, capacity, width = tokens.shape
    frames = own_frames * frame_count
    positions = capacity // frame_count
    rows = frames * positions
    clips = patch_counts.shape[0]
    attn_scale = 1.0 / math.sqrt(width // HEADS)
    where = jnp.stack([group_idx, frame_pos % 2, frame_pos]).astype(jnp.int32)

    def to_positions(value, *extra):
        chunks = value[0].reshape(own_frames, frame_count, positions, width).transpose(1, 0, 2, 3)
        chunks = chunks.reshape(frame_count, own_frames * positions, width)
        for more in extra:
            more = jnp.broadcast_to(more[None], (frame_count, *more.shape))
            chunks = jnp.concatenate([chunks, more], axis=1)
        return lax.all_to_all(chunks, "frame", 0, 0, tiled=True)

    def to_frames(value, *wait_for):
        chunks = value.reshape(frame_count, own_frames, positions, width)
        moved = after(lax.all_to_all(chunks, "frame", 0, 0, tiled=True), *wait_for)
        return moved.transpose(1, 0, 2, 3).reshape(1, own_frames, capacity, width)

    layout = row_items(patch_counts, assignment, group_idx, capacity)
    my_rows = lax.dynamic_slice_in_dim(layout, frame_pos * positions, positions, 0)
    class_hot = (class_ids[:, None] == jnp.arange(CLASSES, dtype=jnp.int32)[None, :]).astype(F32)
    condition = time_features(timesteps) + jnp.dot(class_hot, class_table, precision=HIGHEST)
    activated = jax.nn.silu(condition)
    ada_part = jnp.dot(activated, w_ada.astype(F32), precision=HIGHEST) + b_ada.astype(F32)

    ada_cols, bias_cols = b_ada.shape[0], b_fc1.shape[0]
    small_rows, small_cols = round_up(clips + 1, 16), round_up(max(ada_cols, bias_cols), LANES)
    small = jnp.concatenate(
        [
            jnp.pad(ada_part.astype(BF16), ((0, 0), (0, width - ada_cols))),
            jnp.pad(b_fc1[None], ((0, small_rows - clips - 1), (0, width - bias_cols))),
        ],
        axis=0,
    )
    x_arrived = to_positions(tokens, small)
    small_all = x_arrived[:, own_frames * positions :]
    x_arrived = x_arrived.reshape(-1, width)
    clip_slots = round_up(clips, 16)
    mod = small_all[:, :clips, :ada_cols].transpose(1, 0, 2).reshape(clips, -1)
    mod = by_tile(my_rows, mod, frames)
    bias = small_all[:, clips, :bias_cols].reshape(1, -1)
    hot = jnp.pad(my_rows.astype(BF16), ((0, 0), (0, clip_slots - clips)))
    hot = jnp.repeat(hot, frames, axis=0)

    shard_rows = w_out.shape[0]
    got_attn = gather_frame(jnp.stack([*jnp.split(w_qkv, 3, axis=1), w_out]))
    spread_attn = Spread(got_attn, True)
    near_attn = spread_attn.near()
    got_fc1 = gather_frame(
        jnp.stack(jnp.split(w_fc1, 4, axis=1))
    )
    far_attn = spread_attn.far()
    fc2_rows = w_fc2.shape[0] // 4
    got_fc2 = gather_frame(after(w_fc2.reshape(4, fc2_rows, width), x_arrived, *far_attn))

    square = is_square()
    chips = frame_count // 2
    spread_fc1 = Spread(got_fc1, True)
    spread_fc2 = Spread(got_fc2, False)
    near_fc1 = spread_fc1.near(*far_attn)
    x_rows, first_in, projected, full_attn = qkv_call(
        where, x_arrived, mod, spread_attn.pieces(), positions, frames, own_frames
    )
    cot_arrived = to_positions(after(cotangent, projected)).reshape(rows, width)
    mixed = attend(after(projected, *near_fc1), positions, frames, attn_scale)
    far_fc1 = spread_fc1.far()
    near_fc2 = spread_fc2.near(*far_fc1)
    attn_out, middle, second_in = out_call(
        after(mixed, *far_fc1), x_rows, mod, full_attn, frames
    )
    far_fc2 = spread_fc2.far()
    post_act, slope, full_fc1 = fc1_call(
        where, second_in, bias, spread_fc1.pieces()
    )
    grad_rows, grad_mlp = cot_call(after(cot_arrived, post_act), hot, mod, positions, frames, own_frames)

    if square:
        sum_fc2 = Collect(where, *fc2_terms(where, post_act, after(grad_mlp, *near_fc2), chips))
        sum_fc2.pair()
        seen = (sum_fc2.give,)
    else:
        part_fc2 = lax.dot_general(post_act, grad_mlp, ROW_DIMS, preferred_element_type=F32)
        part_fc2 = part_fc2.reshape(frame_count, 4, fc2_rows, width).transpose(1, 0, 2, 3)
        seen = ()
    block_rows, grad_pre, part_bias, sum_gate_mlp = fc2_call(
        where,
        post_act,
        slope,
        after(grad_mlp, *seen),
        grad_rows,
        middle,
        hot,
        mod,
        spread_fc2.pieces(),
        positions,
        frames,
    )
    if square:
        seen = sum_fc2.near(grad_pre)
        sum_fc1 = Collect(where, *fc1_terms(where, second_in, after(grad_pre, *seen), chips))
        sum_fc1.pair()
        seen = (sum_fc1.give,)
    else:
        part_fc1 = [dot(second_in, part, ROW_DIMS) for part in jnp.split(grad_pre, 4, axis=1)]
        part_fc1 = jnp.stack(part_fc1).reshape(4, frame_count, shard_rows, -1)
    grad_middle, grad_attn, grad_mixed, sums_mlp = fc1_back_call(
        after(grad_pre, *seen), full_fc1, middle, attn_out, grad_rows, hot, mod, full_attn, frames
    )
    seen = ()
    if square:
        seen = (*sum_fc2.far(grad_mixed), *sum_fc1.near(grad_mixed))
    grad_proj = attend_back(
        projected, after(grad_mixed, *seen), positions, frames, attn_scale
    )
    block_out = to_frames(block_rows, grad_proj)
    seen = ()
    if square:
        seen = (*sum_fc2.line(grad_proj), *sum_fc1.far(grad_proj), block_out)
    token_rows, sums_attn = qkv_back_call(
        after(grad_proj, *seen), full_attn, x_rows, grad_middle, hot, mod, positions, frames
    )
    if square:
        seen = (token_rows, sum_fc2.own, *sum_fc1.line(token_rows))
        sum_attn = Collect(
            where, *attn_terms(where, first_in, after(grad_proj, *seen), mixed, grad_attn, chips)
        )
        sum_attn.pair()
        sum_attn.near()
        sum_attn.far()
        seen = sum_attn.line(sum_fc1.own)
        last = (sum_attn.own,)
        grad_tokens = to_frames(token_rows, *seen)
        sum_fc2, sum_fc1, sum_attn = sum_fc2.finish(*seen), sum_fc1.finish(*seen), sum_attn.finish()
    else:
        grad_tokens = to_frames(token_rows)
        part_attn = [dot(first_in, part, ROW_DIMS) for part in jnp.split(grad_proj, 3, axis=1)]
        part_attn = jnp.stack([*part_attn, dot(mixed, grad_attn, ROW_DIMS)])
        part_attn = part_attn.reshape(4, frame_count, shard_rows, width)
        seen, last = (), ()
        sum_fc2, sum_fc1, sum_attn = sum_plain(part_fc2), sum_plain(part_fc1), sum_plain(part_attn)
    part_mod = jnp.concatenate([sums_attn, sums_mlp, sum_gate_mlp[None]], axis=0)[:, :clips]
    part_mod = part_mod.transpose(1, 0, 2).reshape(clips, frame_count, ada_cols)
    part_small = jnp.concatenate(
        [
            jnp.pad(part_mod, ((0, 0), (0, 0), (0, small_cols - ada_cols))),
            jnp.pad(
                part_bias.reshape(1, frame_count, bias_cols),
                ((0, small_rows - clips - 1), (0, 0), (0, small_cols - bias_cols)),
            ),
        ],
        axis=0,
    ).astype(BF16)
    small_terms = lax.all_to_all(after(part_small, *seen).transpose(1, 0, 2), "frame", 0, 0, tiled=False)
    small_terms = after(small_terms, *last)
    small_sum = sum_items(jnp.sum(small_terms.astype(F32), axis=0))
    grad_modulation = small_sum[:clips, :ada_cols]
    sum_bias = small_sum[clips, :bias_cols]
    grad_b_ada = jnp.sum(grad_modulation, axis=0)
    high = grad_modulation.astype(BF16)
    low = (grad_modulation - high.astype(F32)).astype(BF16)
    act_part = (dot(high, w_ada, COL_DIMS) + dot(low, w_ada, COL_DIMS)).astype(BF16)
    grad_w_ada = lax.dot_general(
        activated, after(grad_modulation, act_part), ROW_DIMS, precision=HIGHEST
    )
    grad_activated = jnp.sum(share_small(act_part).astype(F32), axis=0)
    _, silu_back = jax.vjp(jax.nn.silu, condition)
    grad_condition = silu_back(grad_activated)[0]
    grad_table = lax.dot_general(class_hot, grad_condition, ROW_DIMS, precision=HIGHEST)
    return (
        block_out,
        grad_tokens,
        by_column_quarter(sum_attn)[:, : 3 * width].astype(F32),
        sum_attn[3].astype(F32),
        by_column_quarter(sum_fc1).astype(F32),
        sum_bias,
        sum_fc2.reshape(-1, width).astype(F32),
        grad_w_ada,
        grad_b_ada,
        grad_table,
    )


def solution(mesh):
    return jax.shard_map(
        body,
        mesh=mesh,
        in_specs=(
            P("item", "frame", None, None),
            P("item", "frame", None, None),
            P(),
            P(),
            P(),
            P(),
            P("frame", None),
            P("frame", None),
            P("frame", None),
            P("frame"),
            P("frame", None),
            P(None, "frame"),
            P("frame"),
            P(),
        ),
        out_specs=(
            P("item", "frame", None, None),
            P("item", "frame", None, None),
            P("frame", None),
            P("frame", None),
            P("frame", None),
            P("frame"),
            P("frame", None),
            P(None, "frame"),
            P("frame"),
            P(),
        ),
        check_vma=False,
    )
```

```python
import math

import jax
import jax.numpy as jnp
from jax import lax
from jax.experimental import pallas as pl
from jax.experimental.pallas import tpu as pltpu
from jax.sharding import PartitionSpec as P

D = 1152
HEADS = 16
CLASSES = 101


HIGHEST = lax.Precision.HIGHEST
ROW_DIMS = (((0,), (0,)), ((), ()))
COL_DIMS = (((1,), (1,)), ((), ()))


def layer_norm(values):
    center = values - jnp.mean(values, axis=-1, keepdims=True)
    return center * lax.rsqrt(jnp.mean(center * center, axis=-1, keepdims=True) + 1e-06)


def time_features(timesteps):
    half_width = D // 2
    frequency = jnp.exp(-math.log(10000.0) * jnp.arange(half_width, dtype=jnp.float32) / half_width)
    angles = timesteps.astype(jnp.float32)[:, None] * frequency[None, :]
    return jnp.concatenate([jnp.cos(angles), jnp.sin(angles)], axis=1)


def row_items(patch_counts, assignment, group_idx, total):
    numbers = jnp.arange(patch_counts.shape[0], dtype=jnp.int32)
    same_group = assignment[None, :] == assignment[:, None]
    earlier = numbers[None, :] < numbers[:, None]
    offsets = jnp.sum(jnp.where(same_group & earlier, patch_counts[None, :], 0), axis=1)
    row_ids = jnp.arange(total, dtype=jnp.int32)[:, None]
    inside = (
        (assignment[None, :] == group_idx)
        & (row_ids >= offsets[None, :])
        & (row_ids < offsets[None, :] + patch_counts[None, :])
    )
    return inside.astype(jnp.float32)


def gelu_tanh(pre_vals):
    return jax.nn.gelu(pre_vals, approximate=True)

LANES = 128


def pair_windows(heads, head_dim):
    windows = []
    for head in range(0, heads, 2):
        low, high = head * head_dim, (head + 2) * head_dim
        start, end = low // LANES * LANES, -(-high // LANES) * LANES
        windows.append((start, end, low, low + head_dim, high))
    return windows


def stacked(value, window):
    start, end, first, second, last = window
    lanes = start + lax.broadcasted_iota(jnp.int32, (1, end - start), 1)
    masks = [
        ((lanes >= low) & (lanes < high)).astype(jnp.float32).astype(jnp.bfloat16)
        for low, high in ((first, second), (second, last))
    ]
    return jnp.concatenate([value * mask for mask in masks], axis=0)


def tall(wide):
    half = wide.shape[1] // 2
    return jnp.concatenate([wide[:, :half], wide[:, half:]], axis=0)


def add_window(totals, window, value):
    start, end = window[:2]
    for lane in range(start, end, LANES):
        piece = value[:, lane - start : lane - start + LANES]
        totals[lane] = piece if lane not in totals else totals[lane] + piece


def joined(totals):
    return jnp.concatenate([totals[lane] for lane in sorted(totals)], axis=1)


class Spots:
    def __init__(self, rows, frames):
        self.frames, count = frames, rows // frames
        spot = lax.broadcasted_iota(jnp.int32, (frames, 2 * rows), 1) // frames % count
        self.own = [spot == at for at in range(count)]
        self.masks = [own.astype(jnp.float32).astype(jnp.bfloat16) for own in self.own]

    def compact(self, full):
        found = full[: self.frames]
        for at, own in enumerate(self.own[1:], 1):
            found = jnp.where(own, full[at * self.frames : (at + 1) * self.frames], found)
        return found

    def expand(self, compact):
        return jnp.concatenate([compact * mask for mask in self.masks], axis=0)

    def blocks(self, pairs):
        return jnp.concatenate(
            [
                self.compact(
                    lax.dot_general(left, right, COL_DIMS, preferred_element_type=jnp.float32)
                )
                for left, right in pairs
            ],
            axis=1,
        )

    def probs(self, pairs, scale):
        scores = self.blocks(pairs) * scale
        weights = jnp.exp(scores - jnp.max(scores, axis=0, keepdims=True))
        return weights / jnp.sum(weights, axis=0, keepdims=True)


def attend_kernel(frames, scale, proj_ref, mixed_ref):
    rows, width = mixed_ref.shape
    spots = Spots(rows, frames)
    windows = pair_windows(HEADS, width // HEADS)

    def part(index, window):
        return proj_ref[:, index * width + window[0] : index * width + window[1]]

    prob = spots.probs(
        [(part(1, window), stacked(part(0, window), window)) for window in windows], scale
    ).astype(jnp.bfloat16)
    totals = {}
    for at, window in enumerate(windows):
        wide = spots.expand(prob[:, at * 2 * rows : (at + 1) * 2 * rows])
        add_window(
            totals,
            window,
            lax.dot_general(
                tall(wide),
                stacked(part(2, window), window),
                ROW_DIMS,
                preferred_element_type=jnp.float32,
            ),
        )
    mixed_ref[...] = joined(totals).astype(jnp.bfloat16)


def attend_back_kernel(frames, scale, proj_ref, grad_ref, out_ref):
    rows, width = grad_ref.shape
    spots = Spots(rows, frames)
    windows = pair_windows(HEADS, width // HEADS)

    def part(index, window):
        return proj_ref[:, index * width + window[0] : index * width + window[1]]

    def grads(window):
        return stacked(grad_ref[:, window[0] : window[1]], window)

    prob = spots.probs(
        [(part(1, window), stacked(part(0, window), window)) for window in windows], scale
    )
    grad_prob = spots.blocks([(part(2, window), grads(window)) for window in windows])
    weighted = prob * grad_prob
    grad_scores = weighted - prob * jnp.sum(weighted, axis=0, keepdims=True)
    grad_scores, prob = grad_scores.astype(jnp.bfloat16), prob.astype(jnp.bfloat16)
    to_query, to_key, to_value = {}, {}, {}
    for at, window in enumerate(windows):
        span = slice(at * 2 * rows, (at + 1) * 2 * rows)
        wide = spots.expand(grad_scores[:, span])
        add_window(
            to_value,
            window,
            jnp.dot(
                spots.expand(prob[:, span]), grads(window), preferred_element_type=jnp.float32
            ),
        )
        add_window(
            to_key,
            window,
            jnp.dot(
                wide, stacked(part(0, window), window), preferred_element_type=jnp.float32
            ),
        )
        add_window(
            to_query,
            window,
            lax.dot_general(
                tall(wide),
                stacked(part(1, window), window),
                ROW_DIMS,
                preferred_element_type=jnp.float32,
            ),
        )
    out_ref[:, :width] = (joined(to_query) * scale).astype(jnp.bfloat16)
    out_ref[:, width : 2 * width] = (joined(to_key) * scale).astype(jnp.bfloat16)
    out_ref[:, 2 * width :] = joined(to_value).astype(jnp.bfloat16)


def tile_rows(positions, frames):
    for count in (8, 4, 2):
        if positions % count == 0:
            return count * frames
    return frames


def attend(projected, positions, frames, scale):
    rows, width = projected.shape[0], projected.shape[1] // 3
    tile = tile_rows(positions, frames)
    return pl.pallas_call(
        lambda *refs: attend_kernel(frames, scale, *refs),
        out_shape=jax.ShapeDtypeStruct((rows, width), jnp.bfloat16),
        grid=(rows // tile,),
        in_specs=[pl.BlockSpec((tile, 3 * width), lambda step: (step, 0))],
        out_specs=pl.BlockSpec((tile, width), lambda step: (step, 0)),
        cost_estimate=pl.CostEstimate(
            flops=9 * 10**9, bytes_accessed=8 * rows * width, transcendentals=0
        ),
        compiler_params=pltpu.CompilerParams(vmem_limit_bytes=VMEM_LIMIT),
        name="attend",
    )(projected)


def attend_back(projected, grad_mixed, positions, frames, scale):
    rows, width = projected.shape[0], projected.shape[1] // 3
    tile = tile_rows(positions, frames)
    return pl.pallas_call(
        lambda *refs: attend_back_kernel(frames, scale, *refs),
        out_shape=jax.ShapeDtypeStruct((rows, 3 * width), jnp.bfloat16),
        grid=(rows // tile,),
        in_specs=[
            pl.BlockSpec((tile, 3 * width), lambda step: (step, 0)),
            pl.BlockSpec((tile, width), lambda step: (step, 0)),
        ],
        out_specs=pl.BlockSpec((tile, 3 * width), lambda step: (step, 0)),
        cost_estimate=pl.CostEstimate(
            flops=12 * 10**9, bytes_accessed=14 * rows * width, transcendentals=0
        ),
        compiler_params=pltpu.CompilerParams(vmem_limit_bytes=VMEM_LIMIT),
        name="attend_back",
    )(projected, grad_mixed)


VMEM_LIMIT = 58 << 20
BF16, F32 = jnp.bfloat16, jnp.float32


def row_tile(rows):
    for tile in (224, 128, 112, 64, 32, 16):
        if rows % tile == 0:
            return tile
    return rows


def dot(left, right, dims=(((1,), (0,)), ((), ()))):
    return lax.dot_general(left, right, dims, preferred_element_type=F32)


def call(kernel, name, grid, ins, outs, scratch=(), flops=0, vmem=VMEM_LIMIT):
    moved = sum(array.size * array.dtype.itemsize for array, _ in ins)
    moved += sum(math.prod(shape) * jnp.dtype(dtype).itemsize for shape, dtype, _ in outs)
    return pl.pallas_call(
        kernel,
        out_shape=[jax.ShapeDtypeStruct(shape, dtype) for shape, dtype, _ in outs],
        grid=grid,
        in_specs=[spec for _, spec in ins],
        out_specs=[spec for _, _, spec in outs],
        scratch_shapes=list(scratch),
        cost_estimate=pl.CostEstimate(flops=flops, bytes_accessed=moved, transcendentals=0),
        compiler_params=pltpu.CompilerParams(vmem_limit_bytes=vmem),
        name=name,
    )(*[array for array, _ in ins])


HBM = pl.BlockSpec(memory_space=pl.ANY)
SCALARS = pl.BlockSpec(memory_space=pltpu.SMEM)


def whole(array):
    return pl.BlockSpec(array.shape, lambda step: (0,) * array.ndim)


def tiled(tile, width):
    return pl.BlockSpec((tile, width), lambda step: (step, 0))


class Pieces:
    def __init__(self, arrays, places, shape, by_columns, flipped):
        self.arrays, self.places, self.shape = arrays, places, shape
        self.by_columns, self.flipped = by_columns, flipped

    def quarter(self, where_ref, turn):
        return where_ref[0] ^ turn if self.flipped else turn

    def columns(self, slot):
        width = self.shape[1] // 4
        return pl.ds(pl.multiple_of(slot * width, width), width)

    def start(self, where_ref, refs, full, sems):
        for ref, place in zip(refs, self.places):
            slot, first, count = place(where_ref[0], where_ref[1])
            if self.by_columns:
                target = full.at[pl.ds(first, count), self.columns(slot)]
                pltpu.make_async_copy(ref, target, sems.at[slot]).start()
                continue
            for turn in range(count):
                target = full.at[first + turn, slot]
                sem = sems.at[(first + turn) // (self.shape[0] // 4)]
                pltpu.make_async_copy(ref.at[turn], target, sem).start()

    def part(self, full, at):
        if self.by_columns:
            return full.at[:, self.columns(at)]
        turns = self.shape[0] // 4
        return full.at[at * turns : (at + 1) * turns]

    def wait(self, at, full, sems):
        part = self.part(full, at)
        pltpu.make_async_copy(part, part, sems.at[at]).wait()

    def scratch(self):
        return [pltpu.VMEM(self.shape, BF16), pltpu.SemaphoreType.DMA((5,))]


def norm_parts(values):
    center = values - jnp.mean(values, axis=1, keepdims=True)
    inverse = lax.rsqrt(jnp.mean(center * center, axis=1, keepdims=True) + 1e-06)
    return center * inverse, inverse


def norm_back(normed, inverse, grad):
    mean_grad = jnp.mean(grad, axis=1, keepdims=True)
    mean_both = jnp.mean(grad * normed, axis=1, keepdims=True)
    return (grad - mean_grad - normed * mean_both) * inverse


def gather_order(first, count, frames, positions, own_frames, chunk):
    at = first + lax.broadcasted_iota(jnp.int32, (count, 1), 0)
    source = lax.broadcasted_iota(jnp.int32, (1, frames // own_frames * chunk), 1)
    frame, position = at % frames, at // frames
    wanted = frame // own_frames * chunk + frame % own_frames * positions + position
    return (source == wanted).astype(F32).astype(BF16)


def row_order(rows, first, count, inner, outer):
    at = first + lax.broadcasted_iota(jnp.int32, (count, 1), 0)
    source = lax.broadcasted_iota(jnp.int32, (1, rows), 1)
    return (source == (at % outer) * inner + at // outer).astype(F32).astype(BF16)


def clip_sums(hot, values):
    high = values.astype(BF16)
    low = (values - high.astype(F32)).astype(BF16)
    return dot(hot, high, ROW_DIMS) + dot(hot, low, ROW_DIMS)


def by_tile(my_rows, mod, frames):
    count = row_tile(my_rows.shape[0] * frames) // frames
    tiles = my_rows.astype(BF16).reshape(-1, count, my_rows.shape[1])
    tiles = jnp.pad(tiles, ((0, 0), (0, -count % 8), (0, 0)))
    return lax.dot_general(tiles, mod, (((2,), (0,)), ((), ())), preferred_element_type=F32)


def tile_mod(mod):
    return pl.BlockSpec((1, *mod.shape[1:]), lambda step: (step, 0, 0))


def spread_rows(mod_ref, part, count, frames):
    width = mod_ref.shape[2] // 6
    cols = slice(part * width, (part + 1) * width)
    rows = [
        jnp.broadcast_to(mod_ref[0, at : at + 1, cols], (frames, width)) for at in range(count)
    ]
    return jnp.concatenate(rows, axis=0)


def first_step(step, action):
    @pl.when(step == 0)
    def _():
        action()


def add_into(ref, index, value):
    @pl.when(pl.program_id(0) == 0)
    def _():
        ref[index] = jnp.zeros_like(ref[index])

    ref[index] += value


def qkv_call(where, arrived, mod, pieces, positions, frames, own_frames):
    rows, width = positions * frames, arrived.shape[1]
    chunk = arrived.shape[0] * own_frames // frames
    tile = row_tile(rows)
    steps = rows // tile
    count = len(pieces.arrays)

    def kernel(where_ref, x_ref, mod_ref, *rest):
        piece_refs, rest = rest[:count], rest[count:]
        x_out, first_out, proj_out, full_out, full, sems = rest
        step = pl.program_id(0)

        @pl.when(step == 0)
        def _():
            pieces.start(where_ref, piece_refs, full, sems)

        order = gather_order(step * tile, tile, frames, positions, own_frames, chunk)
        inputs = dot(order, x_ref[...])
        x_out[...] = inputs.astype(BF16)
        normed, _ = norm_parts(inputs)
        shift = spread_rows(mod_ref, 0, tile // frames, frames)
        scale = spread_rows(mod_ref, 1, tile // frames, frames)
        first = (normed * (1.0 + scale) + shift).astype(BF16)
        first_out[...] = first
        back = pltpu.make_async_copy(full, full_out, sems.at[4])

        @pl.when(step == 0)
        def _():
            for turn in range(4):
                slot = pieces.quarter(where_ref, turn)
                pieces.wait(slot, full, sems)

                @pl.when(slot < 3)
                def _():
                    weight = pieces.part(full, slot)[...]
                    proj_out[:, pieces.columns(slot)] = dot(first, weight).astype(BF16)

            back.start()

        @pl.when(step > 0)
        def _():
            proj_out[...] = dot(first, full[:, : 3 * width]).astype(BF16)

        @pl.when(step == steps - 1)
        def _():
            back.wait()

    return call(
        kernel,
        "project",
        (steps,),
        [
            (where, SCALARS),
            (arrived, whole(arrived)),
            (mod, tile_mod(mod)),
            *[(array, HBM) for array in pieces.arrays],
        ],
        [
            ((rows, width), BF16, tiled(tile, width)),
            ((rows, width), BF16, tiled(tile, width)),
            ((rows, 3 * width), BF16, tiled(tile, 3 * width)),
            (pieces.shape, BF16, HBM),
        ],
        pieces.scratch(),
        flops=20 * 10**9,
    )


def out_call(mixed, x_rows, mod, full_attn, frames):
    rows, width = mixed.shape
    tile = row_tile(rows)

    def kernel(mixed_ref, x_ref, mod_ref, w_ref, attn_out, middle_out, second_out):
        attn = dot(mixed_ref[...], w_ref[...])
        shift, scale, gate = [
            spread_rows(mod_ref, part, tile // frames, frames)
            for part in (3, 4, 2)
        ]
        middle = x_ref[...].astype(F32) + gate * attn
        normed, _ = norm_parts(middle)
        attn_out[...] = attn.astype(BF16)
        middle_out[...] = middle
        second_out[...] = (normed * (1.0 + scale) + shift).astype(BF16)

    return call(
        kernel,
        "attn_out",
        (rows // tile,),
        [
            (mixed, tiled(tile, width)),
            (x_rows, tiled(tile, width)),
            (mod, tile_mod(mod)),
            (full_attn, pl.BlockSpec((width, width), lambda step: (0, 3))),
        ],
        [
            ((rows, width), BF16, tiled(tile, width)),
            ((rows, width), F32, tiled(tile, width)),
            ((rows, width), BF16, tiled(tile, width)),
        ],
        flops=9 * 10**9,
    )


GELU_A = math.sqrt(2.0 / math.pi)
GELU_B = GELU_A * 0.044715


def fc1_call(where, second_in, bias, pieces):
    rows, width = second_in.shape
    tile = row_tile(rows)
    steps = rows // tile
    count = len(pieces.arrays)
    part = pieces.shape[1] // 4

    def kernel(where_ref, x_ref, bias_ref, *rest):
        piece_refs, rest = rest[:count], rest[count:]
        post_out, slope_out, full_out, full, sems = rest
        step = pl.program_id(0)
        back = pltpu.make_async_copy(full, full_out, sems.at[4])

        def run(cols):
            pre = dot(x_ref[...], full[:, cols]) + bias_ref[:, cols].astype(F32)
            square = pre * pre
            curve = jnp.tanh(pre * (GELU_A + GELU_B * square))
            half = 0.5 + 0.5 * curve
            post_out[:, cols] = (pre * half).astype(BF16)
            rise = (0.5 * pre) * (1.0 - curve * curve)
            slope_out[:, cols] = (half + rise * (GELU_A + 3.0 * GELU_B * square)).astype(BF16)

        @pl.when(step == 0)
        def _():
            pieces.start(where_ref, piece_refs, full, sems)
            for turn in range(4):
                slot = pieces.quarter(where_ref, turn)
                pieces.wait(slot, full, sems)
                run(pieces.columns(slot))
            back.start()

        @pl.when(step > 0)
        def _():
            for half in range(2):
                run(slice(half * 2 * part, (half + 1) * 2 * part))

        @pl.when(step == steps - 1)
        def _():
            back.wait()

    return call(
        kernel,
        "fc1",
        (steps,),
        [
            (where, SCALARS),
            (second_in, tiled(tile, width)),
            (bias, whole(bias)),
            *[(array, HBM) for array in pieces.arrays],
        ],
        [
            ((rows, 4 * part), BF16, tiled(tile, 4 * part)),
            ((rows, 4 * part), BF16, tiled(tile, 4 * part)),
            (pieces.shape, BF16, HBM),
        ],
        pieces.scratch(),
        flops=25 * 10**9,
    )


def cot_call(arrived, hot, mod, positions, frames, own_frames):
    rows, width = arrived.shape
    tile = row_tile(rows)

    def kernel(cot_ref, hot_ref, mod_ref, rows_out, mlp_out):
        first = pl.program_id(0) * tile
        order = gather_order(first, tile, frames, positions, own_frames, own_frames * positions)
        hot = hot_ref[...]
        valid = jnp.sum(hot.astype(F32), axis=1, keepdims=True)
        grad = dot(order, cot_ref[...]) * valid
        rows_out[...] = grad.astype(BF16)
        mlp_out[...] = (grad * spread_rows(mod_ref, 5, tile // frames, frames)).astype(BF16)

    return call(
        kernel,
        "cotangent",
        (rows // tile,),
        [
            (arrived, whole(arrived)),
            (hot, tiled(tile, hot.shape[1])),
            (mod, tile_mod(mod)),
        ],
        [
            ((rows, width), BF16, tiled(tile, width)),
            ((rows, width), BF16, tiled(tile, width)),
        ],
        flops=6 * 10**9,
    )


def fc2_call(where, post_act, slope, grad_mlp, grad_rows, middle, hot, mod, pieces, positions, frames):
    rows, hidden = post_act.shape
    width = grad_mlp.shape[1]
    tile = row_tile(rows)
    steps = rows // tile
    count = len(pieces.arrays)
    clips = hot.shape[1]

    def kernel(where_ref, post_ref, slope_ref, gmlp_ref, grows_ref, mid_ref, hot_ref, mod_ref, *rest):
        piece_refs, rest = rest[:count], rest[count:]
        block_out, pre_out, bias_out, gate_out, full, sems, held, sums = rest
        step = pl.program_id(0)

        def run(first, last):
            part = hidden // 4
            cols = slice(first * part, last * part)
            turns = pieces.shape[0] // 4
            weight = full[first * turns : last * turns].reshape((last - first) * part, width)
            term = dot(post_ref[:, cols], weight)
            sums[...] = term if not first else sums[...] + term
            grad_pre = dot(gmlp_ref[...], weight, COL_DIMS) * slope_ref[:, cols].astype(F32)
            grad_pre = grad_pre.astype(BF16)
            pre_out[:, cols] = grad_pre
            total = jnp.sum(grad_pre.astype(F32), axis=0, keepdims=True)
            add_into(bias_out, (slice(None), cols), total)

        @pl.when(step == 0)
        def _():
            pieces.start(where_ref, piece_refs, full, sems)
            for at in range(4):
                pieces.wait(at, full, sems)
                run(at, at + 1)

        @pl.when(step > 0)
        def _():
            run(0, 2)
            run(2, 4)

        total = sums[...]
        hot = hot_ref[...]
        valid = jnp.sum(hot.astype(F32), axis=1, keepdims=True)
        gate = spread_rows(mod_ref, 5, tile // frames, frames)
        result = valid * (mid_ref[...] + gate * total)
        held[pl.ds(pl.multiple_of(step * tile, 16), tile), :] = result.astype(BF16)
        add_into(gate_out, slice(None), clip_sums(hot, grows_ref[...].astype(F32) * total))

        @pl.when(step == steps - 1)
        def _():
            for at in range(steps):
                order = row_order(rows, at * tile, tile, frames, positions)
                block_out[at * tile : (at + 1) * tile, :] = dot(order, held[...]).astype(BF16)

    return call(
        kernel,
        "fc2",
        (steps,),
        [
            (where, SCALARS),
            (post_act, tiled(tile, hidden)),
            (slope, tiled(tile, hidden)),
            (grad_mlp, tiled(tile, width)),
            (grad_rows, tiled(tile, width)),
            (middle, tiled(tile, width)),
            (hot, tiled(tile, clips)),
            (mod, tile_mod(mod)),
            *[(array, HBM) for array in pieces.arrays],
        ],
        [
            ((rows, width), BF16, pl.BlockSpec((rows, width), lambda step: (0, 0))),
            ((rows, hidden), BF16, tiled(tile, hidden)),
            ((1, hidden), F32, pl.BlockSpec((1, hidden), lambda step: (0, 0))),
            ((clips, width), F32, pl.BlockSpec((clips, width), lambda step: (0, 0))),
        ],
        [*pieces.scratch(), pltpu.VMEM((rows, width), BF16), pltpu.VMEM((tile, width), F32)],
        flops=44 * 10**9,
    )


def load_and_dot(step, left_ref, w_ref, held, sems, total, parts):
    width = left_ref.shape[1] // parts
    runs = [slice(at * width, (at + 1) * width) for at in range(parts)]
    loads = [
        pltpu.make_async_copy(w_ref.at[:, run], held.at[:, run], sems.at[at])
        for at, run in enumerate(runs)
    ]

    @pl.when(step == 0)
    def _():
        for load in loads:
            load.start()
        for at, load in enumerate(loads):
            load.wait()
            term = dot(left_ref[:, runs[at]], held[:, runs[at]], COL_DIMS)
            total[...] = term if not at else total[...] + term

    @pl.when(step > 0)
    def _():
        total[...] = dot(left_ref[...], held[...], COL_DIMS)

    return total[...]


def fc1_back_call(grad_pre, full_fc1, middle, attn_out, grad_rows, hot, mod, full_attn, frames):
    rows, hidden = grad_pre.shape
    width = middle.shape[1]
    tile = row_tile(rows)
    clips = hot.shape[1]

    def kernel(pre_ref, w_ref, mid_ref, attn_ref, grows_ref, hot_ref, mod_ref, wo_ref, *outs):
        gmid_out, gattn_out, gmix_out, sums_out, held, sems, total = outs
        step = pl.program_id(0)
        grad = load_and_dot(step, pre_ref, w_ref, held, sems, total, 4)
        hot = hot_ref[...]
        scale = spread_rows(mod_ref, 4, tile // frames, frames)
        gate = spread_rows(mod_ref, 2, tile // frames, frames)
        normed, inverse = norm_parts(mid_ref[...])
        grad_middle = grows_ref[...].astype(F32) + norm_back(normed, inverse, grad * (1.0 + scale))
        gmid_out[...] = grad_middle
        grad_attn = (grad_middle * gate).astype(BF16)
        gattn_out[...] = grad_attn
        gmix_out[...] = dot(grad_attn, wo_ref[...], COL_DIMS).astype(BF16)
        add_into(sums_out, 0, clip_sums(hot, grad_middle * attn_ref[...].astype(F32)))
        add_into(sums_out, 1, clip_sums(hot, grad))
        add_into(sums_out, 2, clip_sums(hot, grad * normed))

    return call(
        kernel,
        "fc1_back",
        (rows // tile,),
        [
            (grad_pre, tiled(tile, hidden)),
            (full_fc1, HBM),
            (middle, tiled(tile, width)),
            (attn_out, tiled(tile, width)),
            (grad_rows, tiled(tile, width)),
            (hot, tiled(tile, clips)),
            (mod, tile_mod(mod)),
            (full_attn, pl.BlockSpec((width, width), lambda step: (0, 3))),
        ],
        [
            ((rows, width), F32, tiled(tile, width)),
            ((rows, width), BF16, tiled(tile, width)),
            ((rows, width), BF16, tiled(tile, width)),
            ((3, clips, width), F32, pl.BlockSpec((3, clips, width), lambda step: (0, 0, 0))),
        ],
        [
            pltpu.VMEM(full_fc1.shape, BF16),
            pltpu.SemaphoreType.DMA((4,)),
            pltpu.VMEM((tile, width), F32),
        ],
        flops=32 * 10**9,
    )


def qkv_back_call(grad_proj, full_attn, x_rows, grad_middle, hot, mod, positions, frames):
    rows, width = x_rows.shape
    tile = row_tile(rows)
    steps = rows // tile
    clips = hot.shape[1]

    def kernel(proj_ref, w_ref, x_ref, gmid_ref, hot_ref, mod_ref, tok_out, sums_out, held, w_held, sems, total):
        step = pl.program_id(0)
        grad = load_and_dot(step, proj_ref, w_ref, w_held, sems, total, 3)
        hot = hot_ref[...]
        scale = spread_rows(mod_ref, 1, tile // frames, frames)
        normed, inverse = norm_parts(x_ref[...].astype(F32))
        result = gmid_ref[...] + norm_back(normed, inverse, grad * (1.0 + scale))
        held[pl.ds(pl.multiple_of(step * tile, 16), tile), :] = result.astype(BF16)
        add_into(sums_out, 0, clip_sums(hot, grad))
        add_into(sums_out, 1, clip_sums(hot, grad * normed))

        @pl.when(step == steps - 1)
        def _():
            for at in range(steps):
                order = row_order(rows, at * tile, tile, frames, positions)
                tok_out[at * tile : (at + 1) * tile, :] = dot(order, held[...]).astype(BF16)

    return call(
        kernel,
        "project_back",
        (steps,),
        [
            (grad_proj, tiled(tile, 3 * width)),
            (full_attn, HBM),
            (x_rows, tiled(tile, width)),
            (grad_middle, tiled(tile, width)),
            (hot, tiled(tile, clips)),
            (mod, tile_mod(mod)),
        ],
        [
            ((rows, width), BF16, pl.BlockSpec((rows, width), lambda step: (0, 0))),
            ((2, clips, width), F32, pl.BlockSpec((2, clips, width), lambda step: (0, 0, 0))),
        ],
        [
            pltpu.VMEM((rows, width), BF16),
            pltpu.VMEM((width, 3 * width), BF16),
            pltpu.SemaphoreType.DMA((3,)),
            pltpu.VMEM((tile, width), F32),
        ],
        flops=23 * 10**9,
    )


def split_store(product, where_ref, keep_out, give_out, rows, slot_first, slot=0):
    units = product.shape[0] // rows
    for core in range(2):

        @pl.when(where_ref[1] == core)
        def _():
            for unit in range(units):
                piece = product[unit * rows : (unit + 1) * rows]
                side = unit % 2 if slot_first else unit // 4
                out = keep_out if side == core else give_out
                if slot_first:
                    out[slot, unit // 2] = piece
                else:
                    out[unit % 4, 0] = piece


def terms_out(chips, rows, width, slot_first, slots=1):
    if slot_first:
        spec = pl.BlockSpec((slots, chips, rows, width), lambda step: (step, 0, 0, 0))
    else:
        spec = pl.BlockSpec((4, 1, rows, width), lambda step: (0, step, 0, 0))
    return [((4, chips, rows, width), BF16, spec)] * 2


def fc2_terms(where, post_act, grad_mlp, chips):
    count, hidden = post_act.shape
    width = grad_mlp.shape[1]
    block, rows = hidden // chips, hidden // chips // 8

    def kernel(where_ref, left_ref, right_ref, keep_out, give_out):
        product = dot(left_ref[...], right_ref[...], ROW_DIMS).astype(BF16)
        split_store(product, where_ref, keep_out, give_out, rows, False)

    return call(
        kernel,
        "fc2_terms",
        (chips,),
        [
            (where, SCALARS),
            (post_act, pl.BlockSpec((count, block), lambda step: (0, step))),
            (grad_mlp, whole(grad_mlp)),
        ],
        terms_out(chips, rows, width, False),
        flops=18 * 10**9,
    )


def fc1_terms(where, second_in, grad_pre, chips):
    count, hidden = grad_pre.shape
    width = second_in.shape[1]
    rows, part = width // chips // 2, hidden // 4

    def kernel(where_ref, left_ref, right_ref, keep_out, give_out):
        product = dot(left_ref[...], right_ref[...], ROW_DIMS).astype(BF16)
        for slot in range(2):
            piece = product[:, slot * part : (slot + 1) * part]
            split_store(piece, where_ref, keep_out, give_out, rows, True, slot)

    return call(
        kernel,
        "fc1_terms",
        (2,),
        [
            (where, SCALARS),
            (second_in, whole(second_in)),
            (grad_pre, pl.BlockSpec((count, 2 * part), lambda step: (0, step))),
        ],
        terms_out(chips, rows, part, True, 2),
        flops=18 * 10**9,
    )


def attn_terms(where, first_in, grad_proj, mixed, grad_attn, chips):
    count, width = first_in.shape
    rows = width // chips // 2

    def kernel(where_ref, first_ref, proj_ref, mixed_ref, attn_ref, keep_out, give_out):
        step = pl.program_id(0)

        @pl.when(step < 3)
        def _():
            product = dot(first_ref[...], proj_ref[...], ROW_DIMS).astype(BF16)
            split_store(product, where_ref, keep_out, give_out, rows, True)

        @pl.when(step == 3)
        def _():
            product = dot(mixed_ref[...], attn_ref[...], ROW_DIMS).astype(BF16)
            split_store(product, where_ref, keep_out, give_out, rows, True)

    return call(
        kernel,
        "attn_terms",
        (4,),
        [
            (where, SCALARS),
            (first_in, whole(first_in)),
            (
                grad_proj,
                pl.BlockSpec((count, width), lambda step: (0, jnp.minimum(step, 2))),
            ),
            (mixed, whole(mixed)),
            (grad_attn, whole(grad_attn)),
        ],
        terms_out(chips, rows, width, True),
        flops=19 * 10**9,
    )


def plane_terms(where, keep, got):
    _, chips, rows, width = keep.shape
    cut = chips // 2
    flips = (1, 3, 2, 0)

    def place(step, where_ref):
        flip = 0
        for at in range(4):
            flip = jnp.where(step == at, flips[at], flip)
        return where_ref[0] ^ flip, 0, 0, 0

    def kernel(where_ref, keep_ref, got_ref, x_out, y_out, stay_out):
        targets = {
            1: ((x_out, 0), (stay_out, 3)),
            3: ((x_out, 1), (y_out, 1)),
            2: ((stay_out, 1), (y_out, 0)),
            0: ((stay_out, 0), (stay_out, 2)),
        }
        for at, flip in enumerate(flips):

            @pl.when(pl.program_id(0) == at)
            def _(flip=flip):
                for half, (out, slot) in enumerate(targets[flip]):
                    span = slice(half * cut, half * cut + cut)
                    out[slot] = keep_ref[0, span] + got_ref[0, span]

    block = (1, chips, rows, width)
    shapes = [(2, cut, rows, width), (2, cut, rows, width), (4, cut, rows, width)]
    return pl.pallas_call(
        kernel,
        out_shape=[jax.ShapeDtypeStruct(shape, BF16) for shape in shapes],
        grid_spec=pltpu.PrefetchScalarGridSpec(
            num_scalar_prefetch=1,
            grid=(4,),
            in_specs=[pl.BlockSpec(block, place), pl.BlockSpec(block, place)],
            out_specs=[
                pl.BlockSpec(shape, lambda step, where_ref: (0, 0, 0, 0)) for shape in shapes
            ],
        ),
        cost_estimate=pl.CostEstimate(
            flops=7 * 10**9, bytes_accessed=6 * keep.size, transcendentals=0
        ),
        compiler_params=pltpu.CompilerParams(vmem_limit_bytes=VMEM_LIMIT),
        name="plane_terms",
    )(where, keep, got)


X_SWAP = [(0, 1), (1, 0), (2, 3), (3, 2)]
Y_SWAP = [(0, 2), (2, 0), (1, 3), (3, 1)]


def swap_x(value):
    return lax.ppermute(value, "item", X_SWAP)


def swap_y(value):
    return lax.ppermute(value, "item", Y_SWAP)


def swap_core(value):
    count = lax.axis_size("frame")
    return lax.ppermute(value, "frame", [(at, at ^ 1) for at in range(count)])


def is_square():
    return lax.axis_size("item") == 4 and lax.axis_size("frame") % 2 == 0


def after(value, *others):
    return lax.optimization_barrier((value, *others))[0]


def after2(values, *others):
    return lax.optimization_barrier((*values, *others))[: len(values)]


def pick(stack, index):
    return lax.dynamic_index_in_dim(stack, index, 0, keepdims=False)


def by_column_quarter(stack):
    return jnp.concatenate([stack[part] for part in range(4)], axis=1)


def gather_frame(parts):
    if not is_square():
        return lax.all_gather(parts, "frame", axis=1)
    return lax.all_gather(pick(parts, lax.axis_index("item")), "frame", axis=0)


class Spread:
    def __init__(self, gathered, slot_first):
        self.gathered, self.slot_first = gathered, slot_first
        self.square = is_square()

    def near(self, *wait_for):
        if not self.square:
            return ()
        self.gathered = after(self.gathered, *wait_for)
        half = self.gathered.shape[0] // 2
        core = lax.axis_index("frame") % 2
        own = lax.dynamic_slice_in_dim(self.gathered, core * half, half, 0)
        self.cut = half // 2
        self.from_x, self.from_y = swap_x(own), swap_y(own)
        return self.from_x, self.from_y

    def far(self, *wait_for):
        if not self.square:
            return ()
        from_x, from_y = after2((self.from_x, self.from_y), *wait_for)
        self.far_low, self.far_high = swap_y(from_x[: self.cut]), swap_x(from_y[self.cut :])
        self.core_x, self.core_y = swap_core(from_x), swap_core(from_y)
        return self.far_low, self.far_high

    def pieces(self):
        gathered, slot_first = self.gathered, self.slot_first
        if not self.square:
            _, count, rows, width = gathered.shape
            if slot_first:
                return Pieces(
                    [gathered[part].reshape(count * rows, width) for part in range(4)],
                    [lambda item, core, part=part: (part, 0, count * rows) for part in range(4)],
                    (count * rows, 4 * width),
                    True,
                    False,
                )
            return Pieces(
                [gathered[part] for part in range(4)],
                [lambda item, core, part=part: (part, 0, count) for part in range(4)],
                (count, 4, rows, width),
                False,
                False,
            )
        count, rows, width = gathered.shape
        half, cut = count // 2, self.cut
        far = [self.far_low, self.far_high]
        arrays = [gathered, self.from_x, self.from_y, *far, self.core_x, self.core_y]
        arrays += [swap_core(value) for value in far]
        unit = rows if slot_first else 1
        if slot_first:
            arrays = [array.reshape(-1, width) for array in arrays]
            shape = (count * rows, 4 * width)
        else:
            shape = (count, 4, rows, width)
        places = [lambda item, core: (item, 0, count * unit)]
        for flip in (0, 1):
            for slot, start, length in ((1, 0, half), (2, 0, half), (3, 0, cut), (3, cut, half - cut)):
                places.append(
                    lambda item, core, flip=flip, slot=slot, start=start, length=length: (
                        item ^ slot,
                        ((core ^ flip) * half + start) * unit,
                        length * unit,
                    )
                )
        order = (0, 1, 5, 2, 6, 3, 4, 7, 8)
        arrays, places = [arrays[at] for at in order], [places[at] for at in order]
        return Pieces(arrays, places, shape, slot_first, True)


class Collect:
    def __init__(self, where, keep, give):
        self.where, self.keep, self.give = where, keep, give
        self.item = lax.axis_index("item")

    def pair(self, *wait_for):
        self.give = after(self.give, *wait_for)
        self.got = swap_core(self.give)

    def near(self, *wait_for):
        got = after(self.got, *wait_for)
        x_out, y_out, self.stay = plane_terms(self.where, self.keep, got)
        self.x_in, self.y_in = swap_x(x_out), swap_y(y_out)
        return (self.stay,)

    def far(self, *wait_for):
        x_in, y_in = after2((self.x_in, self.y_in), *wait_for)
        low_on, high_on = self.stay[1] + x_in[1], self.stay[3] + y_in[1]
        self.low, self.high = self.stay[0] + x_in[0], self.stay[2] + y_in[0]
        self.y_far, self.x_far = swap_y(low_on), swap_x(high_on)
        return low_on, high_on

    def line(self, *wait_for):
        y_far, x_far = after2((self.y_far, self.x_far), *wait_for)
        plane = jnp.concatenate([self.low + y_far, self.high + x_far], axis=0)
        count = lax.axis_size("frame")
        groups = [list(range(side, count, 2)) for side in range(2)]
        self.own = lax.psum_scatter(
            plane, "frame", scatter_dimension=0, tiled=False, axis_index_groups=groups
        )
        return (plane,)

    def finish(self, *wait_for):
        own, item = after(self.own, *wait_for), self.item
        far = lax.ppermute(own, "item", [(at, at ^ 3) for at in range(4)])
        stack = jnp.stack([own, swap_x(own), swap_y(own), far])
        return jnp.stack([pick(stack, item ^ part) for part in range(4)])


def sum_plain(partial):
    share = lax.psum_scatter(partial.astype(BF16), "frame", scatter_dimension=1, tiled=False)
    return lax.psum(share, "item")


def share_small(value):
    count = lax.axis_size("frame")
    return lax.all_to_all(
        jnp.broadcast_to(value[None], (count, *value.shape)), "frame", 0, 0, tiled=False
    )


def sum_items(value):
    if not is_square():
        return lax.psum(value.astype(BF16), "item").astype(F32)
    low = value.astype(BF16)
    far = lax.ppermute(low, "item", [(at, at ^ 3) for at in range(4)])
    return value + swap_x(low).astype(F32) + swap_y(low).astype(F32) + far.astype(F32)


def round_up(number, unit):
    return -(-number // unit) * unit


def body(
    tokens,
    cotangent,
    patch_counts,
    assignment,
    timesteps,
    class_ids,
    w_qkv,
    w_out,
    w_fc1,
    b_fc1,
    w_fc2,
    w_ada,
    b_ada,
    class_table,
):
    frame_count = lax.axis_size("frame")
    group_idx = lax.axis_index("item")
    frame_pos = lax.axis_index("frame")
    _, own_frames, capacity, width = tokens.shape
    frames = own_frames * frame_count
    positions = capacity // frame_count
    rows = frames * positions
    clips = patch_counts.shape[0]
    attn_scale = 1.0 / math.sqrt(width // HEADS)
    where = jnp.stack([group_idx, frame_pos % 2, frame_pos]).astype(jnp.int32)

    def to_positions(value, *extra):
        chunks = value[0].reshape(own_frames, frame_count, positions, width).transpose(1, 0, 2, 3)
        chunks = chunks.reshape(frame_count, own_frames * positions, width)
        for more in extra:
            more = jnp.broadcast_to(more[None], (frame_count, *more.shape))
            chunks = jnp.concatenate([chunks, more], axis=1)
        return lax.all_to_all(chunks, "frame", 0, 0, tiled=True)

    def to_frames(value, *wait_for):
        chunks = value.reshape(frame_count, own_frames, positions, width)
        moved = after(lax.all_to_all(chunks, "frame", 0, 0, tiled=True), *wait_for)
        return moved.transpose(1, 0, 2, 3).reshape(1, own_frames, capacity, width)

    layout = row_items(patch_counts, assignment, group_idx, capacity)
    my_rows = lax.dynamic_slice_in_dim(layout, frame_pos * positions, positions, 0)
    class_hot = (class_ids[:, None] == jnp.arange(CLASSES, dtype=jnp.int32)[None, :]).astype(F32)
    condition = time_features(timesteps) + jnp.dot(class_hot, class_table, precision=HIGHEST)
    activated = jax.nn.silu(condition)
    ada_part = jnp.dot(activated, w_ada.astype(F32), precision=HIGHEST) + b_ada.astype(F32)

    ada_cols, bias_cols = b_ada.shape[0], b_fc1.shape[0]
    small_rows, small_cols = round_up(clips + 1, 16), round_up(max(ada_cols, bias_cols), LANES)
    small = jnp.concatenate(
        [
            jnp.pad(ada_part.astype(BF16), ((0, 0), (0, width - ada_cols))),
            jnp.pad(b_fc1[None], ((0, small_rows - clips - 1), (0, width - bias_cols))),
        ],
        axis=0,
    )
    x_arrived = to_positions(tokens, small)
    small_all = x_arrived[:, own_frames * positions :]
    x_arrived = x_arrived.reshape(-1, width)
    clip_slots = round_up(clips, 16)
    mod = small_all[:, :clips, :ada_cols].transpose(1, 0, 2).reshape(clips, -1)
    mod = by_tile(my_rows, mod, frames)
    bias = small_all[:, clips, :bias_cols].reshape(1, -1)
    hot = jnp.pad(my_rows.astype(BF16), ((0, 0), (0, clip_slots - clips)))
    hot = jnp.repeat(hot, frames, axis=0)

    shard_rows = w_out.shape[0]
    got_attn = gather_frame(jnp.stack([*jnp.split(w_qkv, 3, axis=1), w_out]))
    spread_attn = Spread(got_attn, True)
    near_attn = spread_attn.near()
    got_fc1 = gather_frame(
        jnp.stack(jnp.split(w_fc1, 4, axis=1))
    )
    far_attn = spread_attn.far()
    fc2_rows = w_fc2.shape[0] // 4
    got_fc2 = gather_frame(after(w_fc2.reshape(4, fc2_rows, width), x_arrived, *far_attn))

    square = is_square()
    chips = frame_count // 2
    spread_fc1 = Spread(got_fc1, True)
    spread_fc2 = Spread(got_fc2, False)
    near_fc1 = spread_fc1.near(*far_attn)
    x_rows, first_in, projected, full_attn = qkv_call(
        where, x_arrived, mod, spread_attn.pieces(), positions, frames, own_frames
    )
    cot_arrived = to_positions(after(cotangent, projected)).reshape(rows, width)
    mixed = attend(after(projected, *near_fc1), positions, frames, attn_scale)
    far_fc1 = spread_fc1.far()
    near_fc2 = spread_fc2.near(*far_fc1)
    attn_out, middle, second_in = out_call(
        after(mixed, *far_fc1), x_rows, mod, full_attn, frames
    )
    far_fc2 = spread_fc2.far()
    post_act, slope, full_fc1 = fc1_call(
        where, second_in, bias, spread_fc1.pieces()
    )
    grad_rows, grad_mlp = cot_call(after(cot_arrived, post_act), hot, mod, positions, frames, own_frames)

    if square:
        sum_fc2 = Collect(where, *fc2_terms(where, post_act, after(grad_mlp, *near_fc2), chips))
        sum_fc2.pair()
        seen = (sum_fc2.give,)
    else:
        part_fc2 = lax.dot_general(post_act, grad_mlp, ROW_DIMS, preferred_element_type=F32)
        part_fc2 = part_fc2.reshape(frame_count, 4, fc2_rows, width).transpose(1, 0, 2, 3)
        seen = ()
    block_rows, grad_pre, part_bias, sum_gate_mlp = fc2_call(
        where,
        post_act,
        slope,
        after(grad_mlp, *seen),
        grad_rows,
        middle,
        hot,
        mod,
        spread_fc2.pieces(),
        positions,
        frames,
    )
    if square:
        seen = sum_fc2.near(grad_pre)
        sum_fc1 = Collect(where, *fc1_terms(where, second_in, after(grad_pre, *seen), chips))
        sum_fc1.pair()
        seen = (sum_fc1.give,)
    else:
        part_fc1 = [dot(second_in, part, ROW_DIMS) for part in jnp.split(grad_pre, 4, axis=1)]
        part_fc1 = jnp.stack(part_fc1).reshape(4, frame_count, shard_rows, -1)
    grad_middle, grad_attn, grad_mixed, sums_mlp = fc1_back_call(
        after(grad_pre, *seen), full_fc1, middle, attn_out, grad_rows, hot, mod, full_attn, frames
    )
    seen = ()
    if square:
        seen = (*sum_fc2.far(grad_mixed), *sum_fc1.near(grad_mixed))
    grad_proj = attend_back(
        projected, after(grad_mixed, *seen), positions, frames, attn_scale
    )
    block_out = to_frames(block_rows, grad_proj)
    seen = ()
    if square:
        seen = (*sum_fc2.line(grad_proj), block_out)
    token_rows, sums_attn = qkv_back_call(
        after(grad_proj, *seen), full_attn, x_rows, grad_middle, hot, mod, positions, frames
    )
    if square:
        seen = (token_rows, sum_fc2.own, *sum_fc1.far(token_rows))
        sum_attn = Collect(
            where, *attn_terms(where, first_in, after(grad_proj, *seen), mixed, grad_attn, chips)
        )
        sum_attn.pair()
        sum_fc1.line(sum_attn.give)
        sum_attn.near()
        sum_attn.far()
        seen = sum_attn.line(sum_fc1.own)
        last = (sum_attn.own,)
        grad_tokens = to_frames(token_rows, *seen)
        sum_fc2, sum_fc1, sum_attn = sum_fc2.finish(*seen), sum_fc1.finish(*seen), sum_attn.finish()
    else:
        grad_tokens = to_frames(token_rows)
        part_attn = [dot(first_in, part, ROW_DIMS) for part in jnp.split(grad_proj, 3, axis=1)]
        part_attn = jnp.stack([*part_attn, dot(mixed, grad_attn, ROW_DIMS)])
        part_attn = part_attn.reshape(4, frame_count, shard_rows, width)
        seen, last = (), ()
        sum_fc2, sum_fc1, sum_attn = sum_plain(part_fc2), sum_plain(part_fc1), sum_plain(part_attn)
    part_mod = jnp.concatenate([sums_attn, sums_mlp, sum_gate_mlp[None]], axis=0)[:, :clips]
    part_mod = part_mod.transpose(1, 0, 2).reshape(clips, frame_count, ada_cols)
    part_small = jnp.concatenate(
        [
            jnp.pad(part_mod, ((0, 0), (0, 0), (0, small_cols - ada_cols))),
            jnp.pad(
                part_bias.reshape(1, frame_count, bias_cols),
                ((0, small_rows - clips - 1), (0, 0), (0, small_cols - bias_cols)),
            ),
        ],
        axis=0,
    ).astype(BF16)
    small_terms = lax.all_to_all(after(part_small, *seen).transpose(1, 0, 2), "frame", 0, 0, tiled=False)
    small_terms = after(small_terms, *last)
    small_sum = sum_items(jnp.sum(small_terms.astype(F32), axis=0))
    grad_modulation = small_sum[:clips, :ada_cols]
    sum_bias = small_sum[clips, :bias_cols]
    grad_b_ada = jnp.sum(grad_modulation, axis=0)
    high = grad_modulation.astype(BF16)
    low = (grad_modulation - high.astype(F32)).astype(BF16)
    act_part = (dot(high, w_ada, COL_DIMS) + dot(low, w_ada, COL_DIMS)).astype(BF16)
    grad_w_ada = lax.dot_general(
        activated, after(grad_modulation, act_part), ROW_DIMS, precision=HIGHEST
    )
    grad_activated = jnp.sum(share_small(act_part).astype(F32), axis=0)
    _, silu_back = jax.vjp(jax.nn.silu, condition)
    grad_condition = silu_back(grad_activated)[0]
    grad_table = lax.dot_general(class_hot, grad_condition, ROW_DIMS, precision=HIGHEST)
    return (
        block_out,
        grad_tokens,
        by_column_quarter(sum_attn)[:, : 3 * width].astype(F32),
        sum_attn[3].astype(F32),
        by_column_quarter(sum_fc1).astype(F32),
        sum_bias,
        sum_fc2.reshape(-1, width).astype(F32),
        grad_w_ada,
        grad_b_ada,
        grad_table,
    )


def solution(mesh):
    return jax.shard_map(
        body,
        mesh=mesh,
        in_specs=(
            P("item", "frame", None, None),
            P("item", "frame", None, None),
            P(),
            P(),
            P(),
            P(),
            P("frame", None),
            P("frame", None),
            P("frame", None),
            P("frame"),
            P("frame", None),
            P(None, "frame"),
            P("frame"),
            P(),
        ),
        out_specs=(
            P("item", "frame", None, None),
            P("item", "frame", None, None),
            P("frame", None),
            P("frame", None),
            P("frame", None),
            P("frame"),
            P("frame", None),
            P(None, "frame"),
            P("frame"),
            P(),
        ),
        check_vma=False,
    )
```

```python
import math

import jax
import jax.numpy as jnp
from jax import lax
from jax.experimental import pallas as pl
from jax.experimental.pallas import tpu as pltpu
from jax.sharding import PartitionSpec as P

D = 1152
HEADS = 16
CLASSES = 101


HIGHEST = lax.Precision.HIGHEST
ROW_DIMS = (((0,), (0,)), ((), ()))
COL_DIMS = (((1,), (1,)), ((), ()))


def layer_norm(values):
    center = values - jnp.mean(values, axis=-1, keepdims=True)
    return center * lax.rsqrt(jnp.mean(center * center, axis=-1, keepdims=True) + 1e-06)


def time_features(timesteps):
    half_width = D // 2
    frequency = jnp.exp(-math.log(10000.0) * jnp.arange(half_width, dtype=jnp.float32) / half_width)
    angles = timesteps.astype(jnp.float32)[:, None] * frequency[None, :]
    return jnp.concatenate([jnp.cos(angles), jnp.sin(angles)], axis=1)


def row_items(patch_counts, assignment, group_idx, total):
    numbers = jnp.arange(patch_counts.shape[0], dtype=jnp.int32)
    same_group = assignment[None, :] == assignment[:, None]
    earlier = numbers[None, :] < numbers[:, None]
    offsets = jnp.sum(jnp.where(same_group & earlier, patch_counts[None, :], 0), axis=1)
    row_ids = jnp.arange(total, dtype=jnp.int32)[:, None]
    inside = (
        (assignment[None, :] == group_idx)
        & (row_ids >= offsets[None, :])
        & (row_ids < offsets[None, :] + patch_counts[None, :])
    )
    return inside.astype(jnp.float32)


def gelu_tanh(pre_vals):
    return jax.nn.gelu(pre_vals, approximate=True)

LANES = 128


def pair_windows(heads, head_dim):
    windows = []
    for head in range(0, heads, 2):
        low, high = head * head_dim, (head + 2) * head_dim
        start, end = low // LANES * LANES, -(-high // LANES) * LANES
        windows.append((start, end, low, low + head_dim, high))
    return windows


def stacked(value, window):
    start, end, first, second, last = window
    lanes = start + lax.broadcasted_iota(jnp.int32, (1, end - start), 1)
    masks = [
        ((lanes >= low) & (lanes < high)).astype(jnp.float32).astype(jnp.bfloat16)
        for low, high in ((first, second), (second, last))
    ]
    return jnp.concatenate([value * mask for mask in masks], axis=0)


def tall(wide):
    half = wide.shape[1] // 2
    return jnp.concatenate([wide[:, :half], wide[:, half:]], axis=0)


def add_window(totals, window, value):
    start, end = window[:2]
    for lane in range(start, end, LANES):
        piece = value[:, lane - start : lane - start + LANES]
        totals[lane] = piece if lane not in totals else totals[lane] + piece


def joined(totals):
    return jnp.concatenate([totals[lane] for lane in sorted(totals)], axis=1)


class Spots:
    def __init__(self, rows, frames):
        self.frames, count = frames, rows // frames
        spot = lax.broadcasted_iota(jnp.int32, (frames, 2 * rows), 1) // frames % count
        self.own = [spot == at for at in range(count)]
        self.masks = [own.astype(jnp.float32).astype(jnp.bfloat16) for own in self.own]

    def compact(self, full):
        found = full[: self.frames]
        for at, own in enumerate(self.own[1:], 1):
            found = jnp.where(own, full[at * self.frames : (at + 1) * self.frames], found)
        return found

    def expand(self, compact):
        return jnp.concatenate([compact * mask for mask in self.masks], axis=0)

    def blocks(self, pairs):
        return jnp.concatenate(
            [
                self.compact(
                    lax.dot_general(left, right, COL_DIMS, preferred_element_type=jnp.float32)
                )
                for left, right in pairs
            ],
            axis=1,
        )

    def probs(self, pairs, scale):
        scores = self.blocks(pairs) * scale
        weights = jnp.exp(scores - jnp.max(scores, axis=0, keepdims=True))
        return weights / jnp.sum(weights, axis=0, keepdims=True)


def attend_kernel(frames, scale, proj_ref, mixed_ref):
    rows, width = mixed_ref.shape
    spots = Spots(rows, frames)
    windows = pair_windows(HEADS, width // HEADS)

    def part(index, window):
        return proj_ref[:, index * width + window[0] : index * width + window[1]]

    prob = spots.probs(
        [(part(1, window), stacked(part(0, window), window)) for window in windows], scale
    ).astype(jnp.bfloat16)
    totals = {}
    for at, window in enumerate(windows):
        wide = spots.expand(prob[:, at * 2 * rows : (at + 1) * 2 * rows])
        add_window(
            totals,
            window,
            lax.dot_general(
                tall(wide),
                stacked(part(2, window), window),
                ROW_DIMS,
                preferred_element_type=jnp.float32,
            ),
        )
    mixed_ref[...] = joined(totals).astype(jnp.bfloat16)


def attend_back_kernel(frames, scale, proj_ref, grad_ref, out_ref):
    rows, width = grad_ref.shape
    spots = Spots(rows, frames)
    windows = pair_windows(HEADS, width // HEADS)

    def part(index, window):
        return proj_ref[:, index * width + window[0] : index * width + window[1]]

    def grads(window):
        return stacked(grad_ref[:, window[0] : window[1]], window)

    prob = spots.probs(
        [(part(1, window), stacked(part(0, window), window)) for window in windows], scale
    )
    grad_prob = spots.blocks([(part(2, window), grads(window)) for window in windows])
    weighted = prob * grad_prob
    grad_scores = weighted - prob * jnp.sum(weighted, axis=0, keepdims=True)
    grad_scores, prob = grad_scores.astype(jnp.bfloat16), prob.astype(jnp.bfloat16)
    to_query, to_key, to_value = {}, {}, {}
    for at, window in enumerate(windows):
        span = slice(at * 2 * rows, (at + 1) * 2 * rows)
        wide = spots.expand(grad_scores[:, span])
        add_window(
            to_value,
            window,
            jnp.dot(
                spots.expand(prob[:, span]), grads(window), preferred_element_type=jnp.float32
            ),
        )
        add_window(
            to_key,
            window,
            jnp.dot(
                wide, stacked(part(0, window), window), preferred_element_type=jnp.float32
            ),
        )
        add_window(
            to_query,
            window,
            lax.dot_general(
                tall(wide),
                stacked(part(1, window), window),
                ROW_DIMS,
                preferred_element_type=jnp.float32,
            ),
        )
    out_ref[:, :width] = (joined(to_query) * scale).astype(jnp.bfloat16)
    out_ref[:, width : 2 * width] = (joined(to_key) * scale).astype(jnp.bfloat16)
    out_ref[:, 2 * width :] = joined(to_value).astype(jnp.bfloat16)


def tile_rows(positions, frames):
    for count in (8, 4, 2):
        if positions % count == 0:
            return count * frames
    return frames


def attend(projected, positions, frames, scale):
    rows, width = projected.shape[0], projected.shape[1] // 3
    tile = tile_rows(positions, frames)
    return pl.pallas_call(
        lambda *refs: attend_kernel(frames, scale, *refs),
        out_shape=jax.ShapeDtypeStruct((rows, width), jnp.bfloat16),
        grid=(rows // tile,),
        in_specs=[pl.BlockSpec((tile, 3 * width), lambda step: (step, 0))],
        out_specs=pl.BlockSpec((tile, width), lambda step: (step, 0)),
        cost_estimate=pl.CostEstimate(
            flops=9 * 10**9, bytes_accessed=8 * rows * width, transcendentals=0
        ),
        compiler_params=pltpu.CompilerParams(vmem_limit_bytes=VMEM_LIMIT),
        name="attend",
    )(projected)


def attend_back(projected, grad_mixed, positions, frames, scale):
    rows, width = projected.shape[0], projected.shape[1] // 3
    tile = tile_rows(positions, frames)
    return pl.pallas_call(
        lambda *refs: attend_back_kernel(frames, scale, *refs),
        out_shape=jax.ShapeDtypeStruct((rows, 3 * width), jnp.bfloat16),
        grid=(rows // tile,),
        in_specs=[
            pl.BlockSpec((tile, 3 * width), lambda step: (step, 0)),
            pl.BlockSpec((tile, width), lambda step: (step, 0)),
        ],
        out_specs=pl.BlockSpec((tile, 3 * width), lambda step: (step, 0)),
        cost_estimate=pl.CostEstimate(
            flops=12 * 10**9, bytes_accessed=14 * rows * width, transcendentals=0
        ),
        compiler_params=pltpu.CompilerParams(vmem_limit_bytes=VMEM_LIMIT),
        name="attend_back",
    )(projected, grad_mixed)


VMEM_LIMIT = 58 << 20
BF16, F32 = jnp.bfloat16, jnp.float32


def row_tile(rows):
    for tile in (224, 128, 112, 64, 32, 16):
        if rows % tile == 0:
            return tile
    return rows


def dot(left, right, dims=(((1,), (0,)), ((), ()))):
    return lax.dot_general(left, right, dims, preferred_element_type=F32)


def call(kernel, name, grid, ins, outs, scratch=(), flops=0, vmem=VMEM_LIMIT):
    moved = sum(array.size * array.dtype.itemsize for array, _ in ins)
    moved += sum(math.prod(shape) * jnp.dtype(dtype).itemsize for shape, dtype, _ in outs)
    return pl.pallas_call(
        kernel,
        out_shape=[jax.ShapeDtypeStruct(shape, dtype) for shape, dtype, _ in outs],
        grid=grid,
        in_specs=[spec for _, spec in ins],
        out_specs=[spec for _, _, spec in outs],
        scratch_shapes=list(scratch),
        cost_estimate=pl.CostEstimate(flops=flops, bytes_accessed=moved, transcendentals=0),
        compiler_params=pltpu.CompilerParams(vmem_limit_bytes=vmem),
        name=name,
    )(*[array for array, _ in ins])


HBM = pl.BlockSpec(memory_space=pl.ANY)
SCALARS = pl.BlockSpec(memory_space=pltpu.SMEM)


def whole(array):
    return pl.BlockSpec(array.shape, lambda step: (0,) * array.ndim)


def tiled(tile, width):
    return pl.BlockSpec((tile, width), lambda step: (step, 0))


class Pieces:
    def __init__(self, arrays, places, shape, by_columns, flipped):
        self.arrays, self.places, self.shape = arrays, places, shape
        self.by_columns, self.flipped = by_columns, flipped

    def quarter(self, where_ref, turn):
        return where_ref[0] ^ turn if self.flipped else turn

    def columns(self, slot):
        width = self.shape[1] // 4
        return pl.ds(pl.multiple_of(slot * width, width), width)

    def start(self, where_ref, refs, full, sems):
        for ref, place in zip(refs, self.places):
            slot, first, count = place(where_ref[0], where_ref[1])
            if self.by_columns:
                target = full.at[pl.ds(first, count), self.columns(slot)]
                pltpu.make_async_copy(ref, target, sems.at[slot]).start()
                continue
            for turn in range(count):
                target = full.at[first + turn, slot]
                sem = sems.at[(first + turn) // (self.shape[0] // 4)]
                pltpu.make_async_copy(ref.at[turn], target, sem).start()

    def part(self, full, at):
        if self.by_columns:
            return full.at[:, self.columns(at)]
        turns = self.shape[0] // 4
        return full.at[at * turns : (at + 1) * turns]

    def wait(self, at, full, sems):
        part = self.part(full, at)
        pltpu.make_async_copy(part, part, sems.at[at]).wait()

    def scratch(self):
        return [pltpu.VMEM(self.shape, BF16), pltpu.SemaphoreType.DMA((5,))]


def norm_parts(values):
    center = values - jnp.mean(values, axis=1, keepdims=True)
    inverse = lax.rsqrt(jnp.mean(center * center, axis=1, keepdims=True) + 1e-06)
    return center * inverse, inverse


def norm_back(normed, inverse, grad):
    mean_grad = jnp.mean(grad, axis=1, keepdims=True)
    mean_both = jnp.mean(grad * normed, axis=1, keepdims=True)
    return (grad - mean_grad - normed * mean_both) * inverse


def gather_order(first, count, frames, positions, own_frames, chunk):
    at = first + lax.broadcasted_iota(jnp.int32, (count, 1), 0)
    source = lax.broadcasted_iota(jnp.int32, (1, frames // own_frames * chunk), 1)
    frame, position = at % frames, at // frames
    wanted = frame // own_frames * chunk + frame % own_frames * positions + position
    return (source == wanted).astype(F32).astype(BF16)


def row_order(rows, first, count, inner, outer):
    at = first + lax.broadcasted_iota(jnp.int32, (count, 1), 0)
    source = lax.broadcasted_iota(jnp.int32, (1, rows), 1)
    return (source == (at % outer) * inner + at // outer).astype(F32).astype(BF16)


def clip_sums(hot, values):
    high = values.astype(BF16)
    low = (values - high.astype(F32)).astype(BF16)
    return dot(hot, high, ROW_DIMS) + dot(hot, low, ROW_DIMS)


def by_tile(my_rows, mod, frames):
    count = row_tile(my_rows.shape[0] * frames) // frames
    tiles = my_rows.astype(BF16).reshape(-1, count, my_rows.shape[1])
    tiles = jnp.pad(tiles, ((0, 0), (0, -count % 8), (0, 0)))
    return lax.dot_general(tiles, mod, (((2,), (0,)), ((), ())), preferred_element_type=F32)


def tile_mod(mod):
    return pl.BlockSpec((1, *mod.shape[1:]), lambda step: (step, 0, 0))


def spread_rows(mod_ref, part, count, frames):
    width = mod_ref.shape[2] // 6
    cols = slice(part * width, (part + 1) * width)
    rows = [
        jnp.broadcast_to(mod_ref[0, at : at + 1, cols], (frames, width)) for at in range(count)
    ]
    return jnp.concatenate(rows, axis=0)


def first_step(step, action):
    @pl.when(step == 0)
    def _():
        action()


def add_into(ref, index, value):
    @pl.when(pl.program_id(0) == 0)
    def _():
        ref[index] = jnp.zeros_like(ref[index])

    ref[index] += value


def qkv_call(where, arrived, mod, pieces, positions, frames, own_frames):
    rows, width = positions * frames, arrived.shape[1]
    chunk = arrived.shape[0] * own_frames // frames
    tile = row_tile(rows)
    steps = rows // tile
    count = len(pieces.arrays)

    def kernel(where_ref, x_ref, mod_ref, *rest):
        piece_refs, rest = rest[:count], rest[count:]
        x_out, first_out, proj_out, full_out, full, sems = rest
        step = pl.program_id(0)

        @pl.when(step == 0)
        def _():
            pieces.start(where_ref, piece_refs, full, sems)

        order = gather_order(step * tile, tile, frames, positions, own_frames, chunk)
        inputs = dot(order, x_ref[...])
        x_out[...] = inputs.astype(BF16)
        normed, _ = norm_parts(inputs)
        shift = spread_rows(mod_ref, 0, tile // frames, frames)
        scale = spread_rows(mod_ref, 1, tile // frames, frames)
        first = (normed * (1.0 + scale) + shift).astype(BF16)
        first_out[...] = first
        back = pltpu.make_async_copy(full, full_out, sems.at[4])

        @pl.when(step == 0)
        def _():
            for turn in range(4):
                slot = pieces.quarter(where_ref, turn)
                pieces.wait(slot, full, sems)

                @pl.when(slot < 3)
                def _():
                    weight = pieces.part(full, slot)[...]
                    proj_out[:, pieces.columns(slot)] = dot(first, weight).astype(BF16)

            back.start()

        @pl.when(step > 0)
        def _():
            proj_out[...] = dot(first, full[:, : 3 * width]).astype(BF16)

        @pl.when(step == steps - 1)
        def _():
            back.wait()

    return call(
        kernel,
        "project",
        (steps,),
        [
            (where, SCALARS),
            (arrived, whole(arrived)),
            (mod, tile_mod(mod)),
            *[(array, HBM) for array in pieces.arrays],
        ],
        [
            ((rows, width), BF16, tiled(tile, width)),
            ((rows, width), BF16, tiled(tile, width)),
            ((rows, 3 * width), BF16, tiled(tile, 3 * width)),
            (pieces.shape, BF16, HBM),
        ],
        pieces.scratch(),
        flops=20 * 10**9,
    )


def out_call(mixed, x_rows, mod, full_attn, frames):
    rows, width = mixed.shape
    tile = row_tile(rows)

    def kernel(mixed_ref, x_ref, mod_ref, w_ref, attn_out, middle_out, second_out):
        attn = dot(mixed_ref[...], w_ref[...])
        shift, scale, gate = [
            spread_rows(mod_ref, part, tile // frames, frames)
            for part in (3, 4, 2)
        ]
        middle = x_ref[...].astype(F32) + gate * attn
        normed, _ = norm_parts(middle)
        attn_out[...] = attn.astype(BF16)
        middle_out[...] = middle
        second_out[...] = (normed * (1.0 + scale) + shift).astype(BF16)

    return call(
        kernel,
        "attn_out",
        (rows // tile,),
        [
            (mixed, tiled(tile, width)),
            (x_rows, tiled(tile, width)),
            (mod, tile_mod(mod)),
            (full_attn, pl.BlockSpec((width, width), lambda step: (0, 3))),
        ],
        [
            ((rows, width), BF16, tiled(tile, width)),
            ((rows, width), F32, tiled(tile, width)),
            ((rows, width), BF16, tiled(tile, width)),
        ],
        flops=9 * 10**9,
    )


GELU_A = math.sqrt(2.0 / math.pi)
GELU_B = GELU_A * 0.044715


def fc1_call(where, second_in, bias, pieces):
    rows, width = second_in.shape
    tile = row_tile(rows)
    steps = rows // tile
    count = len(pieces.arrays)
    part = pieces.shape[1] // 4

    def kernel(where_ref, x_ref, bias_ref, *rest):
        piece_refs, rest = rest[:count], rest[count:]
        post_out, slope_out, full_out, full, sems = rest
        step = pl.program_id(0)
        back = pltpu.make_async_copy(full, full_out, sems.at[4])

        def run(cols):
            pre = dot(x_ref[...], full[:, cols]) + bias_ref[:, cols].astype(F32)
            square = pre * pre
            curve = jnp.tanh(pre * (GELU_A + GELU_B * square))
            half = 0.5 + 0.5 * curve
            post_out[:, cols] = (pre * half).astype(BF16)
            rise = (0.5 * pre) * (1.0 - curve * curve)
            slope_out[:, cols] = (half + rise * (GELU_A + 3.0 * GELU_B * square)).astype(BF16)

        @pl.when(step == 0)
        def _():
            pieces.start(where_ref, piece_refs, full, sems)
            for turn in range(4):
                slot = pieces.quarter(where_ref, turn)
                pieces.wait(slot, full, sems)
                run(pieces.columns(slot))
            back.start()

        @pl.when(step > 0)
        def _():
            for half in range(2):
                run(slice(half * 2 * part, (half + 1) * 2 * part))

        @pl.when(step == steps - 1)
        def _():
            back.wait()

    return call(
        kernel,
        "fc1",
        (steps,),
        [
            (where, SCALARS),
            (second_in, tiled(tile, width)),
            (bias, whole(bias)),
            *[(array, HBM) for array in pieces.arrays],
        ],
        [
            ((rows, 4 * part), BF16, tiled(tile, 4 * part)),
            ((rows, 4 * part), BF16, tiled(tile, 4 * part)),
            (pieces.shape, BF16, HBM),
        ],
        pieces.scratch(),
        flops=25 * 10**9,
    )


def cot_call(arrived, hot, mod, positions, frames, own_frames):
    rows, width = arrived.shape
    tile = row_tile(rows)

    def kernel(cot_ref, hot_ref, mod_ref, rows_out, mlp_out):
        first = pl.program_id(0) * tile
        order = gather_order(first, tile, frames, positions, own_frames, own_frames * positions)
        hot = hot_ref[...]
        valid = jnp.sum(hot.astype(F32), axis=1, keepdims=True)
        grad = dot(order, cot_ref[...]) * valid
        rows_out[...] = grad.astype(BF16)
        mlp_out[...] = (grad * spread_rows(mod_ref, 5, tile // frames, frames)).astype(BF16)

    return call(
        kernel,
        "cotangent",
        (rows // tile,),
        [
            (arrived, whole(arrived)),
            (hot, tiled(tile, hot.shape[1])),
            (mod, tile_mod(mod)),
        ],
        [
            ((rows, width), BF16, tiled(tile, width)),
            ((rows, width), BF16, tiled(tile, width)),
        ],
        flops=6 * 10**9,
    )


def fc2_call(where, post_act, slope, grad_mlp, grad_rows, middle, hot, mod, pieces, positions, frames):
    rows, hidden = post_act.shape
    width = grad_mlp.shape[1]
    tile = row_tile(rows)
    steps = rows // tile
    count = len(pieces.arrays)
    clips = hot.shape[1]

    def kernel(where_ref, post_ref, slope_ref, gmlp_ref, grows_ref, mid_ref, hot_ref, mod_ref, *rest):
        piece_refs, rest = rest[:count], rest[count:]
        block_out, pre_out, bias_out, gate_out, full, sems, held, sums = rest
        step = pl.program_id(0)

        def run(first, last):
            part = hidden // 4
            cols = slice(first * part, last * part)
            turns = pieces.shape[0] // 4
            weight = full[first * turns : last * turns].reshape((last - first) * part, width)
            term = dot(post_ref[:, cols], weight)
            sums[...] = term if not first else sums[...] + term
            grad_pre = dot(gmlp_ref[...], weight, COL_DIMS) * slope_ref[:, cols].astype(F32)
            grad_pre = grad_pre.astype(BF16)
            pre_out[:, cols] = grad_pre
            total = jnp.sum(grad_pre.astype(F32), axis=0, keepdims=True)
            add_into(bias_out, (slice(None), cols), total)

        @pl.when(step == 0)
        def _():
            pieces.start(where_ref, piece_refs, full, sems)
            for at in range(4):
                pieces.wait(at, full, sems)
                run(at, at + 1)

        @pl.when(step > 0)
        def _():
            run(0, 2)
            run(2, 4)

        total = sums[...]
        hot = hot_ref[...]
        valid = jnp.sum(hot.astype(F32), axis=1, keepdims=True)
        gate = spread_rows(mod_ref, 5, tile // frames, frames)
        result = valid * (mid_ref[...] + gate * total)
        held[pl.ds(pl.multiple_of(step * tile, 16), tile), :] = result.astype(BF16)
        add_into(gate_out, slice(None), clip_sums(hot, grows_ref[...].astype(F32) * total))

        @pl.when(step == steps - 1)
        def _():
            for at in range(steps):
                order = row_order(rows, at * tile, tile, frames, positions)
                block_out[at * tile : (at + 1) * tile, :] = dot(order, held[...]).astype(BF16)

    return call(
        kernel,
        "fc2",
        (steps,),
        [
            (where, SCALARS),
            (post_act, tiled(tile, hidden)),
            (slope, tiled(tile, hidden)),
            (grad_mlp, tiled(tile, width)),
            (grad_rows, tiled(tile, width)),
            (middle, tiled(tile, width)),
            (hot, tiled(tile, clips)),
            (mod, tile_mod(mod)),
            *[(array, HBM) for array in pieces.arrays],
        ],
        [
            ((rows, width), BF16, pl.BlockSpec((rows, width), lambda step: (0, 0))),
            ((rows, hidden), BF16, tiled(tile, hidden)),
            ((1, hidden), F32, pl.BlockSpec((1, hidden), lambda step: (0, 0))),
            ((clips, width), F32, pl.BlockSpec((clips, width), lambda step: (0, 0))),
        ],
        [*pieces.scratch(), pltpu.VMEM((rows, width), BF16), pltpu.VMEM((tile, width), F32)],
        flops=44 * 10**9,
    )


def load_and_dot(step, left_ref, w_ref, held, sems, total, parts):
    width = left_ref.shape[1] // parts
    runs = [slice(at * width, (at + 1) * width) for at in range(parts)]
    loads = [
        pltpu.make_async_copy(w_ref.at[:, run], held.at[:, run], sems.at[at])
        for at, run in enumerate(runs)
    ]

    @pl.when(step == 0)
    def _():
        for load in loads:
            load.start()
        for at, load in enumerate(loads):
            load.wait()
            term = dot(left_ref[:, runs[at]], held[:, runs[at]], COL_DIMS)
            total[...] = term if not at else total[...] + term

    @pl.when(step > 0)
    def _():
        total[...] = dot(left_ref[...], held[...], COL_DIMS)

    return total[...]


def fc1_back_call(grad_pre, full_fc1, middle, attn_out, grad_rows, hot, mod, full_attn, frames):
    rows, hidden = grad_pre.shape
    width = middle.shape[1]
    tile = row_tile(rows)
    clips = hot.shape[1]

    def kernel(pre_ref, w_ref, mid_ref, attn_ref, grows_ref, hot_ref, mod_ref, wo_ref, *outs):
        gmid_out, gattn_out, gmix_out, sums_out, held, sems, total = outs
        step = pl.program_id(0)
        grad = load_and_dot(step, pre_ref, w_ref, held, sems, total, 4)
        hot = hot_ref[...]
        scale = spread_rows(mod_ref, 4, tile // frames, frames)
        gate = spread_rows(mod_ref, 2, tile // frames, frames)
        normed, inverse = norm_parts(mid_ref[...])
        grad_middle = grows_ref[...].astype(F32) + norm_back(normed, inverse, grad * (1.0 + scale))
        gmid_out[...] = grad_middle
        grad_attn = (grad_middle * gate).astype(BF16)
        gattn_out[...] = grad_attn
        gmix_out[...] = dot(grad_attn, wo_ref[...], COL_DIMS).astype(BF16)
        add_into(sums_out, 0, clip_sums(hot, grad_middle * attn_ref[...].astype(F32)))
        add_into(sums_out, 1, clip_sums(hot, grad))
        add_into(sums_out, 2, clip_sums(hot, grad * normed))

    return call(
        kernel,
        "fc1_back",
        (rows // tile,),
        [
            (grad_pre, tiled(tile, hidden)),
            (full_fc1, HBM),
            (middle, tiled(tile, width)),
            (attn_out, tiled(tile, width)),
            (grad_rows, tiled(tile, width)),
            (hot, tiled(tile, clips)),
            (mod, tile_mod(mod)),
            (full_attn, pl.BlockSpec((width, width), lambda step: (0, 3))),
        ],
        [
            ((rows, width), F32, tiled(tile, width)),
            ((rows, width), BF16, tiled(tile, width)),
            ((rows, width), BF16, tiled(tile, width)),
            ((3, clips, width), F32, pl.BlockSpec((3, clips, width), lambda step: (0, 0, 0))),
        ],
        [
            pltpu.VMEM(full_fc1.shape, BF16),
            pltpu.SemaphoreType.DMA((4,)),
            pltpu.VMEM((tile, width), F32),
        ],
        flops=32 * 10**9,
    )


def qkv_back_call(grad_proj, full_attn, x_rows, grad_middle, hot, mod, positions, frames):
    rows, width = x_rows.shape
    tile = row_tile(rows)
    steps = rows // tile
    clips = hot.shape[1]

    def kernel(proj_ref, w_ref, x_ref, gmid_ref, hot_ref, mod_ref, tok_out, sums_out, held, w_held, sems, total):
        step = pl.program_id(0)
        grad = load_and_dot(step, proj_ref, w_ref, w_held, sems, total, 3)
        hot = hot_ref[...]
        scale = spread_rows(mod_ref, 1, tile // frames, frames)
        normed, inverse = norm_parts(x_ref[...].astype(F32))
        result = gmid_ref[...] + norm_back(normed, inverse, grad * (1.0 + scale))
        held[pl.ds(pl.multiple_of(step * tile, 16), tile), :] = result.astype(BF16)
        add_into(sums_out, 0, clip_sums(hot, grad))
        add_into(sums_out, 1, clip_sums(hot, grad * normed))

        @pl.when(step == steps - 1)
        def _():
            for at in range(steps):
                order = row_order(rows, at * tile, tile, frames, positions)
                tok_out[at * tile : (at + 1) * tile, :] = dot(order, held[...]).astype(BF16)

    return call(
        kernel,
        "project_back",
        (steps,),
        [
            (grad_proj, tiled(tile, 3 * width)),
            (full_attn, HBM),
            (x_rows, tiled(tile, width)),
            (grad_middle, tiled(tile, width)),
            (hot, tiled(tile, clips)),
            (mod, tile_mod(mod)),
        ],
        [
            ((rows, width), BF16, pl.BlockSpec((rows, width), lambda step: (0, 0))),
            ((2, clips, width), F32, pl.BlockSpec((2, clips, width), lambda step: (0, 0, 0))),
        ],
        [
            pltpu.VMEM((rows, width), BF16),
            pltpu.VMEM((width, 3 * width), BF16),
            pltpu.SemaphoreType.DMA((3,)),
            pltpu.VMEM((tile, width), F32),
        ],
        flops=23 * 10**9,
    )


def split_store(product, where_ref, keep_out, give_out, rows, slot_first, slot=0):
    units = product.shape[0] // rows
    for core in range(2):

        @pl.when(where_ref[1] == core)
        def _():
            for unit in range(units):
                piece = product[unit * rows : (unit + 1) * rows]
                side = unit % 2 if slot_first else unit // 4
                out = keep_out if side == core else give_out
                if slot_first:
                    out[slot, unit // 2] = piece
                else:
                    out[unit % 4, 0] = piece


def terms_out(chips, rows, width, slot_first, slots=1):
    if slot_first:
        spec = pl.BlockSpec((slots, chips, rows, width), lambda step: (step, 0, 0, 0))
    else:
        spec = pl.BlockSpec((4, 1, rows, width), lambda step: (0, step, 0, 0))
    return [((4, chips, rows, width), BF16, spec)] * 2


def fc2_terms(where, post_act, grad_mlp, chips):
    count, hidden = post_act.shape
    width = grad_mlp.shape[1]
    block, rows = hidden // chips, hidden // chips // 8

    def kernel(where_ref, left_ref, right_ref, keep_out, give_out):
        product = dot(left_ref[...], right_ref[...], ROW_DIMS).astype(BF16)
        split_store(product, where_ref, keep_out, give_out, rows, False)

    return call(
        kernel,
        "fc2_terms",
        (chips,),
        [
            (where, SCALARS),
            (post_act, pl.BlockSpec((count, block), lambda step: (0, step))),
            (grad_mlp, whole(grad_mlp)),
        ],
        terms_out(chips, rows, width, False),
        flops=18 * 10**9,
    )


def fc1_terms(where, second_in, grad_pre, chips):
    count, hidden = grad_pre.shape
    width = second_in.shape[1]
    rows, part = width // chips // 2, hidden // 4

    def kernel(where_ref, left_ref, right_ref, keep_out, give_out):
        product = dot(left_ref[...], right_ref[...], ROW_DIMS).astype(BF16)
        for slot in range(2):
            piece = product[:, slot * part : (slot + 1) * part]
            split_store(piece, where_ref, keep_out, give_out, rows, True, slot)

    return call(
        kernel,
        "fc1_terms",
        (2,),
        [
            (where, SCALARS),
            (second_in, whole(second_in)),
            (grad_pre, pl.BlockSpec((count, 2 * part), lambda step: (0, step))),
        ],
        terms_out(chips, rows, part, True, 2),
        flops=18 * 10**9,
    )


def attn_terms(where, first_in, grad_proj, mixed, grad_attn, chips):
    count, width = first_in.shape
    rows = width // chips // 2

    def kernel(where_ref, first_ref, proj_ref, mixed_ref, attn_ref, keep_out, give_out):
        step = pl.program_id(0)

        @pl.when(step < 3)
        def _():
            product = dot(first_ref[...], proj_ref[...], ROW_DIMS).astype(BF16)
            split_store(product, where_ref, keep_out, give_out, rows, True)

        @pl.when(step == 3)
        def _():
            product = dot(mixed_ref[...], attn_ref[...], ROW_DIMS).astype(BF16)
            split_store(product, where_ref, keep_out, give_out, rows, True)

    return call(
        kernel,
        "attn_terms",
        (4,),
        [
            (where, SCALARS),
            (first_in, whole(first_in)),
            (
                grad_proj,
                pl.BlockSpec((count, width), lambda step: (0, jnp.minimum(step, 2))),
            ),
            (mixed, whole(mixed)),
            (grad_attn, whole(grad_attn)),
        ],
        terms_out(chips, rows, width, True),
        flops=19 * 10**9,
    )


def plane_terms(where, keep, got):
    _, chips, rows, width = keep.shape
    cut = chips // 2
    flips = (1, 3, 2, 0)

    def place(step, where_ref):
        flip = 0
        for at in range(4):
            flip = jnp.where(step == at, flips[at], flip)
        return where_ref[0] ^ flip, 0, 0, 0

    def kernel(where_ref, keep_ref, got_ref, x_out, y_out, stay_out):
        targets = {
            1: ((x_out, 0), (stay_out, 3)),
            3: ((x_out, 1), (y_out, 1)),
            2: ((stay_out, 1), (y_out, 0)),
            0: ((stay_out, 0), (stay_out, 2)),
        }
        for at, flip in enumerate(flips):

            @pl.when(pl.program_id(0) == at)
            def _(flip=flip):
                for half, (out, slot) in enumerate(targets[flip]):
                    span = slice(half * cut, half * cut + cut)
                    out[slot] = keep_ref[0, span] + got_ref[0, span]

    block = (1, chips, rows, width)
    shapes = [(2, cut, rows, width), (2, cut, rows, width), (4, cut, rows, width)]
    return pl.pallas_call(
        kernel,
        out_shape=[jax.ShapeDtypeStruct(shape, BF16) for shape in shapes],
        grid_spec=pltpu.PrefetchScalarGridSpec(
            num_scalar_prefetch=1,
            grid=(4,),
            in_specs=[pl.BlockSpec(block, place), pl.BlockSpec(block, place)],
            out_specs=[
                pl.BlockSpec(shape, lambda step, where_ref: (0, 0, 0, 0)) for shape in shapes
            ],
        ),
        cost_estimate=pl.CostEstimate(
            flops=7 * 10**9, bytes_accessed=6 * keep.size, transcendentals=0
        ),
        compiler_params=pltpu.CompilerParams(vmem_limit_bytes=VMEM_LIMIT),
        name="plane_terms",
    )(where, keep, got)


X_SWAP = [(0, 1), (1, 0), (2, 3), (3, 2)]
Y_SWAP = [(0, 2), (2, 0), (1, 3), (3, 1)]


def swap_x(value):
    return lax.ppermute(value, "item", X_SWAP)


def swap_y(value):
    return lax.ppermute(value, "item", Y_SWAP)


def swap_core(value):
    count = lax.axis_size("frame")
    return lax.ppermute(value, "frame", [(at, at ^ 1) for at in range(count)])


def is_square():
    return lax.axis_size("item") == 4 and lax.axis_size("frame") % 2 == 0


def after(value, *others):
    return lax.optimization_barrier((value, *others))[0]


def after2(values, *others):
    return lax.optimization_barrier((*values, *others))[: len(values)]


def pick(stack, index):
    return lax.dynamic_index_in_dim(stack, index, 0, keepdims=False)


def by_column_quarter(stack):
    return jnp.concatenate([stack[part] for part in range(4)], axis=1)


def gather_frame(parts):
    if not is_square():
        return lax.all_gather(parts, "frame", axis=1)
    return lax.all_gather(pick(parts, lax.axis_index("item")), "frame", axis=0)


class Spread:
    def __init__(self, gathered, slot_first):
        self.gathered, self.slot_first = gathered, slot_first
        self.square = is_square()

    def near(self, *wait_for):
        if not self.square:
            return ()
        self.gathered = after(self.gathered, *wait_for)
        half = self.gathered.shape[0] // 2
        core = lax.axis_index("frame") % 2
        own = lax.dynamic_slice_in_dim(self.gathered, core * half, half, 0)
        self.cut = half // 2
        self.from_x, self.from_y = swap_x(own), swap_y(own)
        return self.from_x, self.from_y

    def far(self, *wait_for):
        if not self.square:
            return ()
        from_x, from_y = after2((self.from_x, self.from_y), *wait_for)
        self.far_low, self.far_high = swap_y(from_x[: self.cut]), swap_x(from_y[self.cut :])
        self.core_x, self.core_y = swap_core(from_x), swap_core(from_y)
        return self.far_low, self.far_high

    def pieces(self):
        gathered, slot_first = self.gathered, self.slot_first
        if not self.square:
            _, count, rows, width = gathered.shape
            if slot_first:
                return Pieces(
                    [gathered[part].reshape(count * rows, width) for part in range(4)],
                    [lambda item, core, part=part: (part, 0, count * rows) for part in range(4)],
                    (count * rows, 4 * width),
                    True,
                    False,
                )
            return Pieces(
                [gathered[part] for part in range(4)],
                [lambda item, core, part=part: (part, 0, count) for part in range(4)],
                (count, 4, rows, width),
                False,
                False,
            )
        count, rows, width = gathered.shape
        half, cut = count // 2, self.cut
        far = [self.far_low, self.far_high]
        arrays = [gathered, self.from_x, self.from_y, *far, self.core_x, self.core_y]
        arrays += [swap_core(value) for value in far]
        unit = rows if slot_first else 1
        if slot_first:
            arrays = [array.reshape(-1, width) for array in arrays]
            shape = (count * rows, 4 * width)
        else:
            shape = (count, 4, rows, width)
        places = [lambda item, core: (item, 0, count * unit)]
        for flip in (0, 1):
            for slot, start, length in ((1, 0, half), (2, 0, half), (3, 0, cut), (3, cut, half - cut)):
                places.append(
                    lambda item, core, flip=flip, slot=slot, start=start, length=length: (
                        item ^ slot,
                        ((core ^ flip) * half + start) * unit,
                        length * unit,
                    )
                )
        order = (0, 1, 5, 2, 6, 3, 4, 7, 8)
        arrays, places = [arrays[at] for at in order], [places[at] for at in order]
        return Pieces(arrays, places, shape, slot_first, True)


class Collect:
    def __init__(self, where, keep, give):
        self.where, self.keep, self.give = where, keep, give
        self.item = lax.axis_index("item")

    def pair(self, *wait_for):
        self.give = after(self.give, *wait_for)
        self.got = swap_core(self.give)

    def near(self, *wait_for):
        got = after(self.got, *wait_for)
        x_out, y_out, self.stay = plane_terms(self.where, self.keep, got)
        self.x_in, self.y_in = swap_x(x_out), swap_y(y_out)
        return (self.stay,)

    def far(self, *wait_for):
        x_in, y_in = after2((self.x_in, self.y_in), *wait_for)
        low_on, high_on = self.stay[1] + x_in[1], self.stay[3] + y_in[1]
        self.low, self.high = self.stay[0] + x_in[0], self.stay[2] + y_in[0]
        self.y_far, self.x_far = swap_y(low_on), swap_x(high_on)
        return low_on, high_on

    def line(self, *wait_for):
        y_far, x_far = after2((self.y_far, self.x_far), *wait_for)
        plane = jnp.concatenate([self.low + y_far, self.high + x_far], axis=0)
        count = lax.axis_size("frame")
        groups = [list(range(side, count, 2)) for side in range(2)]
        self.own = lax.psum_scatter(
            plane, "frame", scatter_dimension=0, tiled=False, axis_index_groups=groups
        )
        return (plane,)

    def finish(self, *wait_for):
        own, item = after(self.own, *wait_for), self.item
        far = lax.ppermute(own, "item", [(at, at ^ 3) for at in range(4)])
        stack = jnp.stack([own, swap_x(own), swap_y(own), far])
        return jnp.stack([pick(stack, item ^ part) for part in range(4)])


def sum_plain(partial):
    share = lax.psum_scatter(partial.astype(BF16), "frame", scatter_dimension=1, tiled=False)
    return lax.psum(share, "item")


def share_small(value):
    count = lax.axis_size("frame")
    return lax.all_to_all(
        jnp.broadcast_to(value[None], (count, *value.shape)), "frame", 0, 0, tiled=False
    )


def sum_items(value):
    if not is_square():
        return lax.psum(value.astype(BF16), "item").astype(F32)
    low = value.astype(BF16)
    far = lax.ppermute(low, "item", [(at, at ^ 3) for at in range(4)])
    return value + swap_x(low).astype(F32) + swap_y(low).astype(F32) + far.astype(F32)


def round_up(number, unit):
    return -(-number // unit) * unit


def body(
    tokens,
    cotangent,
    patch_counts,
    assignment,
    timesteps,
    class_ids,
    w_qkv,
    w_out,
    w_fc1,
    b_fc1,
    w_fc2,
    w_ada,
    b_ada,
    class_table,
):
    frame_count = lax.axis_size("frame")
    group_idx = lax.axis_index("item")
    frame_pos = lax.axis_index("frame")
    _, own_frames, capacity, width = tokens.shape
    frames = own_frames * frame_count
    positions = capacity // frame_count
    rows = frames * positions
    clips = patch_counts.shape[0]
    attn_scale = 1.0 / math.sqrt(width // HEADS)
    where = jnp.stack([group_idx, frame_pos % 2, frame_pos]).astype(jnp.int32)

    def to_positions(value, *extra):
        chunks = value[0].reshape(own_frames, frame_count, positions, width).transpose(1, 0, 2, 3)
        chunks = chunks.reshape(frame_count, own_frames * positions, width)
        for more in extra:
            more = jnp.broadcast_to(more[None], (frame_count, *more.shape))
            chunks = jnp.concatenate([chunks, more], axis=1)
        return lax.all_to_all(chunks, "frame", 0, 0, tiled=True)

    def send_frames(value):
        chunks = value.reshape(frame_count, own_frames, positions, width)
        return lax.all_to_all(chunks, "frame", 0, 0, tiled=True)

    def to_frames(arrived, *wait_for):
        moved = after(arrived, *wait_for).transpose(1, 0, 2, 3)
        return moved.reshape(1, own_frames, capacity, width)

    layout = row_items(patch_counts, assignment, group_idx, capacity)
    my_rows = lax.dynamic_slice_in_dim(layout, frame_pos * positions, positions, 0)
    class_hot = (class_ids[:, None] == jnp.arange(CLASSES, dtype=jnp.int32)[None, :]).astype(F32)
    condition = time_features(timesteps) + jnp.dot(class_hot, class_table, precision=HIGHEST)
    activated = jax.nn.silu(condition)
    ada_part = jnp.dot(activated, w_ada.astype(F32), precision=HIGHEST) + b_ada.astype(F32)

    ada_cols, bias_cols = b_ada.shape[0], b_fc1.shape[0]
    small_rows, small_cols = round_up(clips + 1, 16), round_up(max(ada_cols, bias_cols), LANES)
    small = jnp.concatenate(
        [
            jnp.pad(ada_part.astype(BF16), ((0, 0), (0, width - ada_cols))),
            jnp.pad(b_fc1[None], ((0, small_rows - clips - 1), (0, width - bias_cols))),
        ],
        axis=0,
    )
    x_arrived = to_positions(tokens, small)
    small_all = x_arrived[:, own_frames * positions :]
    x_arrived = x_arrived.reshape(-1, width)
    clip_slots = round_up(clips, 16)
    mod = small_all[:, :clips, :ada_cols].transpose(1, 0, 2).reshape(clips, -1)
    mod = by_tile(my_rows, mod, frames)
    bias = small_all[:, clips, :bias_cols].reshape(1, -1)
    hot = jnp.pad(my_rows.astype(BF16), ((0, 0), (0, clip_slots - clips)))
    hot = jnp.repeat(hot, frames, axis=0)

    shard_rows = w_out.shape[0]
    got_attn = gather_frame(jnp.stack([*jnp.split(w_qkv, 3, axis=1), w_out]))
    spread_attn = Spread(got_attn, True)
    near_attn = spread_attn.near()
    got_fc1 = gather_frame(
        jnp.stack(jnp.split(w_fc1, 4, axis=1))
    )
    far_attn = spread_attn.far()
    fc2_rows = w_fc2.shape[0] // 4
    got_fc2 = gather_frame(after(w_fc2.reshape(4, fc2_rows, width), x_arrived, *far_attn))

    square = is_square()
    chips = frame_count // 2
    spread_fc1 = Spread(got_fc1, True)
    spread_fc2 = Spread(got_fc2, False)
    near_fc1 = spread_fc1.near(*far_attn)
    x_rows, first_in, projected, full_attn = qkv_call(
        where, x_arrived, mod, spread_attn.pieces(), positions, frames, own_frames
    )
    cot_arrived = to_positions(after(cotangent, projected)).reshape(rows, width)
    mixed = attend(after(projected, *near_fc1), positions, frames, attn_scale)
    far_fc1 = spread_fc1.far()
    near_fc2 = spread_fc2.near(*far_fc1)
    attn_out, middle, second_in = out_call(
        after(mixed, *far_fc1), x_rows, mod, full_attn, frames
    )
    far_fc2 = spread_fc2.far()
    post_act, slope, full_fc1 = fc1_call(
        where, second_in, bias, spread_fc1.pieces()
    )
    grad_rows, grad_mlp = cot_call(after(cot_arrived, post_act), hot, mod, positions, frames, own_frames)

    if square:
        sum_fc2 = Collect(where, *fc2_terms(where, post_act, after(grad_mlp, *near_fc2), chips))
        sum_fc2.pair()
        seen = (sum_fc2.give,)
    else:
        part_fc2 = lax.dot_general(post_act, grad_mlp, ROW_DIMS, preferred_element_type=F32)
        part_fc2 = part_fc2.reshape(frame_count, 4, fc2_rows, width).transpose(1, 0, 2, 3)
        seen = ()
    block_rows, grad_pre, part_bias, sum_gate_mlp = fc2_call(
        where,
        post_act,
        slope,
        after(grad_mlp, *seen),
        grad_rows,
        middle,
        hot,
        mod,
        spread_fc2.pieces(),
        positions,
        frames,
    )
    if square:
        seen = sum_fc2.near(grad_pre)
        sum_fc1 = Collect(where, *fc1_terms(where, second_in, after(grad_pre, *seen), chips))
        sum_fc1.pair()
        seen = (sum_fc1.give,)
    else:
        part_fc1 = [dot(second_in, part, ROW_DIMS) for part in jnp.split(grad_pre, 4, axis=1)]
        part_fc1 = jnp.stack(part_fc1).reshape(4, frame_count, shard_rows, -1)
    grad_middle, grad_attn, grad_mixed, sums_mlp = fc1_back_call(
        after(grad_pre, *seen), full_fc1, middle, attn_out, grad_rows, hot, mod, full_attn, frames
    )
    seen = ()
    if square:
        seen = (*sum_fc2.far(grad_mixed), *sum_fc1.near(grad_mixed))
    grad_proj = attend_back(
        projected, after(grad_mixed, *seen), positions, frames, attn_scale
    )
    out_arrived = send_frames(block_rows)
    seen = ()
    if square:
        seen = (*sum_fc2.line(grad_proj), out_arrived)
    token_rows, sums_attn = qkv_back_call(
        after(grad_proj, *seen), full_attn, x_rows, grad_middle, hot, mod, positions, frames
    )
    if square:
        seen = (token_rows, sum_fc2.own, *sum_fc1.far(token_rows))
        sum_attn = Collect(
            where, *attn_terms(where, first_in, after(grad_proj, *seen), mixed, grad_attn, chips)
        )
        sum_attn.pair()
        block_out = to_frames(out_arrived, sum_attn.give)
        sum_fc1.line(sum_attn.give)
        sum_attn.near()
        sum_attn.far()
        seen = sum_attn.line(sum_fc1.own)
        last = (sum_attn.own,)
        grad_tokens = to_frames(send_frames(token_rows), *seen)
        sum_fc2, sum_fc1, sum_attn = sum_fc2.finish(*seen), sum_fc1.finish(*seen), sum_attn.finish()
    else:
        grad_tokens, block_out = to_frames(send_frames(token_rows)), to_frames(out_arrived)
        part_attn = [dot(first_in, part, ROW_DIMS) for part in jnp.split(grad_proj, 3, axis=1)]
        part_attn = jnp.stack([*part_attn, dot(mixed, grad_attn, ROW_DIMS)])
        part_attn = part_attn.reshape(4, frame_count, shard_rows, width)
        seen, last = (), ()
        sum_fc2, sum_fc1, sum_attn = sum_plain(part_fc2), sum_plain(part_fc1), sum_plain(part_attn)
    part_mod = jnp.concatenate([sums_attn, sums_mlp, sum_gate_mlp[None]], axis=0)[:, :clips]
    part_mod = part_mod.transpose(1, 0, 2).reshape(clips, frame_count, ada_cols)
    part_small = jnp.concatenate(
        [
            jnp.pad(part_mod, ((0, 0), (0, 0), (0, small_cols - ada_cols))),
            jnp.pad(
                part_bias.reshape(1, frame_count, bias_cols),
                ((0, small_rows - clips - 1), (0, 0), (0, small_cols - bias_cols)),
            ),
        ],
        axis=0,
    ).astype(BF16)
    small_terms = lax.all_to_all(after(part_small, *seen).transpose(1, 0, 2), "frame", 0, 0, tiled=False)
    small_terms = after(small_terms, *last)
    small_sum = sum_items(jnp.sum(small_terms.astype(F32), axis=0))
    grad_modulation = small_sum[:clips, :ada_cols]
    sum_bias = small_sum[clips, :bias_cols]
    grad_b_ada = jnp.sum(grad_modulation, axis=0)
    high = grad_modulation.astype(BF16)
    low = (grad_modulation - high.astype(F32)).astype(BF16)
    act_part = (dot(high, w_ada, COL_DIMS) + dot(low, w_ada, COL_DIMS)).astype(BF16)
    grad_w_ada = lax.dot_general(
        activated, after(grad_modulation, act_part), ROW_DIMS, precision=HIGHEST
    )
    grad_activated = jnp.sum(share_small(act_part).astype(F32), axis=0)
    _, silu_back = jax.vjp(jax.nn.silu, condition)
    grad_condition = silu_back(grad_activated)[0]
    grad_table = lax.dot_general(class_hot, grad_condition, ROW_DIMS, precision=HIGHEST)
    return (
        block_out,
        grad_tokens,
        by_column_quarter(sum_attn)[:, : 3 * width].astype(F32),
        sum_attn[3].astype(F32),
        by_column_quarter(sum_fc1).astype(F32),
        sum_bias,
        sum_fc2.reshape(-1, width).astype(F32),
        grad_w_ada,
        grad_b_ada,
        grad_table,
    )


def solution(mesh):
    return jax.shard_map(
        body,
        mesh=mesh,
        in_specs=(
            P("item", "frame", None, None),
            P("item", "frame", None, None),
            P(),
            P(),
            P(),
            P(),
            P("frame", None),
            P("frame", None),
            P("frame", None),
            P("frame"),
            P("frame", None),
            P(None, "frame"),
            P("frame"),
            P(),
        ),
        out_specs=(
            P("item", "frame", None, None),
            P("item", "frame", None, None),
            P("frame", None),
            P("frame", None),
            P("frame", None),
            P("frame"),
            P("frame", None),
            P(None, "frame"),
            P("frame"),
            P(),
        ),
        check_vma=False,
    )
```
